32 devices in a mesh: grp: 2 (over x), aux: 16 (over z, y, core).
Axes of the slice: x: 2, y: 2, z: 4, core: 2. Of those that a mesh axis runs over, the one named last changes fastest.
Arguments:
- tiles: bfloat16 [2048, 5, 128, 128], P(('grp', 'aux')), parts along dimension 0, may hold values from -6 to 6
- c_orbitals: bfloat16 [8192, 128], P(('grp', 'aux')), parts along dimension 0, may hold values from -0.0078125 to 0.0078125
- basis_order: int32 [64], P('grp'), parts along dimension 0, may hold values from 0 to 31, as said below
- tile_block: int32 [2048], P(('grp', 'aux')), parts along dimension 0, may hold values from 0 to 31, as said below
- tile_aux: int32 [2048], P(('grp', 'aux')), parts along dimension 0, may hold values from 0 to 7
- live: int32 [32], P(('grp', 'aux')), parts along dimension 0, may hold values from 1 to 64, as said below
Outputs:
- exchange_c: bfloat16 [8192, 128], P(('grp', 'aux')), parts along dimension 0
The draws below stay inside these ranges and needn't reach their ends.
There are 2 independent parts, one for each index of `grp`. The reference program is written for one: setup_inputs(seed, part) draws one part's arguments, and reference() takes and returns one part's arrays. A program takes and returns all parts, laid end to end along the dimension named above; each array names one. Nothing has to cross between parts.
Inputs may be any that keep to these rules, and one draw needn't show every extreme that they name: `basis_order`: a permutation of the 32 basis blocks; device d owns positions d * 2 to (d + 1) * 2 - 1. `tile_block`: the tiles of one device name at most one of the blocks owned by any one device. `live`: some device uses all 64 slots.
All inputs are finite; a program needn't handle non-finite values.
Results may differ from the reference program's by a relative error of at most 0.0034.
Values may be sent and summed in bfloat16 or wider, within the bound.
No kernel may reach another device: no remote copies, remote signals or barrier semaphores. Data moves between devices by JAX's collectives and lax.ppermute only.
A program may use at most 128 MiB of HBM per device.

```python
import jax
import jax.numpy as jnp
from jax import lax

NOCC = 128
BLK = 128
AUXB = 5
AB_DEV = 8
BB_DEV = 2
NT_DEV = 64
NBB = 32
NBAS = 4096
N_AUX = 16


def shared_order(key):
    return jax.random.permutation(jax.random.fold_in(key, 11), NBB).astype(jnp.int32)


def draw_basis_order(key, part):
    order = shared_order(key)
    return order


def draw_tile_block(key, part):
    order = shared_order(key)
    key = jax.random.fold_in(key, 2)
    first, second = jax.random.split(key)
    chosen = jax.random.randint(first, (N_AUX, N_AUX), 0, BB_DEV)
    scores = jax.random.randint(second, (N_AUX, N_AUX), 0, 1 << 20) * N_AUX + jnp.arange(N_AUX, dtype=jnp.int32)[None, :]
    shuffled = jnp.argsort(scores, axis=1).astype(jnp.int32)
    column = jnp.arange(NT_DEV, dtype=jnp.int32) % N_AUX
    owners = shuffled[:, column]
    slot = jnp.take_along_axis(chosen, owners, axis=1)
    return order[owners * BB_DEV + slot].reshape(N_AUX * NT_DEV).astype(jnp.int32)


def draw_live(key, part):
    key = jax.random.fold_in(key, 3)
    first, second, third = jax.random.split(key, 3)
    base = jax.random.randint(first, (N_AUX,), max(1, NT_DEV // 2), NT_DEV + 1)
    full = jax.random.randint(second, (N_AUX,), 0, 8) == 0
    pick = jax.random.randint(third, (), 0, N_AUX)
    full = full | (jnp.arange(N_AUX, dtype=jnp.int32) == pick)
    return jnp.where(full, NT_DEV, base).astype(jnp.int32)


def with_ends(array, own_key, smallest, high):
    longest = array.shape.index(max(array.shape))
    spots = []
    for shift in (0, 1):
        where = [jax.random.randint(jax.random.fold_in(own_key, axis), (), 0, length) for axis, length in enumerate(array.shape)]
        where[longest] = (where[longest] + shift) % array.shape[longest]
        spots.append(tuple(where))
    return array.at[spots[0]].set(smallest).at[spots[1]].set(high)


def steps_of(own_key, dims, cuts, low, largest):
    factor_of, own = 1.0, jax.random.fold_in(own_key, 6)
    for dim, blocks in cuts:
        steps = jnp.exp(jax.random.uniform(jax.random.fold_in(own, dim), (blocks,), jnp.float32, low / len(cuts), largest / len(cuts)))
        factor_of = factor_of * jnp.repeat(steps, dims[dim] // blocks).reshape([-1 if axis == dim else 1 for axis in range(len(dims))])
    return factor_of


def normal_values(stream_key, extent, width, limit, cuts=(), kind=jnp.bfloat16):
    level = steps_of(stream_key, extent, cuts, -0.22, 0.18) if cuts else 1.0
    result = jax.random.normal(stream_key, extent, jnp.float32) * width * level
    return jnp.minimum(jnp.maximum(result, -limit), limit).astype(kind)


def setup_inputs(seed: int = 0, part: int = 0) -> dict:
    splits = jax.random.split(jax.random.key(seed), 7)
    part_splits = jax.random.split(jax.random.fold_in(splits[6], part), 7)
    tiles = normal_values(part_splits[0], (N_AUX * NT_DEV, AUXB, BLK, NOCC), 1.0, 6.0, ((0, 16),))
    c_orbitals = normal_values(part_splits[1], (NBAS, NOCC), (AUXB * NOCC * BLK * 6) ** -0.5, 0.0078125, ((0, 16),))
    basis_order = draw_basis_order(jax.random.fold_in(jax.random.fold_in(splits[6], part), 71), part)
    tile_block = draw_tile_block(jax.random.fold_in(jax.random.fold_in(splits[6], part), 71), part)
    tile_aux = with_ends(jax.random.randint(part_splits[4], (N_AUX * NT_DEV,), 0, AB_DEV), jax.random.fold_in(part_splits[4], 1), 0, AB_DEV - 1).astype(jnp.int32)
    live = draw_live(jax.random.fold_in(jax.random.fold_in(splits[6], part), 71), part)
    return {"tiles": tiles, "c_orbitals": c_orbitals, "basis_order": basis_order, "tile_block": tile_block, "tile_aux": tile_aux, "live": live}


def reference(tiles, c_orbitals, basis_order, tile_block, tile_aux, live):
    inverse = jnp.zeros((NBB,), jnp.int32).at[basis_order].set(jnp.arange(NBB, dtype=jnp.int32))
    position = inverse[tile_block].reshape(N_AUX, NT_DEV)
    blocks = c_orbitals.reshape(NBB, BLK, NOCC)
    tiles_dev = tiles.reshape(N_AUX, NT_DEV, AUXB, BLK, NOCC)
    aux_dev = tile_aux.reshape(N_AUX, NT_DEV)

    def one_device(total, items):
        tile_set, where_to, aux_ids, count = items
        alive = (jnp.arange(NT_DEV, dtype=jnp.int32) < count).astype(jnp.float32)
        picked = blocks[where_to].astype(jnp.float32)
        half = jnp.einsum("tpmi,tmj->tpij", tile_set.astype(jnp.float32), picked)
        member = (aux_ids[None, :] == jnp.arange(AB_DEV, dtype=jnp.int32)[:, None]).astype(jnp.float32) * alive[None, :]
        fitted = jnp.einsum("at,tpij->apij", member, half, precision=lax.Precision.HIGHEST).astype(jnp.bfloat16)
        per_tile = fitted[aux_ids].astype(jnp.float32)
        partial_value = jnp.einsum("tpmi,tpij->tmj", tile_set.astype(jnp.float32), per_tile) * alive[:, None, None]
        return total.at[where_to].add(partial_value), None

    start = jnp.zeros((NBB, BLK, NOCC), jnp.float32)
    total, unused = lax.scan(one_device, start, (tiles_dev, position, aux_dev, live))
    return total.reshape(NBAS, NOCC).astype(jnp.bfloat16)
```

```python
import functools

import jax
import jax.numpy as jnp
from jax import lax
from jax.experimental import pallas as pl
from jax.experimental.pallas import tpu as pltpu
from jax.sharding import PartitionSpec as P

AB_DEV = 8
CHUNK = 4
AHEAD = 8
TAIL = 16
DIRECT_LIMIT = 32


def plan(tile_block, tile_aux, live, basis_order, own, n_aux, bb_dev):
    slots = tile_block.shape[0]
    nbb = basis_order.shape[0]
    chunks = slots // CHUNK + AB_DEV
    t = lax.iota(jnp.int32, slots)
    alive = t < live[0]
    position = jnp.sum(
        jnp.where(
            basis_order[None, :] == tile_block[:, None], lax.iota(jnp.int32, nbb)[None, :], 0
        ),
        axis=1,
    )
    where_to = position // bb_dev
    where_to = jnp.bitwise_xor(where_to, own)
    which = position % bb_dev
    group = jnp.where(alive, tile_aux, AB_DEV)
    ids = lax.iota(jnp.int32, AB_DEV)
    counts = jnp.sum((group[None, :] == ids[:, None]).astype(jnp.int32), axis=1)
    need = (counts + CHUNK - 1) // CHUNK
    ends = jnp.sum(jnp.where(ids[None, :] <= ids[:, None], need[None, :], 0), axis=1)
    rank = jnp.sum(
        ((group[None, :] == group[:, None]) & (t[None, :] < t[:, None])).astype(jnp.int32), axis=1
    )
    start = jnp.sum(jnp.where(group[:, None] > ids[None, :], need[None, :], 0), axis=1)
    place = jnp.where(alive, start * CHUNK + rank, -1)
    q = lax.iota(jnp.int32, chunks * CHUNK)
    hit = place[None, :] == q[:, None]
    lead = place[None, :] == (q // CHUNK * CHUNK)[:, None]
    valid = jnp.any(hit, axis=1)
    slot = jnp.sum(jnp.where(hit, t[None, :], 0), axis=1)
    slot = jnp.where(valid, slot, jnp.sum(jnp.where(lead, t[None, :], 0), axis=1))
    block = jnp.where(valid, jnp.sum(jnp.where(hit, where_to[None, :], 0), axis=1), n_aux)
    gid = jnp.sum(
        (lax.iota(jnp.int32, chunks)[:, None] >= ends[None, :]).astype(jnp.int32), axis=1
    )
    bit = jnp.max(
        jnp.where(
            (where_to[None, :] == lax.iota(jnp.int32, n_aux)[:, None]) & alive[None, :],
            which[None, :],
            0,
        ),
        axis=1,
    )
    return slot, block, jnp.concatenate([gid, ends]), bit


def build_kernel(
    direct, n_aux, chunks, slot_ref, block_ref, gid_ref, bit_ref, tiles_hbm, *refs
):
    n_refs = n_aux if direct else 1
    c_refs, out_refs = refs[:n_refs], refs[n_refs : 2 * n_refs]
    tiles, ct, zacc, zb, acc, sems = refs[2 * n_refs :]
    blk, nocc = ct.shape[2], ct.shape[1]
    auxb = tiles.shape[1]
    total = gid_ref[chunks + AB_DEV - 1]

    def copies(chunk):
        for i in range(CHUNK):
            pos = chunk * CHUNK + i
            slot = slot_ref[pos]
            yield block_ref[pos] < n_aux, pltpu.make_async_copy(
                tiles_hbm.at[slot], tiles.at[slot], sems.at[chunk]
            )

    def start(chunk):
        for used, copy in copies(chunk):
            @pl.when(used)
            def _():
                copy.start()

    def wait(chunk):
        for used, copy in copies(chunk):
            @pl.when(used)
            def _():
                copy.wait()

    @pl.loop(0, jnp.minimum(total, AHEAD))
    def _(chunk):
        start(chunk)

    def turn(m, source):
        ct[m] = source[pl.ds(pl.multiple_of(bit_ref[m] * blk, blk), blk), :].T

    if direct:
        for m in range(n_aux):
            turn(m, c_refs[m])
    else:
        @pl.loop(0, n_aux)
        def _(m):
            turn(m, c_refs[0].at[m])

    ct[n_aux] = jnp.zeros((nocc, blk), ct.dtype)
    acc[...] = jnp.zeros(acc.shape, acc.dtype)
    zacc[...] = jnp.zeros(zacc.shape, zacc.dtype)

    @pl.loop(0, total)
    def _(chunk):
        @pl.when(chunk + AHEAD < total)
        def _():
            start(chunk + AHEAD)

        wait(chunk)
        g = gid_ref[chunk]
        spots = [chunk * CHUNK + i for i in range(CHUNK)]
        left = jnp.concatenate([ct[block_ref[pos]] for pos in spots], axis=1)
        for p in range(auxb):
            right = jnp.concatenate([tiles[slot_ref[pos], p] for pos in spots], axis=0)
            zacc[g, p] += jnp.dot(left, right, preferred_element_type=jnp.float32)

    for g in range(AB_DEV):
        for p in range(auxb):
            zb[g, :, p * nocc : (p + 1) * nocc] = zacc[g, p].astype(zb.dtype)

    @pl.loop(0, total)
    def _(chunk):
        g = gid_ref[chunk]
        spots = [chunk * CHUNK + i for i in range(CHUNK)]
        left = jnp.concatenate(
            [
                jnp.concatenate([tiles[slot_ref[pos], p] for p in range(auxb)], axis=1)
                for pos in spots
            ],
            axis=0,
        )
        value = lax.dot_general(
            left, zb[g], (((1,), (1,)), ((), ())), preferred_element_type=jnp.float32
        )
        for i, pos in enumerate(spots):
            acc[block_ref[pos]] += value[i * blk : (i + 1) * blk]

    def put(m, target):
        target[:blk, :] = acc[m].astype(target.dtype)
        target[blk:, :] = jnp.full((TAIL, nocc), bit_ref[m], jnp.int32).astype(
            jnp.float32
        ).astype(target.dtype)

    if direct:
        for m in range(n_aux):
            put(m, out_refs[m])
    else:
        @pl.loop(0, n_aux)
        def _(m):
            put(m, out_refs[0].at[m])


def contributions(direct, n_aux, meta, tiles, shards):
    slots, auxb, blk, nocc = tiles.shape
    chunks = slots // CHUNK + AB_DEV
    rows = blk + TAIL
    smem = pl.BlockSpec(memory_space=pltpu.SMEM)
    vmem = pl.BlockSpec(memory_space=pltpu.VMEM)
    if direct:
        out_shape = [jax.ShapeDtypeStruct((rows, nocc), jnp.bfloat16)] * n_aux
    else:
        out_shape = [jax.ShapeDtypeStruct((n_aux, rows, nocc), jnp.bfloat16)]
    return pl.pallas_call(
        functools.partial(build_kernel, direct, n_aux, chunks),
        out_shape=out_shape,
        in_specs=[smem] * 4 + [pl.BlockSpec(memory_space=pl.ANY)] + [vmem] * len(shards),
        out_specs=[vmem] * len(out_shape),
        scratch_shapes=[
            pltpu.VMEM(tiles.shape, jnp.bfloat16),
            pltpu.VMEM((n_aux + 1, nocc, blk), jnp.bfloat16),
            pltpu.VMEM((AB_DEV, auxb, nocc, nocc), jnp.float32),
            pltpu.VMEM((AB_DEV, nocc, auxb * nocc), jnp.bfloat16),
            pltpu.VMEM((n_aux + 1, blk, nocc), jnp.float32),
            pltpu.SemaphoreType.DMA((chunks,)),
        ],
        compiler_params=pltpu.CompilerParams(vmem_limit_bytes=44 * 1024 * 1024),
        cost_estimate=pl.CostEstimate(
            flops=4 * tiles.size * nocc, bytes_accessed=2 * tiles.size, transcendentals=0
        ),
        name="exchange",
    )(*meta, tiles, *shards)


def on_device(tiles, c_orbitals, basis_order, tile_block, tile_aux, live):
    blk, nocc = tiles.shape[2:]
    n_aux = lax.axis_size("aux")
    bb_dev = basis_order.shape[0] // n_aux
    me = lax.axis_index("aux")
    direct = n_aux <= DIRECT_LIMIT

    def swap(array, m):
        return lax.ppermute(array, "aux", [(i, i ^ m) for i in range(n_aux)])

    if direct:
        shards = [c_orbitals] + [None] * (n_aux - 1)
        for m in range(2, n_aux, 2):
            shards[m] = swap(c_orbitals, m)
        for m in range(0, n_aux, 2):
            shards[m + 1] = swap(shards[m], 1)
    else:
        whole = lax.all_gather(c_orbitals, "aux", axis=0, tiled=True)
        shards = [whole.reshape(n_aux, bb_dev * blk, nocc)]
    meta = plan(
        tile_block, tile_aux, live, basis_order, me if direct else jnp.int32(0), n_aux, bb_dev
    )
    parts = contributions(direct, n_aux, meta, tiles, shards)
    if direct:
        parts = [parts[0]] + [swap(parts[m], m) for m in range(1, n_aux)]
    else:
        moved = lax.all_to_all(parts[0], "aux", 0, 0, tiled=True)
        parts = [moved[m] for m in range(n_aux)]
    sums = [jnp.zeros((blk, nocc), jnp.float32) for _ in range(bb_dev)]
    for part in parts:
        value = part[:blk].astype(jnp.float32)
        which = part[blk, 0].astype(jnp.float32)
        for b in range(bb_dev):
            sums[b] = sums[b] + jnp.where(which == b, value, 0.0)
    return jnp.concatenate(sums, axis=0).astype(jnp.bfloat16)


def solution(mesh):
    return jax.shard_map(
        on_device,
        mesh=mesh,
        in_specs=(
            P(("grp", "aux"), None, None, None),
            P(("grp", "aux"), None),
            P("grp"),
            P(("grp", "aux")),
            P(("grp", "aux")),
            P(("grp", "aux")),
        ),
        out_specs=P(("grp", "aux"), None),
        check_vma=False,
    )
```

```python
import functools

import jax
import jax.numpy as jnp
from jax import lax
from jax.experimental import pallas as pl
from jax.experimental.pallas import tpu as pltpu
from jax.sharding import PartitionSpec as P

AB_DEV = 8
CHUNK = 4
AHEAD = 8
TAIL = 16
DIRECT_LIMIT = 32


def plan(tile_block, tile_aux, live, basis_order, me, n_aux, bb_dev):
    slots = tile_block.shape[0]
    nbb = basis_order.shape[0]
    chunks = slots // CHUNK + AB_DEV
    t = lax.iota(jnp.int32, slots)
    alive = t < live[0]
    position = jnp.sum(
        jnp.where(
            basis_order[None, :] == tile_block[:, None], lax.iota(jnp.int32, nbb)[None, :], 0
        ),
        axis=1,
    )
    where_to = position // bb_dev
    which = position % bb_dev
    group = jnp.where(alive, tile_aux, AB_DEV)
    ids = lax.iota(jnp.int32, AB_DEV)
    counts = jnp.sum((group[None, :] == ids[:, None]).astype(jnp.int32), axis=1)
    need = (counts + CHUNK - 1) // CHUNK
    ends = jnp.sum(jnp.where(ids[None, :] <= ids[:, None], need[None, :], 0), axis=1)
    rank = jnp.sum(
        ((group[None, :] == group[:, None]) & (t[None, :] < t[:, None])).astype(jnp.int32), axis=1
    )
    start = jnp.sum(jnp.where(group[:, None] > ids[None, :], need[None, :], 0), axis=1)
    place = jnp.where(alive, start * CHUNK + rank, -1)
    q = lax.iota(jnp.int32, chunks * CHUNK)
    hit = place[None, :] == q[:, None]
    lead = place[None, :] == (q // CHUNK * CHUNK)[:, None]
    valid = jnp.any(hit, axis=1)
    slot = jnp.sum(jnp.where(hit, t[None, :], 0), axis=1)
    slot = jnp.where(valid, slot, jnp.sum(jnp.where(lead, t[None, :], 0), axis=1))
    block = jnp.where(valid, jnp.sum(jnp.where(hit, where_to[None, :], 0), axis=1), n_aux)
    gid = jnp.sum(
        (lax.iota(jnp.int32, chunks)[:, None] >= ends[None, :]).astype(jnp.int32), axis=1
    )
    bit = jnp.max(
        jnp.where(
            (where_to[None, :] == lax.iota(jnp.int32, n_aux)[:, None]) & alive[None, :],
            which[None, :],
            0,
        ),
        axis=1,
    )
    return slot, block, jnp.concatenate([gid, ends]), jnp.concatenate([bit, me[None]])


def build_kernel(
    direct, n_aux, chunks, slot_ref, block_ref, gid_ref, bit_ref, tiles_hbm, *refs
):
    c_refs, (out_ref, tiles, ct, zacc, zb, acc, sems) = refs[:-7], refs[-7:]
    blk, nocc = ct.shape[2], ct.shape[1]
    auxb = tiles.shape[1]
    total = gid_ref[chunks + AB_DEV - 1]

    def copies(chunk):
        for i in range(CHUNK):
            pos = chunk * CHUNK + i
            slot = slot_ref[pos]
            yield block_ref[pos] < n_aux, pltpu.make_async_copy(
                tiles_hbm.at[slot], tiles.at[slot], sems.at[chunk]
            )

    def start(chunk):
        for used, copy in copies(chunk):
            @pl.when(used)
            def _():
                copy.start()

    def wait(chunk):
        for used, copy in copies(chunk):
            @pl.when(used)
            def _():
                copy.wait()

    @pl.loop(0, jnp.minimum(total, AHEAD))
    def _(chunk):
        start(chunk)

    def turn(m, source):
        ct[m] = source[pl.ds(pl.multiple_of(bit_ref[m] * blk, blk), blk), :].T

    if direct:
        core = lax.rem(bit_ref[n_aux], 2)
        for chip in range(n_aux // 2):
            turn(2 * chip + core, c_refs[0].at[chip])
            turn(2 * chip + 1 - core, c_refs[1].at[chip])
    else:
        @pl.loop(0, n_aux)
        def _(m):
            turn(m, c_refs[0].at[m])

    ct[n_aux] = jnp.zeros((nocc, blk), ct.dtype)
    acc[...] = jnp.zeros(acc.shape, acc.dtype)
    zacc[...] = jnp.zeros(zacc.shape, zacc.dtype)

    @pl.loop(0, total)
    def _(chunk):
        @pl.when(chunk + AHEAD < total)
        def _():
            start(chunk + AHEAD)

        wait(chunk)
        g = gid_ref[chunk]
        spots = [chunk * CHUNK + i for i in range(CHUNK)]
        left = jnp.concatenate([ct[block_ref[pos]] for pos in spots], axis=1)
        for p in range(auxb):
            right = jnp.concatenate([tiles[slot_ref[pos], p] for pos in spots], axis=0)
            zacc[g, p] += jnp.dot(left, right, preferred_element_type=jnp.float32)

    for g in range(AB_DEV):
        for p in range(auxb):
            zb[g, :, p * nocc : (p + 1) * nocc] = zacc[g, p].astype(zb.dtype)

    @pl.loop(0, total)
    def _(chunk):
        g = gid_ref[chunk]
        spots = [chunk * CHUNK + i for i in range(CHUNK)]
        left = jnp.concatenate(
            [
                jnp.concatenate([tiles[slot_ref[pos], p] for p in range(auxb)], axis=1)
                for pos in spots
            ],
            axis=0,
        )
        value = lax.dot_general(
            left, zb[g], (((1,), (1,)), ((), ())), preferred_element_type=jnp.float32
        )
        for i, pos in enumerate(spots):
            acc[block_ref[pos]] += value[i * blk : (i + 1) * blk]

    @pl.loop(0, n_aux, unroll=8)
    def _(m):
        out_ref[m, :blk, :] = acc[m].astype(out_ref.dtype)
        out_ref[m, blk:, :] = jnp.full((TAIL, nocc), bit_ref[m], jnp.int32).astype(
            jnp.float32
        ).astype(out_ref.dtype)


def contributions(direct, n_aux, meta, tiles, shards):
    slots, auxb, blk, nocc = tiles.shape
    chunks = slots // CHUNK + AB_DEV
    smem = pl.BlockSpec(memory_space=pltpu.SMEM)
    vmem = pl.BlockSpec(memory_space=pltpu.VMEM)
    out_shape = jax.ShapeDtypeStruct((n_aux, blk + TAIL, nocc), jnp.bfloat16)
    return pl.pallas_call(
        functools.partial(build_kernel, direct, n_aux, chunks),
        out_shape=out_shape,
        in_specs=[smem] * 4 + [pl.BlockSpec(memory_space=pl.ANY)] + [vmem] * len(shards),
        out_specs=vmem,
        scratch_shapes=[
            pltpu.VMEM(tiles.shape, jnp.bfloat16),
            pltpu.VMEM((n_aux + 1, nocc, blk), jnp.bfloat16),
            pltpu.VMEM((AB_DEV, auxb, nocc, nocc), jnp.float32),
            pltpu.VMEM((AB_DEV, nocc, auxb * nocc), jnp.bfloat16),
            pltpu.VMEM((n_aux + 1, blk, nocc), jnp.float32),
            pltpu.SemaphoreType.DMA((chunks,)),
        ],
        compiler_params=pltpu.CompilerParams(vmem_limit_bytes=44 * 1024 * 1024),
        cost_estimate=pl.CostEstimate(
            flops=4 * tiles.size * nocc, bytes_accessed=2 * tiles.size, transcendentals=0
        ),
        name="exchange",
    )(*meta, tiles, *shards)


def owner_sum(parts, blk, bb_dev):
    n_aux, rows, nocc = parts.shape

    def kernel(parts_ref, out_ref):
        sums = [jnp.zeros((blk, nocc), jnp.float32) for _ in range(bb_dev)]
        for s in range(n_aux):
            value = parts_ref[s, :blk, :].astype(jnp.float32)
            which = parts_ref[s, blk:, :][:1].astype(jnp.float32)
            for b in range(bb_dev):
                sums[b] = sums[b] + jnp.where(which == b, value, 0.0)
        for b in range(bb_dev):
            out_ref[b * blk : (b + 1) * blk, :] = sums[b].astype(out_ref.dtype)

    vmem = pl.BlockSpec(memory_space=pltpu.VMEM)
    return pl.pallas_call(
        kernel,
        out_shape=jax.ShapeDtypeStruct((bb_dev * blk, nocc), jnp.bfloat16),
        in_specs=[vmem],
        out_specs=vmem,
        name="owner_sum",
    )(parts)


def on_device(tiles, c_orbitals, basis_order, tile_block, tile_aux, live):
    blk, nocc = tiles.shape[2:]
    n_aux = lax.axis_size("aux")
    bb_dev = basis_order.shape[0] // n_aux
    me = lax.axis_index("aux")
    direct = n_aux <= DIRECT_LIMIT
    if direct:
        chips = n_aux // 2
        same = [[2 * chip + core for chip in range(chips)] for core in range(2)]
        wide = jnp.broadcast_to(c_orbitals[None], (chips,) + c_orbitals.shape)
        mine = lax.all_to_all(wide, "aux", 0, 0, axis_index_groups=same, tiled=True)
        other = lax.ppermute(mine, "aux", [(i, i ^ 1) for i in range(n_aux)])
        shards = [mine, other]
    else:
        whole = lax.all_gather(c_orbitals, "aux", axis=0, tiled=True)
        shards = [whole.reshape(n_aux, bb_dev * blk, nocc)]
    meta = plan(tile_block, tile_aux, live, basis_order, me, n_aux, bb_dev)
    parts = contributions(direct, n_aux, meta, tiles, shards)
    moved = lax.all_to_all(parts, "aux", 0, 0, tiled=True)
    return owner_sum(moved, blk, bb_dev)


def solution(mesh):
    return jax.shard_map(
        on_device,
        mesh=mesh,
        in_specs=(
            P(("grp", "aux"), None, None, None),
            P(("grp", "aux"), None),
            P("grp"),
            P(("grp", "aux")),
            P(("grp", "aux")),
            P(("grp", "aux")),
        ),
        out_specs=P(("grp", "aux"), None),
        check_vma=False,
    )
```

```python
import functools

import jax
import jax.numpy as jnp
from jax import lax
from jax.experimental import pallas as pl
from jax.experimental.pallas import tpu as pltpu
from jax.sharding import PartitionSpec as P

AB_DEV = 8
CHUNK = 4
UNROLL = 2
TAIL = 16
PLANE = 4
DIRECT = 16


def plan(tile_block, tile_aux, live, basis_order, me, n_aux, bb_dev):
    slots = tile_block.shape[0]
    nbb = basis_order.shape[0]
    chunks = slots // CHUNK + AB_DEV
    t = lax.iota(jnp.int32, slots)
    alive = t < live[0]
    position = jnp.sum(
        jnp.where(
            basis_order[None, :] == tile_block[:, None], lax.iota(jnp.int32, nbb)[None, :], 0
        ),
        axis=1,
    )
    where_to = position // bb_dev
    which = position % bb_dev
    group = jnp.where(alive, tile_aux, AB_DEV)
    ids = lax.iota(jnp.int32, AB_DEV)
    counts = jnp.sum((group[None, :] == ids[:, None]).astype(jnp.int32), axis=1)
    need = (counts + CHUNK - 1) // CHUNK
    ends = jnp.sum(jnp.where(ids[None, :] <= ids[:, None], need[None, :], 0), axis=1)
    rank = jnp.sum(
        ((group[None, :] == group[:, None]) & (t[None, :] < t[:, None])).astype(jnp.int32), axis=1
    )
    start = jnp.sum(jnp.where(group[:, None] > ids[None, :], need[None, :], 0), axis=1)
    place = jnp.where(alive, start * CHUNK + rank, -1)
    q = lax.iota(jnp.int32, chunks * CHUNK)
    hit = place[None, :] == q[:, None]
    lead = place[None, :] == (q // CHUNK * CHUNK)[:, None]
    valid = jnp.any(hit, axis=1)
    slot = jnp.sum(jnp.where(hit, t[None, :], 0), axis=1)
    slot = jnp.where(valid, slot, jnp.sum(jnp.where(lead, t[None, :], 0), axis=1))
    block = jnp.where(valid, jnp.sum(jnp.where(hit, where_to[None, :], 0), axis=1), n_aux)
    gid = jnp.sum(
        (lax.iota(jnp.int32, chunks)[:, None] >= ends[None, :]).astype(jnp.int32), axis=1
    )
    bit = jnp.max(
        jnp.where(
            (where_to[None, :] == lax.iota(jnp.int32, n_aux)[:, None]) & alive[None, :],
            which[None, :],
            0,
        ),
        axis=1,
    )
    gid = jnp.minimum(gid, AB_DEV - 1)
    return slot, block, jnp.concatenate([gid, ends]), jnp.concatenate([bit, me[None]])


def build_kernel(
    direct, n_aux, chunks, n_in, slot_ref, block_ref, gid_ref, bit_ref, tiles, *refs
):
    c_refs, out_refs, (ct, zacc, zb, acc) = refs[:n_in], refs[n_in:-4], refs[-4:]
    blk, nocc = ct.shape[2], ct.shape[1]
    auxb = tiles.shape[1]
    total = gid_ref[chunks + AB_DEV - 1]
    turns = (total + UNROLL - 1) // UNROLL

    def turn(o, source):
        ct[o] = source[pl.ds(pl.multiple_of(bit_ref[o] * blk, blk), blk), :].T

    me = bit_ref[n_aux]
    if direct:
        for m in range(n_aux):
            turn(me ^ m, c_refs[m])
    else:
        @pl.loop(0, n_aux)
        def _(o):
            turn(o, c_refs[0].at[o])

    ct[n_aux] = jnp.zeros((nocc, blk), ct.dtype)
    acc[...] = jnp.zeros(acc.shape, acc.dtype)
    zacc[...] = jnp.zeros(zacc.shape, zacc.dtype)

    def slab(slot):
        return jnp.concatenate([tiles[slot, p] for p in range(auxb)], axis=1)

    @pl.loop(0, turns)
    def _(step):
        for chunk in [step * UNROLL + u for u in range(UNROLL)]:
            g = gid_ref[chunk]
            spots = [chunk * CHUNK + i for i in range(CHUNK)]
            left = jnp.concatenate([ct[block_ref[pos]] for pos in spots], axis=1)
            right = jnp.concatenate([slab(slot_ref[pos]) for pos in spots], axis=0)
            zacc[g] += jnp.dot(left, right, preferred_element_type=jnp.float32)

    for g in range(AB_DEV):
        zb[g] = zacc[g].astype(zb.dtype)

    @pl.loop(0, turns)
    def _(step):
        for chunk in [step * UNROLL + u for u in range(UNROLL)]:
            g = gid_ref[chunk]
            spots = [chunk * CHUNK + i for i in range(CHUNK)]
            left = jnp.concatenate([slab(slot_ref[pos]) for pos in spots], axis=0)
            value = lax.dot_general(
                left, zb[g], (((1,), (1,)), ((), ())), preferred_element_type=jnp.float32
            )
            for i, pos in enumerate(spots):
                acc[block_ref[pos]] += value[i * blk : (i + 1) * blk]

    def put(o, out_ref, at):
        out_ref[at, :blk, :] = acc[o].astype(out_ref.dtype)
        out_ref[at, blk:, :] = jnp.full((TAIL, nocc), bit_ref[o], jnp.int32).astype(
            jnp.float32
        ).astype(out_ref.dtype)

    if direct:
        half = n_aux // PLANE // 2
        for m in range(n_aux):
            dz, r = divmod(m, PLANE)
            put(me ^ m, out_refs[dz // half * PLANE + r], dz % half)
    else:
        @pl.loop(0, n_aux)
        def _(o):
            put(o, out_refs[0], o)


def contributions(direct, n_aux, meta, tiles, shards):
    slots, auxb, blk, nocc = tiles.shape
    chunks = slots // CHUNK + AB_DEV
    smem = pl.BlockSpec(memory_space=pltpu.SMEM)
    vmem = pl.BlockSpec(memory_space=pltpu.VMEM)
    if direct:
        shape = (n_aux // PLANE // 2, blk + TAIL, nocc)
        out_shape = [jax.ShapeDtypeStruct(shape, jnp.bfloat16)] * (2 * PLANE)
    else:
        out_shape = [jax.ShapeDtypeStruct((n_aux, blk + TAIL, nocc), jnp.bfloat16)]
    return pl.pallas_call(
        functools.partial(build_kernel, direct, n_aux, chunks, len(shards)),
        out_shape=out_shape,
        in_specs=[smem] * 4 + [vmem] * (1 + len(shards)),
        out_specs=[vmem] * len(out_shape),
        scratch_shapes=[
            pltpu.VMEM((n_aux + 1, nocc, blk), jnp.bfloat16),
            pltpu.VMEM((AB_DEV, nocc, auxb * nocc), jnp.float32),
            pltpu.VMEM((AB_DEV, nocc, auxb * nocc), jnp.bfloat16),
            pltpu.VMEM((n_aux + 1, blk, nocc), jnp.float32),
        ],
        compiler_params=pltpu.CompilerParams(
            vmem_limit_bytes=(32 if direct else 46) * 1024 * 1024
        ),
        cost_estimate=pl.CostEstimate(
            flops=4 * tiles.size * nocc, bytes_accessed=2 * tiles.size, transcendentals=0
        ),
        name="exchange",
    )(*meta, tiles, *shards)


def spread(parts, dtypes, blk, bb_dev):
    count, rows, nocc = parts[0].shape

    def kernel(*refs):
        sources, targets = refs[: len(parts)], refs[len(parts) :]
        for i in range(count):
            sums = [jnp.zeros((blk, nocc), jnp.float32) for _ in range(bb_dev)]
            for source in sources:
                value = source[i, :blk, :].astype(jnp.float32)
                which = source[i, blk:, :][:1].astype(jnp.float32)
                for b in range(bb_dev):
                    sums[b] = sums[b] + jnp.where(which == b, value, 0.0)
            for b in range(bb_dev):
                targets[i][b * blk : (b + 1) * blk, :] = sums[b].astype(targets[i].dtype)

    vmem = pl.BlockSpec(memory_space=pltpu.VMEM)
    return pl.pallas_call(
        kernel,
        out_shape=[jax.ShapeDtypeStruct((bb_dev * blk, nocc), dtype) for dtype in dtypes],
        in_specs=[vmem] * len(parts),
        out_specs=[vmem] * count,
        name="spread",
    )(*parts)


def total_of(arrays):
    def kernel(*refs):
        value = refs[0][...].astype(jnp.float32)
        for ref in refs[1:-1]:
            value = value + ref[...].astype(jnp.float32)
        refs[-1][...] = value.astype(refs[-1].dtype)

    vmem = pl.BlockSpec(memory_space=pltpu.VMEM)
    return pl.pallas_call(
        kernel,
        out_shape=jax.ShapeDtypeStruct(arrays[0].shape, jnp.bfloat16),
        in_specs=[vmem] * len(arrays),
        out_specs=vmem,
        name="total_of",
    )(*arrays)


def owner_sum(parts, blk, bb_dev):
    n_aux, rows, nocc = parts.shape

    def kernel(parts_ref, out_ref):
        sums = [jnp.zeros((blk, nocc), jnp.float32) for _ in range(bb_dev)]
        for s in range(n_aux):
            value = parts_ref[s, :blk, :].astype(jnp.float32)
            which = parts_ref[s, blk:, :][:1].astype(jnp.float32)
            for b in range(bb_dev):
                sums[b] = sums[b] + jnp.where(which == b, value, 0.0)
        for b in range(bb_dev):
            out_ref[b * blk : (b + 1) * blk, :] = sums[b].astype(out_ref.dtype)

    vmem = pl.BlockSpec(memory_space=pltpu.VMEM)
    return pl.pallas_call(
        kernel,
        out_shape=jax.ShapeDtypeStruct((bb_dev * blk, nocc), jnp.bfloat16),
        in_specs=[vmem],
        out_specs=vmem,
        name="owner_sum",
    )(parts)


def on_device(tiles, c_orbitals, basis_order, tile_block, tile_aux, live):
    blk, nocc = tiles.shape[2:]
    n_aux = lax.axis_size("aux")
    bb_dev = basis_order.shape[0] // n_aux
    me = lax.axis_index("aux")
    direct = n_aux == DIRECT
    meta = plan(tile_block, tile_aux, live, basis_order, me, n_aux, bb_dev)

    def swap(array, m):
        return lax.ppermute(array, "aux", [(i, i ^ m) for i in range(n_aux)])

    if not direct:
        whole = lax.all_gather(c_orbitals, "aux", axis=0, tiled=True)
        shards = [whole.reshape(n_aux, bb_dev * blk, nocc)]
        (parts,) = contributions(direct, n_aux, meta, tiles, shards)
        moved = lax.all_to_all(parts, "aux", 0, 0, tiled=True)
        return owner_sum(moved, blk, bb_dev)

    depth = n_aux // PLANE
    shards = [c_orbitals] + [None] * (n_aux - 1)
    for dz in range(depth - 1, 0, -1):
        shards[dz * PLANE] = swap(c_orbitals, dz * PLANE)
    for dz in range(depth):
        shards[dz * PLANE + 2] = swap(shards[dz * PLANE], 2)
    for m in range(0, n_aux, 2):
        shards[m + 1] = swap(shards[m], 1)
    parts = contributions(direct, n_aux, meta, tiles, shards)
    half = depth // 2
    near, far = parts[:PLANE], parts[PLANE:]
    far = [far[0]] + [swap(far[r], r) for r in range(1, PLANE)]
    near = [near[0]] + [swap(near[r], r) for r in range(1, PLANE)]
    far = spread(far, [jnp.bfloat16] * half, blk, bb_dev)
    near = spread(near, [jnp.float32] + [jnp.bfloat16] * (half - 1), blk, bb_dev)
    sums = list(near) + list(far)
    return total_of([sums[0]] + [swap(sums[dz], dz * PLANE) for dz in range(1, depth)])


def solution(mesh):
    return jax.shard_map(
        on_device,
        mesh=mesh,
        in_specs=(
            P(("grp", "aux"), None, None, None),
            P(("grp", "aux"), None),
            P("grp"),
            P(("grp", "aux")),
            P(("grp", "aux")),
            P(("grp", "aux")),
        ),
        out_specs=P(("grp", "aux"), None),
        check_vma=False,
    )
```

```python
import functools

import jax
import jax.numpy as jnp
from jax import lax
from jax.experimental import pallas as pl
from jax.experimental.pallas import tpu as pltpu
from jax.sharding import PartitionSpec as P

AB_DEV = 8
CHUNK = 4
UNROLL = 2
LOADS = 8
TAIL = 16
PLANE = 4
SPREAD_COST = 10**10
DIRECT = 16


def layout_of(slots, n_aux):
    chunks = slots // CHUNK + 2 * AB_DEV
    places = chunks * CHUNK
    return chunks, places, {
        "slot": 0,
        "block": places,
        "gid": 2 * places,
        "far": 2 * places + chunks,
        "all": 2 * places + chunks + 1,
        "bit": 2 * places + chunks + 2,
        "size": 2 * places + chunks + 2 + n_aux,
    }


def prepare(tiles, tile_block, tile_aux, live, basis_order, base, n_aux, split, gates):
    slots = tiles.shape[0]
    nbb = basis_order.shape[0]
    bb_dev = nbb // n_aux
    chunks, places, at = layout_of(slots, n_aux)
    step = slots // LOADS

    def kernel(block_ref, aux_ref, live_ref, order_ref, base_ref, source, *refs):
        target, meta, merged, inverse, owner, key_of, spot, sems = refs[len(gates) :]
        for i, gate in enumerate(refs[: len(gates)]):
            merged[i] = gate[...]
        copies = [
            pltpu.make_async_copy(
                source.at[pl.ds(i * step, step)], target.at[pl.ds(i * step, step)], sems.at[i]
            )
            for i in range(LOADS)
        ]
        for copy in copies:
            copy.start()

        @pl.loop(0, nbb)
        def _(k):
            inverse[order_ref[k]] = k

        @pl.loop(0, places)
        def _(i):
            meta[at["slot"] + i] = 0
            meta[at["block"] + i] = n_aux

        @pl.loop(0, chunks)
        def _(i):
            meta[at["gid"] + i] = 0

        @pl.loop(0, n_aux)
        def _(m):
            meta[at["bit"] + m] = 0

        for key in range(2 * AB_DEV):
            spot[key] = 0

        @pl.loop(0, live_ref[0])
        def _(t):
            k = inverse[block_ref[t]]
            m = (k // bb_dev) ^ base_ref[0]
            key = aux_ref[t] + jnp.where(m < split, AB_DEV, 0)
            owner[t] = m
            key_of[t] = key
            spot[key] = spot[key] + 1
            meta[at["bit"] + m] = k % bb_dev

        used = jnp.int32(0)
        for key in range(2 * AB_DEV):
            need = (spot[key] + CHUNK - 1) // CHUNK
            spot[key] = used * CHUNK
            used = used + need
            if key == AB_DEV - 1:
                meta[at["far"]] = used
        meta[at["all"]] = used

        @pl.loop(0, live_ref[0])
        def _(t):
            key = key_of[t]
            pos = spot[key]
            spot[key] = pos + 1
            meta[at["block"] + pos] = owner[t]
            meta[at["slot"] + pos] = t

            @pl.when(pos % CHUNK == 0)
            def _():
                for i in range(1, CHUNK):
                    meta[at["slot"] + pos + i] = t
                meta[at["gid"] + pos // CHUNK] = aux_ref[t]

        for copy in copies:
            copy.wait()

    smem = pl.BlockSpec(memory_space=pltpu.SMEM)
    hbm = pl.BlockSpec(memory_space=pl.ANY)
    vmem = pl.BlockSpec(memory_space=pltpu.VMEM)
    return pl.pallas_call(
        kernel,
        out_shape=[
            jax.ShapeDtypeStruct(tiles.shape, tiles.dtype),
            jax.ShapeDtypeStruct((at["size"],), jnp.int32),
            jax.ShapeDtypeStruct((len(gates),) + gates[0].shape, gates[0].dtype),
        ],
        in_specs=[smem] * 5 + [hbm] + [vmem] * len(gates),
        out_specs=[vmem, smem, vmem],
        scratch_shapes=[
            pltpu.SMEM((nbb,), jnp.int32),
            pltpu.SMEM((slots,), jnp.int32),
            pltpu.SMEM((slots,), jnp.int32),
            pltpu.SMEM((2 * AB_DEV,), jnp.int32),
            pltpu.SemaphoreType.DMA((LOADS,)),
        ],
        cost_estimate=pl.CostEstimate(flops=0, bytes_accessed=4 * tiles.size, transcendentals=0),
        compiler_params=pltpu.CompilerParams(vmem_limit_bytes=16 * 1024 * 1024),
        name="prepare",
    )(tile_block, tile_aux, live, basis_order, base, tiles, *gates)


def slab(tiles, slot):
    return jnp.concatenate([tiles[slot, p] for p in range(tiles.shape[1])], axis=1)


def apply_fitted(meta, at, tiles, zb, acc, low, high):
    blk = acc.shape[2]
    turns = (high - low + UNROLL - 1) // UNROLL

    @pl.loop(0, turns)
    def _(step):
        for chunk in [low + step * UNROLL + u for u in range(UNROLL)]:
            spots = [chunk * CHUNK + i for i in range(CHUNK)]
            right = jnp.concatenate(
                [slab(tiles, meta[at["slot"] + pos]) for pos in spots], axis=0
            )
            value = lax.dot_general(
                zb[meta[at["gid"] + chunk]],
                right,
                (((1,), (1,)), ((), ())),
                preferred_element_type=jnp.float32,
            )
            for i, pos in enumerate(spots):
                acc[meta[at["block"] + pos]] += value[:, i * blk : (i + 1) * blk]


def put(meta, at, acc, m, out_ref, place):
    nocc, blk = acc.shape[1:]
    out_ref[place, :nocc, :] = acc[m].astype(out_ref.dtype)
    out_ref[place, nocc:, :] = jnp.full((TAIL, blk), meta[at["bit"] + m], jnp.int32).astype(
        jnp.float32
    ).astype(out_ref.dtype)


def first_part(direct, n_aux, meta_array, tiles_array, shards, sources):
    slots, auxb, blk, nocc = tiles_array.shape
    chunks, places, at = layout_of(slots, n_aux)
    n_in = len(shards)

    def kernel(meta, tiles, *refs):
        c_refs, out_refs = refs[:n_in], refs[n_in:-4]
        zb, ct, zacc, acc = refs[-4:]
        far, total = meta[at["far"]], meta[at["all"]]

        def turn(m, source):
            row = pl.multiple_of(meta[at["bit"] + m] * blk, blk)
            ct[m] = source[pl.ds(row, blk), :].T

        if direct:
            for m in range(n_aux):
                ref, i = sources[m]
                turn(m, c_refs[ref] if i is None else c_refs[ref].at[i])
        else:
            @pl.loop(0, n_aux)
            def _(m):
                turn(m, c_refs[0].at[m])

        ct[n_aux] = jnp.zeros((nocc, blk), ct.dtype)
        acc[...] = jnp.zeros(acc.shape, acc.dtype)
        zacc[...] = jnp.zeros(zacc.shape, zacc.dtype)

        @pl.loop(0, (total + UNROLL - 1) // UNROLL)
        def _(step):
            for chunk in [step * UNROLL + u for u in range(UNROLL)]:
                spots = [chunk * CHUNK + i for i in range(CHUNK)]
                left = jnp.concatenate([ct[meta[at["block"] + pos]] for pos in spots], axis=1)
                right = jnp.concatenate(
                    [slab(tiles, meta[at["slot"] + pos]) for pos in spots], axis=0
                )
                zacc[meta[at["gid"] + chunk]] += jnp.dot(
                    left, right, preferred_element_type=jnp.float32
                )

        for g in range(AB_DEV):
            zb[g] = zacc[g].astype(zb.dtype)
        apply_fitted(meta, at, tiles, zb, acc, 0, far)
        if direct:
            for m in range(n_aux // 2, n_aux):
                put(meta, at, acc, m, out_refs[m % PLANE], (m - n_aux // 2) // PLANE)
        else:
            @pl.loop(0, n_aux)
            def _(m):
                put(meta, at, acc, m, out_refs[0], m)

    smem = pl.BlockSpec(memory_space=pltpu.SMEM)
    vmem = pl.BlockSpec(memory_space=pltpu.VMEM)
    if direct:
        shape = (n_aux // PLANE // 2, nocc + TAIL, blk)
        out_shape = [jax.ShapeDtypeStruct(shape, jnp.bfloat16)] * PLANE
    else:
        out_shape = [jax.ShapeDtypeStruct((n_aux, nocc + TAIL, blk), jnp.bfloat16)]
    out_shape = out_shape + [jax.ShapeDtypeStruct((AB_DEV, nocc, auxb * nocc), jnp.bfloat16)]
    return pl.pallas_call(
        kernel,
        out_shape=out_shape,
        in_specs=[smem] + [vmem] * (1 + n_in),
        out_specs=[vmem] * len(out_shape),
        scratch_shapes=[
            pltpu.VMEM((n_aux + 1, nocc, blk), jnp.bfloat16),
            pltpu.VMEM((AB_DEV, nocc, auxb * nocc), jnp.float32),
            pltpu.VMEM((n_aux + 1, nocc, blk), jnp.float32),
        ],
        compiler_params=pltpu.CompilerParams(
            vmem_limit_bytes=(20 if direct else 46) * 1024 * 1024
        ),
        cost_estimate=pl.CostEstimate(
            flops=3 * tiles_array.size * nocc, bytes_accessed=tiles_array.size, transcendentals=0
        ),
        name="first_part",
    )(meta_array, tiles_array, *shards)


def second_part(n_aux, meta_array, tiles_array, fitted):
    slots, auxb, blk, nocc = tiles_array.shape
    chunks, places, at = layout_of(slots, n_aux)

    def kernel(meta, tiles, zb, *refs):
        out_refs, acc = refs[:-1], refs[-1]
        acc[...] = jnp.zeros(acc.shape, acc.dtype)
        apply_fitted(meta, at, tiles, zb, acc, meta[at["far"]], meta[at["all"]])
        for m in range(n_aux // 2):
            put(meta, at, acc, m, out_refs[m % PLANE], m // PLANE)

    smem = pl.BlockSpec(memory_space=pltpu.SMEM)
    vmem = pl.BlockSpec(memory_space=pltpu.VMEM)
    shape = (n_aux // PLANE // 2, nocc + TAIL, blk)
    return pl.pallas_call(
        kernel,
        out_shape=[jax.ShapeDtypeStruct(shape, jnp.bfloat16)] * PLANE,
        in_specs=[smem, vmem, vmem],
        out_specs=[vmem] * PLANE,
        scratch_shapes=[pltpu.VMEM((n_aux + 1, nocc, blk), jnp.float32)],
        compiler_params=pltpu.CompilerParams(vmem_limit_bytes=20 * 1024 * 1024),
        cost_estimate=pl.CostEstimate(
            flops=10**10, bytes_accessed=tiles_array.size, transcendentals=0
        ),
        name="second_part",
    )(meta_array, tiles_array, fitted)


def spread(parts, after, dtypes, blk, bb_dev):
    count, rows, nocc = parts[0].shape

    def kernel(*refs):
        sources, targets = refs[: len(parts)], refs[len(parts) + len(after) :]
        for i in range(count):
            sums = [jnp.zeros((blk, nocc), jnp.float32) for _ in range(bb_dev)]
            for source in sources:
                value = source[i, :blk, :].astype(jnp.float32)
                which = source[i, blk:, :][:1].astype(jnp.float32)
                for b in range(bb_dev):
                    sums[b] = sums[b] + jnp.where(which == b, value, 0.0)
            for b in range(bb_dev):
                targets[i][b * blk : (b + 1) * blk, :] = sums[b].astype(targets[i].dtype)

    vmem = pl.BlockSpec(memory_space=pltpu.VMEM)
    return pl.pallas_call(
        kernel,
        out_shape=[jax.ShapeDtypeStruct((bb_dev * blk, nocc), dtype) for dtype in dtypes],
        in_specs=[vmem] * len(parts) + [pl.BlockSpec(memory_space=pl.ANY)] * len(after),
        out_specs=[vmem] * count,
        compiler_params=pltpu.CompilerParams(vmem_limit_bytes=4 * 1024 * 1024),
        cost_estimate=pl.CostEstimate(
            flops=SPREAD_COST, bytes_accessed=SPREAD_COST // 1000, transcendentals=0
        ),
        name="spread",
    )(*parts, *after)


def total_of(arrays, blk):
    rows, nocc = arrays[0].shape

    def kernel(*refs):
        value = refs[0][...].astype(jnp.float32)
        for ref in refs[1:-1]:
            value = value + ref[...].astype(jnp.float32)
        for row in range(0, rows, blk):
            refs[-1][row : row + blk, :] = value[row : row + blk].T.astype(refs[-1].dtype)

    vmem = pl.BlockSpec(memory_space=pltpu.VMEM)
    return pl.pallas_call(
        kernel,
        out_shape=jax.ShapeDtypeStruct((rows, nocc), jnp.bfloat16),
        in_specs=[vmem] * len(arrays),
        out_specs=vmem,
        compiler_params=pltpu.CompilerParams(vmem_limit_bytes=4 * 1024 * 1024),
        name="total_of",
    )(*arrays)


def owner_sum(parts, blk, bb_dev):
    n_aux, rows, nocc = parts.shape

    def kernel(parts_ref, out_ref):
        sums = [jnp.zeros((blk, nocc), jnp.float32) for _ in range(bb_dev)]
        for s in range(n_aux):
            value = parts_ref[s, :blk, :].astype(jnp.float32)
            which = parts_ref[s, blk:, :][:1].astype(jnp.float32)
            for b in range(bb_dev):
                sums[b] = sums[b] + jnp.where(which == b, value, 0.0)
        for b in range(bb_dev):
            out_ref[b * blk : (b + 1) * blk, :] = sums[b].T.astype(out_ref.dtype)

    vmem = pl.BlockSpec(memory_space=pltpu.VMEM)
    return pl.pallas_call(
        kernel,
        out_shape=jax.ShapeDtypeStruct((bb_dev * blk, nocc), jnp.bfloat16),
        in_specs=[vmem],
        out_specs=vmem,
        name="owner_sum",
    )(parts)


def on_device(tiles, c_orbitals, basis_order, tile_block, tile_aux, live):
    blk, nocc = tiles.shape[2:]
    n_aux = lax.axis_size("aux")
    bb_dev = basis_order.shape[0] // n_aux
    direct = n_aux == DIRECT

    def swap(array, m):
        return lax.ppermute(array, "aux", [(i, i ^ m) for i in range(n_aux)])

    def ready(base, split, gates):
        return prepare(
            tiles, tile_block, tile_aux, live, basis_order, base, n_aux, split, gates
        )

    if not direct:
        held, meta, _ = ready(jnp.zeros((1,), jnp.int32), 0, [c_orbitals])
        whole = lax.all_gather(c_orbitals, "aux", axis=0, tiled=True)
        shards = [whole.reshape(n_aux, bb_dev * blk, nocc)]
        parts, _ = first_part(direct, n_aux, meta, held, shards, None)
        moved = lax.all_to_all(parts, "aux", 0, 0, tiled=True)
        return owner_sum(moved, blk, bb_dev)

    depth = n_aux // PLANE
    half = depth // 2
    column = [c_orbitals] + [None] * (depth - 1)
    for dz in range(depth - 1, 0, -1):
        column[dz] = swap(c_orbitals, dz * PLANE)
    base = lax.axis_index("aux").astype(jnp.int32)[None]
    beside = swap(c_orbitals, 2)
    held, meta, early = ready(base, n_aux // 2, column + [beside])
    late = [swap(array, 2) for array in column[1:]]
    shards = [early, swap(early, 1)] + late + [swap(array, 1) for array in late]
    sources = [None] * n_aux
    for dz in range(depth):
        for core in range(2):
            sources[dz * PLANE + core] = (core, dz)
            sources[dz * PLANE + 2 + core] = (
                (core, depth) if dz == 0 else (1 + dz + core * (depth - 1), None)
            )
    *far, fitted = first_part(direct, n_aux, meta, held, shards, sources)
    far = [far[0]] + [swap(far[r], r) for r in range(1, PLANE)]
    near = second_part(n_aux, meta, held, fitted)
    near = [near[0]] + [swap(near[r], r) for r in range(1, PLANE)]
    far = spread(far, [], [jnp.bfloat16] * half, blk, bb_dev)
    near = spread(
        near, [far[0]], [jnp.float32] + [jnp.bfloat16] * (half - 1), blk, bb_dev
    )
    sums = list(near) + list(far)
    return total_of([sums[0]] + [swap(sums[dz], dz * PLANE) for dz in range(1, depth)], blk)


def solution(mesh):
    return jax.shard_map(
        on_device,
        mesh=mesh,
        in_specs=(
            P(("grp", "aux"), None, None, None),
            P(("grp", "aux"), None),
            P("grp"),
            P(("grp", "aux")),
            P(("grp", "aux")),
            P(("grp", "aux")),
        ),
        out_specs=P(("grp", "aux"), None),
        check_vma=False,
    )
```

```python
import functools

import jax
import jax.numpy as jnp
from jax import lax
from jax.experimental import pallas as pl
from jax.experimental.pallas import tpu as pltpu
from jax.sharding import PartitionSpec as P

AB_DEV = 8
CHUNK = 4
UNROLL = 2
AHEAD = 8
FIRST_VMEM = 36
TAIL = 16
PLANE = 4
SPREAD_COST = 10**10
DIRECT = 16


def plan(tile_block, tile_aux, live, basis_order, base, split, n_aux, bb_dev):
    slots = tile_block.shape[0]
    nbb = basis_order.shape[0]
    keys = 2 * AB_DEV
    chunks = slots // CHUNK + keys
    t = lax.iota(jnp.int32, slots)
    alive = t < live[0]
    position = jnp.sum(
        jnp.where(
            basis_order[None, :] == tile_block[:, None], lax.iota(jnp.int32, nbb)[None, :], 0
        ),
        axis=1,
    )
    where_to = jnp.bitwise_xor(position // bb_dev, base)
    which = position % bb_dev
    group = jnp.where(alive, tile_aux + jnp.where(where_to < split, AB_DEV, 0), keys)
    ids = lax.iota(jnp.int32, keys)
    counts = jnp.sum((group[None, :] == ids[:, None]).astype(jnp.int32), axis=1)
    need = (counts + CHUNK - 1) // CHUNK
    ends = jnp.sum(jnp.where(ids[None, :] <= ids[:, None], need[None, :], 0), axis=1)
    rank = jnp.sum(
        ((group[None, :] == group[:, None]) & (t[None, :] < t[:, None])).astype(jnp.int32), axis=1
    )
    start = jnp.sum(jnp.where(group[:, None] > ids[None, :], need[None, :], 0), axis=1)
    place = jnp.where(alive, start * CHUNK + rank, -1)
    q = lax.iota(jnp.int32, chunks * CHUNK)
    hit = place[None, :] == q[:, None]
    lead = place[None, :] == (q // CHUNK * CHUNK)[:, None]
    valid = jnp.any(hit, axis=1)
    slot = jnp.sum(jnp.where(hit, t[None, :], 0), axis=1)
    slot = jnp.where(valid, slot, jnp.sum(jnp.where(lead, t[None, :], 0), axis=1))
    block = jnp.where(valid, jnp.sum(jnp.where(hit, where_to[None, :], 0), axis=1), n_aux)
    gid = jnp.sum(
        (lax.iota(jnp.int32, chunks)[:, None] >= ends[None, :]).astype(jnp.int32), axis=1
    )
    bit = jnp.max(
        jnp.where(
            (where_to[None, :] == lax.iota(jnp.int32, n_aux)[:, None]) & alive[None, :],
            which[None, :],
            0,
        ),
        axis=1,
    )
    gid = gid % AB_DEV
    return slot, block, jnp.concatenate([gid, ends]), bit


def slab(tiles, slot):
    return jnp.concatenate([tiles[slot, p] for p in range(tiles.shape[1])], axis=1)


def apply_fitted(meta, tiles, zb, acc, low, high):
    slot_ref, block_ref, gid_ref, _ = meta
    blk = acc.shape[1]

    @pl.loop(0, (high - low + UNROLL - 1) // UNROLL)
    def _(step):
        for chunk in [low + step * UNROLL + u for u in range(UNROLL)]:
            spots = [chunk * CHUNK + i for i in range(CHUNK)]
            left = jnp.concatenate([slab(tiles, slot_ref[pos]) for pos in spots], axis=0)
            value = jnp.dot(left, zb[gid_ref[chunk]], preferred_element_type=jnp.float32)
            for i, pos in enumerate(spots):
                acc[block_ref[pos]] += value[i * blk : (i + 1) * blk]


def put(bit_ref, acc, m, out_ref, place):
    blk, nocc = acc.shape[1:]
    out_ref[place, :blk, :] = acc[m].astype(out_ref.dtype)
    out_ref[place, blk:, :] = jnp.full((TAIL, nocc), bit_ref[m], jnp.int32).astype(
        jnp.float32
    ).astype(out_ref.dtype)


def first_part(direct, n_aux, meta_arrays, tiles_array, own_array, shards, sources):
    slots, auxb, blk, nocc = tiles_array.shape
    chunks = slots // CHUNK + 2 * AB_DEV
    n_in = len(shards)

    def kernel(slot_ref, block_ref, gid_ref, bit_ref, tiles_hbm, own_hbm, *refs):
        c_refs, out_refs = refs[:n_in], refs[n_in:-8]
        zb, tiles, ct, zacc, acc, own, sems, own_sem = refs[-8:]
        own_copy = pltpu.make_async_copy(own_hbm, own, own_sem)
        own_copy.start()
        far = gid_ref[chunks + AB_DEV - 1]
        total = gid_ref[chunks + 2 * AB_DEV - 1]

        def each(chunk, act):
            for i in range(CHUNK):
                pos = chunk * CHUNK + i
                copy = pltpu.make_async_copy(
                    tiles_hbm.at[slot_ref[pos]], tiles.at[slot_ref[pos]], sems.at[chunk]
                )

                @pl.when(block_ref[pos] < n_aux)
                def _():
                    act(copy)

        @pl.loop(0, jnp.minimum(total, AHEAD))
        def _(chunk):
            each(chunk, lambda copy: copy.start())

        def turn(m, source):
            row = pl.multiple_of(bit_ref[m] * blk, blk)
            ct[m] = source[pl.ds(row, blk), :].T

        if direct:
            for m in range(1, n_aux):
                ref, i = sources[m]
                turn(m, c_refs[ref] if i is None else c_refs[ref].at[i])
        else:
            @pl.loop(0, n_aux)
            def _(m):
                turn(m, c_refs[0].at[m])

        own_copy.wait()
        if direct:
            turn(0, own)
        ct[n_aux] = jnp.zeros((nocc, blk), ct.dtype)
        acc[...] = jnp.zeros(acc.shape, acc.dtype)
        zacc[...] = jnp.zeros(zacc.shape, zacc.dtype)

        @pl.loop(0, (total + UNROLL - 1) // UNROLL)
        def _(step):
            group = [step * UNROLL + u for u in range(UNROLL)]
            for chunk in group:
                @pl.when(chunk + AHEAD < total)
                def _():
                    each(chunk + AHEAD, lambda copy: copy.start())
            for chunk in group:
                each(chunk, lambda copy: copy.wait())
            for chunk in group:
                spots = [chunk * CHUNK + i for i in range(CHUNK)]
                left = jnp.concatenate([ct[block_ref[pos]] for pos in spots], axis=1)
                right = jnp.concatenate([slab(tiles, slot_ref[pos]) for pos in spots], axis=0)
                zacc[gid_ref[chunk]] += jnp.dot(left, right, preferred_element_type=jnp.float32)

        for g in range(AB_DEV):
            for p in range(auxb):
                part = zacc[g, :, p * nocc : (p + 1) * nocc].astype(zb.dtype)
                zb[g, p * nocc : (p + 1) * nocc, :] = part.T
        apply_fitted((slot_ref, block_ref, gid_ref, bit_ref), tiles, zb, acc, 0, far)
        if direct:
            for m in range(n_aux // 2, n_aux):
                put(bit_ref, acc, m, out_refs[m % PLANE], (m - n_aux // 2) // PLANE)
        else:
            @pl.loop(0, n_aux)
            def _(m):
                put(bit_ref, acc, m, out_refs[0], m)

    smem = pl.BlockSpec(memory_space=pltpu.SMEM)
    vmem = pl.BlockSpec(memory_space=pltpu.VMEM)
    if direct:
        shape = (n_aux // PLANE // 2, blk + TAIL, nocc)
        out_shape = [jax.ShapeDtypeStruct(shape, jnp.bfloat16)] * PLANE
    else:
        out_shape = [jax.ShapeDtypeStruct((n_aux, blk + TAIL, nocc), jnp.bfloat16)]
    out_shape = out_shape + [
        jax.ShapeDtypeStruct((AB_DEV, auxb * nocc, nocc), jnp.bfloat16),
        jax.ShapeDtypeStruct(tiles_array.shape, tiles_array.dtype),
    ]
    return pl.pallas_call(
        kernel,
        out_shape=out_shape,
        in_specs=[smem] * 4 + [pl.BlockSpec(memory_space=pl.ANY)] * 2 + [vmem] * n_in,
        out_specs=[vmem] * len(out_shape),
        scratch_shapes=[
            pltpu.VMEM((n_aux + 1, nocc, blk), jnp.bfloat16),
            pltpu.VMEM((AB_DEV, nocc, auxb * nocc), jnp.float32),
            pltpu.VMEM((n_aux + 1, blk, nocc), jnp.float32),
            pltpu.VMEM(own_array.shape, own_array.dtype),
            pltpu.SemaphoreType.DMA((chunks,)),
            pltpu.SemaphoreType.DMA,
        ],
        compiler_params=pltpu.CompilerParams(vmem_limit_bytes=FIRST_VMEM * 1024 * 1024),
        cost_estimate=pl.CostEstimate(
            flops=3 * tiles_array.size * nocc, bytes_accessed=tiles_array.size, transcendentals=0
        ),
        name="first_part",
    )(*meta_arrays, tiles_array, own_array, *shards)


def second_part(n_aux, meta_arrays, tiles_array, fitted):
    slots, auxb, blk, nocc = tiles_array.shape
    chunks = slots // CHUNK + 2 * AB_DEV

    def kernel(slot_ref, block_ref, gid_ref, bit_ref, tiles, zb, *refs):
        out_refs, acc = refs[:-1], refs[-1]
        acc[...] = jnp.zeros(acc.shape, acc.dtype)
        apply_fitted(
            (slot_ref, block_ref, gid_ref, bit_ref),
            tiles,
            zb,
            acc,
            gid_ref[chunks + AB_DEV - 1],
            gid_ref[chunks + 2 * AB_DEV - 1],
        )
        for m in range(n_aux // 2):
            put(bit_ref, acc, m, out_refs[m % PLANE], m // PLANE)

    smem = pl.BlockSpec(memory_space=pltpu.SMEM)
    vmem = pl.BlockSpec(memory_space=pltpu.VMEM)
    shape = (n_aux // PLANE // 2, blk + TAIL, nocc)
    return pl.pallas_call(
        kernel,
        out_shape=[jax.ShapeDtypeStruct(shape, jnp.bfloat16)] * PLANE,
        in_specs=[smem] * 4 + [vmem, vmem],
        out_specs=[vmem] * PLANE,
        scratch_shapes=[pltpu.VMEM((n_aux + 1, blk, nocc), jnp.float32)],
        compiler_params=pltpu.CompilerParams(vmem_limit_bytes=20 * 1024 * 1024),
        cost_estimate=pl.CostEstimate(
            flops=10**10, bytes_accessed=tiles_array.size, transcendentals=0
        ),
        name="second_part",
    )(*meta_arrays, tiles_array, fitted)


def merge(arrays):
    def kernel(*refs):
        for i, ref in enumerate(refs[:-1]):
            refs[-1][i] = ref[...]

    vmem = pl.BlockSpec(memory_space=pltpu.VMEM)
    return pl.pallas_call(
        kernel,
        out_shape=jax.ShapeDtypeStruct((len(arrays),) + arrays[0].shape, arrays[0].dtype),
        in_specs=[vmem] * len(arrays),
        out_specs=vmem,
        compiler_params=pltpu.CompilerParams(vmem_limit_bytes=4 * 1024 * 1024),
        name="merge",
    )(*arrays)


def spread(parts, after, dtypes, blk, bb_dev):
    count, rows, nocc = parts[0].shape

    def kernel(*refs):
        sources, targets = refs[: len(parts)], refs[len(parts) + len(after) :]
        for i in range(count):
            sums = [jnp.zeros((blk, nocc), jnp.float32) for _ in range(bb_dev)]
            for source in sources:
                value = source[i, :blk, :].astype(jnp.float32)
                which = source[i, blk:, :][:1].astype(jnp.float32)
                for b in range(bb_dev):
                    sums[b] = sums[b] + jnp.where(which == b, value, 0.0)
            for b in range(bb_dev):
                targets[i][b * blk : (b + 1) * blk, :] = sums[b].astype(targets[i].dtype)

    vmem = pl.BlockSpec(memory_space=pltpu.VMEM)
    return pl.pallas_call(
        kernel,
        out_shape=[jax.ShapeDtypeStruct((bb_dev * blk, nocc), dtype) for dtype in dtypes],
        in_specs=[vmem] * len(parts) + [pl.BlockSpec(memory_space=pl.ANY)] * len(after),
        out_specs=[vmem] * count,
        compiler_params=pltpu.CompilerParams(vmem_limit_bytes=4 * 1024 * 1024),
        cost_estimate=pl.CostEstimate(
            flops=SPREAD_COST, bytes_accessed=SPREAD_COST // 1000, transcendentals=0
        ),
        name="spread",
    )(*parts, *after)


def total_of(arrays, dtype, cost):
    def kernel(*refs):
        value = refs[0][...].astype(jnp.float32)
        for ref in refs[1:-1]:
            value = value + ref[...].astype(jnp.float32)
        refs[-1][...] = value.astype(refs[-1].dtype)

    vmem = pl.BlockSpec(memory_space=pltpu.VMEM)
    return pl.pallas_call(
        kernel,
        out_shape=jax.ShapeDtypeStruct(arrays[0].shape, dtype),
        in_specs=[vmem] * len(arrays),
        out_specs=vmem,
        compiler_params=pltpu.CompilerParams(vmem_limit_bytes=4 * 1024 * 1024),
        cost_estimate=pl.CostEstimate(flops=cost, bytes_accessed=cost // 1000, transcendentals=0),
        name="total_of",
    )(*arrays)


def owner_sum(parts, blk, bb_dev):
    n_aux, rows, nocc = parts.shape

    def kernel(parts_ref, out_ref):
        sums = [jnp.zeros((blk, nocc), jnp.float32) for _ in range(bb_dev)]
        for s in range(n_aux):
            value = parts_ref[s, :blk, :].astype(jnp.float32)
            which = parts_ref[s, blk:, :][:1].astype(jnp.float32)
            for b in range(bb_dev):
                sums[b] = sums[b] + jnp.where(which == b, value, 0.0)
        for b in range(bb_dev):
            out_ref[b * blk : (b + 1) * blk, :] = sums[b].astype(out_ref.dtype)

    vmem = pl.BlockSpec(memory_space=pltpu.VMEM)
    return pl.pallas_call(
        kernel,
        out_shape=jax.ShapeDtypeStruct((bb_dev * blk, nocc), jnp.bfloat16),
        in_specs=[vmem],
        out_specs=vmem,
        name="owner_sum",
    )(parts)


def on_device(tiles, c_orbitals, basis_order, tile_block, tile_aux, live):
    blk, nocc = tiles.shape[2:]
    n_aux = lax.axis_size("aux")
    bb_dev = basis_order.shape[0] // n_aux
    direct = n_aux == DIRECT

    def swap(array, m):
        return lax.ppermute(array, "aux", [(i, i ^ m) for i in range(n_aux)])

    base = lax.axis_index("aux").astype(jnp.int32) if direct else jnp.int32(0)
    split = n_aux // 2 if direct else 0
    meta = plan(tile_block, tile_aux, live, basis_order, base, split, n_aux, bb_dev)
    if not direct:
        whole = lax.all_gather(c_orbitals, "aux", axis=0, tiled=True)
        shards = [whole.reshape(n_aux, bb_dev * blk, nocc)]
        parts, _, _ = first_part(direct, n_aux, meta, tiles, c_orbitals, shards, None)
        moved = lax.all_to_all(parts, "aux", 0, 0, tiled=True)
        return owner_sum(moved, blk, bb_dev)

    depth = n_aux // PLANE
    half = depth // 2
    column = [c_orbitals] + [None] * (depth - 1)
    for dz in range(depth - 1, 0, -1):
        column[dz] = swap(c_orbitals, dz * PLANE)
    beside = swap(c_orbitals, 2)
    across = swap(c_orbitals, 1)
    early = merge(column[1:] + [beside])
    late = [swap(array, 2) for array in column[1:]]
    shards = [early, swap(early, 1), across] + late + [swap(array, 1) for array in late]
    sources = [None] * n_aux
    for dz in range(1, depth):
        for core in range(2):
            sources[dz * PLANE + core] = (core, dz - 1)
            sources[dz * PLANE + 2 + core] = (2 + dz + core * (depth - 1), None)
    sources[1:PLANE] = [(2, None), (0, depth - 1), (1, depth - 1)]
    *far, fitted, held = first_part(direct, n_aux, meta, tiles, c_orbitals, shards, sources)
    far = [far[0]] + [swap(far[r], r) for r in range(1, PLANE)]
    near = second_part(n_aux, meta, held, fitted)
    near = [near[0]] + [swap(near[r], r) for r in range(1, PLANE)]
    far = spread(far, [], [jnp.bfloat16] * half, blk, bb_dev)
    near = spread(
        near, [far[0]], [jnp.float32] + [jnp.bfloat16] * (half - 1), blk, bb_dev
    )
    far = [swap(far[i], (half + i) * PLANE) for i in range(half)]
    far = total_of(far, jnp.float32, SPREAD_COST)
    near = [near[0]] + [swap(near[dz], dz * PLANE) for dz in range(1, half)]
    return total_of(near + [far], jnp.bfloat16, 0)


def solution(mesh):
    return jax.shard_map(
        on_device,
        mesh=mesh,
        in_specs=(
            P(("grp", "aux"), None, None, None),
            P(("grp", "aux"), None),
            P("grp"),
            P(("grp", "aux")),
            P(("grp", "aux")),
            P(("grp", "aux")),
        ),
        out_specs=P(("grp", "aux"), None),
        check_vma=False,
    )
```

```python
import functools

import jax
import jax.numpy as jnp
from jax import lax
from jax.experimental import pallas as pl
from jax.experimental.pallas import tpu as pltpu
from jax.sharding import PartitionSpec as P

AB_DEV = 8
CHUNK = 4
UNROLL = 2
LOADS = 8
BEGIN_VMEM = 40
TAIL = 16
PLANE = 4
SPREAD_COST = 10**10
DIRECT = 16


def owners_of(tile_block, basis_order, base, bb_dev):
    nbb = basis_order.shape[0]
    position = jnp.sum(
        jnp.where(
            basis_order[None, :] == tile_block[:, None], lax.iota(jnp.int32, nbb)[None, :], 0
        ),
        axis=1,
    )
    return jnp.bitwise_xor(position // bb_dev, base), position % bb_dev


def chunk_lists(where_to, later, alive, tile_aux, n_aux):
    slots = where_to.shape[0]
    keys = 2 * AB_DEV
    chunks = slots // CHUNK + keys
    t = lax.iota(jnp.int32, slots)
    group = jnp.where(alive, tile_aux + jnp.where(later, AB_DEV, 0), keys)
    ids = lax.iota(jnp.int32, keys)
    counts = jnp.sum((group[None, :] == ids[:, None]).astype(jnp.int32), axis=1)
    need = (counts + CHUNK - 1) // CHUNK
    ends = jnp.sum(jnp.where(ids[None, :] <= ids[:, None], need[None, :], 0), axis=1)
    rank = jnp.sum(
        ((group[None, :] == group[:, None]) & (t[None, :] < t[:, None])).astype(jnp.int32), axis=1
    )
    start = jnp.sum(jnp.where(group[:, None] > ids[None, :], need[None, :], 0), axis=1)
    place = jnp.where(alive, start * CHUNK + rank, -1)
    q = lax.iota(jnp.int32, chunks * CHUNK)
    hit = place[None, :] == q[:, None]
    lead = place[None, :] == (q // CHUNK * CHUNK)[:, None]
    valid = jnp.any(hit, axis=1)
    slot = jnp.sum(jnp.where(hit, t[None, :], 0), axis=1)
    slot = jnp.where(valid, slot, jnp.sum(jnp.where(lead, t[None, :], 0), axis=1))
    block = jnp.where(valid, jnp.sum(jnp.where(hit, where_to[None, :], 0), axis=1), n_aux)
    gid = jnp.sum(
        (lax.iota(jnp.int32, chunks)[:, None] >= ends[None, :]).astype(jnp.int32), axis=1
    )
    return slot, block, jnp.concatenate([gid % AB_DEV, ends])


def bits_of(where_to, which, alive, n_aux):
    return jnp.max(
        jnp.where(
            (where_to[None, :] == lax.iota(jnp.int32, n_aux)[:, None]) & alive[None, :],
            which[None, :],
            0,
        ),
        axis=1,
    )


def slab(tiles, slot):
    return jnp.concatenate([tiles[slot, p] for p in range(tiles.shape[1])], axis=1)


def chunk_ends(gid_ref, slots):
    chunks = slots // CHUNK + 2 * AB_DEV
    return gid_ref[chunks + AB_DEV - 1], gid_ref[chunks + 2 * AB_DEV - 1]


def turn(ct, bit_ref, m, source):
    blk = ct.shape[2]
    row = pl.multiple_of(bit_ref[m] * blk, blk)
    ct[m] = source[pl.ds(row, blk), :].T


def fit(lists, tiles, ct, zacc, low, high):
    slot_ref, block_ref, gid_ref = lists

    @pl.loop(0, (high - low + UNROLL - 1) // UNROLL)
    def _(step):
        for chunk in [low + step * UNROLL + u for u in range(UNROLL)]:
            keep = jnp.where(chunk < high, 0, ct.shape[0] - 1)
            spots = [chunk * CHUNK + i for i in range(CHUNK)]
            left = jnp.concatenate(
                [ct[jnp.maximum(block_ref[pos], keep)] for pos in spots], axis=1
            )
            right = jnp.concatenate([slab(tiles, slot_ref[pos]) for pos in spots], axis=0)
            zacc[gid_ref[chunk]] += jnp.dot(left, right, preferred_element_type=jnp.float32)


def apply_fitted(lists, tiles, zb, acc, low, high):
    slot_ref, block_ref, gid_ref = lists
    blk = acc.shape[1]

    @pl.loop(0, (high - low + UNROLL - 1) // UNROLL)
    def _(step):
        for chunk in [low + step * UNROLL + u for u in range(UNROLL)]:
            spots = [chunk * CHUNK + i for i in range(CHUNK)]
            left = jnp.concatenate([slab(tiles, slot_ref[pos]) for pos in spots], axis=0)
            value = jnp.dot(left, zb[gid_ref[chunk]], preferred_element_type=jnp.float32)
            for i, pos in enumerate(spots):
                acc[block_ref[pos]] += value[i * blk : (i + 1) * blk]


def begin(n_aux, lists, bit, tiles_array, own_array, shards, sources):
    slots, auxb, blk, nocc = tiles_array.shape
    n_in = len(shards)
    step = slots // LOADS

    def kernel(slot_ref, block_ref, gid_ref, bit_ref, tiles_hbm, own_hbm, *refs):
        c_refs, (tiles, zacc, ct, own, sems, own_sem) = refs[:n_in], refs[n_in:]
        own_copy = pltpu.make_async_copy(own_hbm, own, own_sem)
        own_copy.start()
        copies = [
            pltpu.make_async_copy(
                tiles_hbm.at[pl.ds(i * step, step)], tiles.at[pl.ds(i * step, step)], sems.at[i]
            )
            for i in range(LOADS)
        ]
        for copy in copies:
            copy.start()
        zacc[...] = jnp.zeros(zacc.shape, zacc.dtype)
        ct[n_aux] = jnp.zeros((nocc, blk), ct.dtype)
        for m, (ref, i) in sources:
            turn(ct, bit_ref, m, c_refs[ref] if i is None else c_refs[ref].at[i])
        own_copy.wait()
        turn(ct, bit_ref, 0, own)
        for copy in copies:
            copy.wait()
        early, _ = chunk_ends(gid_ref, slots)
        fit((slot_ref, block_ref, gid_ref), tiles, ct, zacc, 0, early)

    smem = pl.BlockSpec(memory_space=pltpu.SMEM)
    vmem = pl.BlockSpec(memory_space=pltpu.VMEM)
    hbm = pl.BlockSpec(memory_space=pl.ANY)
    return pl.pallas_call(
        kernel,
        out_shape=[
            jax.ShapeDtypeStruct(tiles_array.shape, tiles_array.dtype),
            jax.ShapeDtypeStruct((AB_DEV, nocc, auxb * nocc), jnp.float32),
        ],
        in_specs=[smem] * 4 + [hbm] * 2 + [vmem] * n_in,
        out_specs=[vmem] * 2,
        scratch_shapes=[
            pltpu.VMEM((n_aux + 1, nocc, blk), jnp.bfloat16),
            pltpu.VMEM(own_array.shape, own_array.dtype),
            pltpu.SemaphoreType.DMA((LOADS,)),
            pltpu.SemaphoreType.DMA,
        ],
        compiler_params=pltpu.CompilerParams(vmem_limit_bytes=BEGIN_VMEM * 1024 * 1024),
        cost_estimate=pl.CostEstimate(
            flops=2 * tiles_array.size * nocc, bytes_accessed=tiles_array.size, transcendentals=0
        ),
        name="begin",
    )(*lists, bit, tiles_array, own_array, *shards)


def put(bit_ref, acc, m, out_ref, place):
    blk, nocc = acc.shape[1:]
    out_ref[place, :blk, :] = acc[m].astype(out_ref.dtype)
    out_ref[place, blk:, :] = jnp.full((TAIL, nocc), bit_ref[m], jnp.int32).astype(
        jnp.float32
    ).astype(out_ref.dtype)


def clear_and_fit(n_aux, ct, acc):
    ct[n_aux] = jnp.zeros(ct.shape[1:], ct.dtype)
    acc[...] = jnp.zeros(acc.shape, acc.dtype)


def round_fitted(zacc, zb):
    groups, nocc, wide = zacc.shape
    for g in range(groups):
        for p in range(wide // nocc):
            part = zacc[g, :, p * nocc : (p + 1) * nocc].astype(zb.dtype)
            zb[g, p * nocc : (p + 1) * nocc, :] = part.T


def first_part(n_aux, fit_lists, lists, bit, tiles_array, partial_fit, shards, sources):
    slots, auxb, blk, nocc = tiles_array.shape
    n_in = len(shards)

    def kernel(*refs):
        fit_refs, refs = refs[:3], refs[3:]
        list_refs, bit_ref, tiles, partial_ref = refs[:3], refs[3], refs[4], refs[5]
        c_refs, out_refs = refs[6 : 6 + n_in], refs[6 + n_in : -4]
        zb, ct, zacc, acc = refs[-4:]
        clear_and_fit(n_aux, ct, acc)
        zacc[...] = partial_ref[...]
        for m, (ref, i) in sources:
            turn(ct, bit_ref, m, c_refs[ref] if i is None else c_refs[ref].at[i])
        fit(fit_refs, tiles, ct, zacc, *chunk_ends(fit_refs[2], slots))
        round_fitted(zacc, zb)
        far, _ = chunk_ends(list_refs[2], slots)
        apply_fitted(list_refs, tiles, zb, acc, 0, far)
        for m in range(n_aux // 2, n_aux):
            put(bit_ref, acc, m, out_refs[m % PLANE], (m - n_aux // 2) // PLANE)

    smem = pl.BlockSpec(memory_space=pltpu.SMEM)
    vmem = pl.BlockSpec(memory_space=pltpu.VMEM)
    shape = (n_aux // PLANE // 2, blk + TAIL, nocc)
    out_shape = [jax.ShapeDtypeStruct(shape, jnp.bfloat16)] * PLANE
    out_shape = out_shape + [jax.ShapeDtypeStruct((AB_DEV, auxb * nocc, nocc), jnp.bfloat16)]
    return pl.pallas_call(
        kernel,
        out_shape=out_shape,
        in_specs=[smem] * 7 + [vmem] * (2 + n_in),
        out_specs=[vmem] * len(out_shape),
        scratch_shapes=[
            pltpu.VMEM((n_aux + 1, nocc, blk), jnp.bfloat16),
            pltpu.VMEM((AB_DEV, nocc, auxb * nocc), jnp.float32),
            pltpu.VMEM((n_aux + 1, blk, nocc), jnp.float32),
        ],
        compiler_params=pltpu.CompilerParams(vmem_limit_bytes=20 * 1024 * 1024),
        cost_estimate=pl.CostEstimate(
            flops=3 * tiles_array.size * nocc, bytes_accessed=tiles_array.size, transcendentals=0
        ),
        name="first_part",
    )(*fit_lists, *lists, bit, tiles_array, partial_fit, *shards)


def second_part(n_aux, lists, bit, tiles_array, fitted):
    slots, auxb, blk, nocc = tiles_array.shape

    def kernel(slot_ref, block_ref, gid_ref, bit_ref, tiles, zb, *refs):
        out_refs, acc = refs[:-1], refs[-1]
        acc[...] = jnp.zeros(acc.shape, acc.dtype)
        apply_fitted(
            (slot_ref, block_ref, gid_ref), tiles, zb, acc, *chunk_ends(gid_ref, slots)
        )
        for m in range(n_aux // 2):
            put(bit_ref, acc, m, out_refs[m % PLANE], m // PLANE)

    smem = pl.BlockSpec(memory_space=pltpu.SMEM)
    vmem = pl.BlockSpec(memory_space=pltpu.VMEM)
    shape = (n_aux // PLANE // 2, blk + TAIL, nocc)
    return pl.pallas_call(
        kernel,
        out_shape=[jax.ShapeDtypeStruct(shape, jnp.bfloat16)] * PLANE,
        in_specs=[smem] * 4 + [vmem, vmem],
        out_specs=[vmem] * PLANE,
        scratch_shapes=[pltpu.VMEM((n_aux + 1, blk, nocc), jnp.float32)],
        compiler_params=pltpu.CompilerParams(vmem_limit_bytes=20 * 1024 * 1024),
        cost_estimate=pl.CostEstimate(
            flops=10**10, bytes_accessed=tiles_array.size, transcendentals=0
        ),
        name="second_part",
    )(*lists, bit, tiles_array, fitted)


def all_in_one(n_aux, lists, bit, tiles_array, whole):
    slots, auxb, blk, nocc = tiles_array.shape

    def kernel(slot_ref, block_ref, gid_ref, bit_ref, tiles, c_ref, out_ref, ct, zacc, zb, acc):
        lists = (slot_ref, block_ref, gid_ref)
        clear_and_fit(n_aux, ct, acc)
        zacc[...] = jnp.zeros(zacc.shape, zacc.dtype)

        @pl.loop(0, n_aux)
        def _(m):
            turn(ct, bit_ref, m, c_ref.at[m])

        _, total = chunk_ends(gid_ref, slots)
        fit(lists, tiles, ct, zacc, 0, total)
        round_fitted(zacc, zb)
        apply_fitted(lists, tiles, zb, acc, 0, total)

        @pl.loop(0, n_aux)
        def _(m):
            put(bit_ref, acc, m, out_ref, m)

    smem = pl.BlockSpec(memory_space=pltpu.SMEM)
    vmem = pl.BlockSpec(memory_space=pltpu.VMEM)
    return pl.pallas_call(
        kernel,
        out_shape=jax.ShapeDtypeStruct((n_aux, blk + TAIL, nocc), jnp.bfloat16),
        in_specs=[smem] * 4 + [vmem] * 2,
        out_specs=vmem,
        scratch_shapes=[
            pltpu.VMEM((n_aux + 1, nocc, blk), jnp.bfloat16),
            pltpu.VMEM((AB_DEV, nocc, auxb * nocc), jnp.float32),
            pltpu.VMEM((AB_DEV, auxb * nocc, nocc), jnp.bfloat16),
            pltpu.VMEM((n_aux + 1, blk, nocc), jnp.float32),
        ],
        compiler_params=pltpu.CompilerParams(vmem_limit_bytes=46 * 1024 * 1024),
        name="all_in_one",
    )(*lists, bit, tiles_array, whole)


def merge(arrays, after):
    def kernel(*refs):
        for i, ref in enumerate(refs[: len(arrays)]):
            refs[-1][i] = ref[...]

    vmem = pl.BlockSpec(memory_space=pltpu.VMEM)
    return pl.pallas_call(
        kernel,
        out_shape=jax.ShapeDtypeStruct((len(arrays),) + arrays[0].shape, arrays[0].dtype),
        in_specs=[vmem] * len(arrays) + [pl.BlockSpec(memory_space=pl.ANY)] * len(after),
        out_specs=vmem,
        compiler_params=pltpu.CompilerParams(vmem_limit_bytes=4 * 1024 * 1024),
        name="merge",
    )(*arrays, *after)


def spread(parts, after, dtypes, blk, bb_dev):
    count, rows, nocc = parts[0].shape

    def kernel(*refs):
        sources, targets = refs[: len(parts)], refs[len(parts) + len(after) :]
        for i in range(count):
            sums = [jnp.zeros((blk, nocc), jnp.float32) for _ in range(bb_dev)]
            for source in sources:
                value = source[i, :blk, :].astype(jnp.float32)
                which = source[i, blk:, :][:1].astype(jnp.float32)
                for b in range(bb_dev):
                    sums[b] = sums[b] + jnp.where(which == b, value, 0.0)
            for b in range(bb_dev):
                targets[i][b * blk : (b + 1) * blk, :] = sums[b].astype(targets[i].dtype)

    vmem = pl.BlockSpec(memory_space=pltpu.VMEM)
    return pl.pallas_call(
        kernel,
        out_shape=[jax.ShapeDtypeStruct((bb_dev * blk, nocc), dtype) for dtype in dtypes],
        in_specs=[vmem] * len(parts) + [pl.BlockSpec(memory_space=pl.ANY)] * len(after),
        out_specs=[vmem] * count,
        compiler_params=pltpu.CompilerParams(vmem_limit_bytes=4 * 1024 * 1024),
        cost_estimate=pl.CostEstimate(
            flops=SPREAD_COST, bytes_accessed=SPREAD_COST // 1000, transcendentals=0
        ),
        name="spread",
    )(*parts, *after)


def total_of(arrays, dtype, cost):
    def kernel(*refs):
        value = refs[0][...].astype(jnp.float32)
        for ref in refs[1:-1]:
            value = value + ref[...].astype(jnp.float32)
        refs[-1][...] = value.astype(refs[-1].dtype)

    vmem = pl.BlockSpec(memory_space=pltpu.VMEM)
    return pl.pallas_call(
        kernel,
        out_shape=jax.ShapeDtypeStruct(arrays[0].shape, dtype),
        in_specs=[vmem] * len(arrays),
        out_specs=vmem,
        compiler_params=pltpu.CompilerParams(vmem_limit_bytes=4 * 1024 * 1024),
        cost_estimate=pl.CostEstimate(flops=cost, bytes_accessed=cost // 1000, transcendentals=0),
        name="total_of",
    )(*arrays)


def owner_sum(parts, blk, bb_dev):
    n_aux, rows, nocc = parts.shape

    def kernel(parts_ref, out_ref):
        sums = [jnp.zeros((blk, nocc), jnp.float32) for _ in range(bb_dev)]
        for s in range(n_aux):
            value = parts_ref[s, :blk, :].astype(jnp.float32)
            which = parts_ref[s, blk:, :][:1].astype(jnp.float32)
            for b in range(bb_dev):
                sums[b] = sums[b] + jnp.where(which == b, value, 0.0)
        for b in range(bb_dev):
            out_ref[b * blk : (b + 1) * blk, :] = sums[b].astype(out_ref.dtype)

    vmem = pl.BlockSpec(memory_space=pltpu.VMEM)
    return pl.pallas_call(
        kernel,
        out_shape=jax.ShapeDtypeStruct((bb_dev * blk, nocc), jnp.bfloat16),
        in_specs=[vmem],
        out_specs=vmem,
        name="owner_sum",
    )(parts)


def on_device(tiles, c_orbitals, basis_order, tile_block, tile_aux, live):
    blk, nocc = tiles.shape[2:]
    n_aux = lax.axis_size("aux")
    bb_dev = basis_order.shape[0] // n_aux
    direct = n_aux == DIRECT

    def swap(array, m):
        return lax.ppermute(array, "aux", [(i, i ^ m) for i in range(n_aux)])

    base = lax.axis_index("aux").astype(jnp.int32) if direct else jnp.int32(0)
    alive = lax.iota(jnp.int32, tile_block.shape[0]) < live[0]
    where_to, which = owners_of(tile_block, basis_order, base, bb_dev)
    bit = bits_of(where_to, which, alive, n_aux)
    if not direct:
        lists = chunk_lists(where_to, where_to < 0, alive, tile_aux, n_aux)
        whole = lax.all_gather(c_orbitals, "aux", axis=0, tiled=True)
        whole = whole.reshape(n_aux, bb_dev * blk, nocc)
        parts = all_in_one(n_aux, lists, bit, tiles, whole)
        moved = lax.all_to_all(parts, "aux", 0, 0, tiled=True)
        return owner_sum(moved, blk, bb_dev)

    depth = n_aux // PLANE
    half = depth // 2
    last = (where_to >= PLANE) & (where_to % PLANE >= 2)
    fit_lists = chunk_lists(where_to, last, alive, tile_aux, n_aux)
    lists = chunk_lists(where_to, where_to < n_aux // 2, alive, tile_aux, n_aux)
    column = [c_orbitals] + [None] * (depth - 1)
    for dz in range(depth - 1, 0, -1):
        column[dz] = swap(c_orbitals, dz * PLANE)
    beside = swap(c_orbitals, 2)
    across = swap(c_orbitals, 1)
    early = merge(column[1:] + [beside], [])
    late = [swap(array, 2) for array in column[1:]]
    early_from = [(1, (2, None)), (2, (0, depth - 1)), (3, (1, depth - 1))]
    late_from = []
    for dz in range(1, depth):
        for core in range(2):
            early_from.append((dz * PLANE + core, (core, dz - 1)))
            late_from.append((dz * PLANE + 2 + core, (core, dz - 1)))
    held, partial_fit = begin(
        n_aux,
        fit_lists,
        bit,
        tiles,
        c_orbitals,
        [early, swap(early, 1), across],
        early_from,
    )
    late = merge(late, [partial_fit])
    *far, fitted = first_part(
        n_aux, fit_lists, lists, bit, held, partial_fit, [late, swap(late, 1)], late_from
    )
    far = [far[0]] + [swap(far[r], r) for r in range(1, PLANE)]
    near = second_part(n_aux, lists, bit, held, fitted)
    near = [near[0]] + [swap(near[r], r) for r in range(1, PLANE)]
    far = spread(far, [], [jnp.bfloat16] * half, blk, bb_dev)
    near = spread(
        near, [far[0]], [jnp.float32] + [jnp.bfloat16] * (half - 1), blk, bb_dev
    )
    far = [swap(far[i], (half + i) * PLANE) for i in range(half)]
    far = total_of(far, jnp.float32, SPREAD_COST)
    near = [near[0]] + [swap(near[dz], dz * PLANE) for dz in range(1, half)]
    return total_of(near + [far], jnp.bfloat16, 0)


def solution(mesh):
    return jax.shard_map(
        on_device,
        mesh=mesh,
        in_specs=(
            P(("grp", "aux"), None, None, None),
            P(("grp", "aux"), None),
            P("grp"),
            P(("grp", "aux")),
            P(("grp", "aux")),
            P(("grp", "aux")),
        ),
        out_specs=P(("grp", "aux"), None),
        check_vma=False,
    )
```

```python
import functools

import jax
import jax.numpy as jnp
from jax import lax
from jax.experimental import pallas as pl
from jax.experimental.pallas import tpu as pltpu
from jax.sharding import PartitionSpec as P

AB_DEV = 8
CHUNK = 4
UNROLL = 2
TAIL = 16
PLANE = 4
SPREAD_COST = 10**10
DIRECT = 16


def owners_of(tile_block, basis_order, base, bb_dev):
    nbb = basis_order.shape[0]
    position = jnp.sum(
        jnp.where(
            basis_order[None, :] == tile_block[:, None], lax.iota(jnp.int32, nbb)[None, :], 0
        ),
        axis=1,
    )
    return jnp.bitwise_xor(position // bb_dev, base), position % bb_dev


def chunk_lists(where_to, later, alive, tile_aux, n_aux):
    slots = where_to.shape[0]
    keys = 2 * AB_DEV
    chunks = slots // CHUNK + keys
    t = lax.iota(jnp.int32, slots)
    group = jnp.where(alive, tile_aux + jnp.where(later, AB_DEV, 0), keys)
    ids = lax.iota(jnp.int32, keys)
    counts = jnp.sum((group[None, :] == ids[:, None]).astype(jnp.int32), axis=1)
    need = (counts + CHUNK - 1) // CHUNK
    ends = jnp.sum(jnp.where(ids[None, :] <= ids[:, None], need[None, :], 0), axis=1)
    rank = jnp.sum(
        ((group[None, :] == group[:, None]) & (t[None, :] < t[:, None])).astype(jnp.int32), axis=1
    )
    start = jnp.sum(jnp.where(group[:, None] > ids[None, :], need[None, :], 0), axis=1)
    place = jnp.where(alive, start * CHUNK + rank, -1)
    q = lax.iota(jnp.int32, chunks * CHUNK)
    hit = place[None, :] == q[:, None]
    lead = place[None, :] == (q // CHUNK * CHUNK)[:, None]
    valid = jnp.any(hit, axis=1)
    slot = jnp.sum(jnp.where(hit, t[None, :], 0), axis=1)
    slot = jnp.where(valid, slot, jnp.sum(jnp.where(lead, t[None, :], 0), axis=1))
    block = jnp.where(valid, jnp.sum(jnp.where(hit, where_to[None, :], 0), axis=1), n_aux)
    gid = jnp.sum(
        (lax.iota(jnp.int32, chunks)[:, None] >= ends[None, :]).astype(jnp.int32), axis=1
    )
    return slot, block, jnp.concatenate([gid % AB_DEV, ends])


def bits_of(where_to, which, alive, n_aux):
    return jnp.max(
        jnp.where(
            (where_to[None, :] == lax.iota(jnp.int32, n_aux)[:, None]) & alive[None, :],
            which[None, :],
            0,
        ),
        axis=1,
    )


def slab(tiles, slot):
    return jnp.concatenate([tiles[slot, p] for p in range(tiles.shape[1])], axis=1)


def chunk_ends(gid_ref, slots):
    chunks = slots // CHUNK + 2 * AB_DEV
    return gid_ref[chunks + AB_DEV - 1], gid_ref[chunks + 2 * AB_DEV - 1]


def turn(ct, bit_ref, m, source):
    blk = ct.shape[2]
    row = pl.multiple_of(bit_ref[m] * blk, blk)
    ct[m] = source[pl.ds(row, blk), :].T


def fit(lists, tiles, ct, zacc, low, high):
    slot_ref, block_ref, gid_ref = lists

    @pl.loop(0, (high - low + UNROLL - 1) // UNROLL)
    def _(step):
        for chunk in [low + step * UNROLL + u for u in range(UNROLL)]:
            keep = jnp.where(chunk < high, 0, ct.shape[0] - 1)
            spots = [chunk * CHUNK + i for i in range(CHUNK)]
            left = jnp.concatenate(
                [ct[jnp.maximum(block_ref[pos], keep)] for pos in spots], axis=1
            )
            right = jnp.concatenate([slab(tiles, slot_ref[pos]) for pos in spots], axis=0)
            zacc[gid_ref[chunk]] += jnp.dot(left, right, preferred_element_type=jnp.float32)


def apply_fitted(lists, tiles, zb, acc, low, high):
    slot_ref, block_ref, gid_ref = lists
    blk = acc.shape[1]

    @pl.loop(0, (high - low + UNROLL - 1) // UNROLL)
    def _(step):
        for chunk in [low + step * UNROLL + u for u in range(UNROLL)]:
            spots = [chunk * CHUNK + i for i in range(CHUNK)]
            left = jnp.concatenate([slab(tiles, slot_ref[pos]) for pos in spots], axis=0)
            value = jnp.dot(left, zb[gid_ref[chunk]], preferred_element_type=jnp.float32)
            for i, pos in enumerate(spots):
                acc[block_ref[pos]] += value[i * blk : (i + 1) * blk]


def begin(n_aux, lists, bit, tiles_array, own_array, shards, sources):
    slots, auxb, blk, nocc = tiles_array.shape
    n_in = len(shards)

    def kernel(slot_ref, block_ref, gid_ref, bit_ref, tiles, own, *refs):
        c_refs, (zacc, ct) = refs[:n_in], refs[n_in:]
        zacc[...] = jnp.zeros(zacc.shape, zacc.dtype)
        ct[n_aux] = jnp.zeros((nocc, blk), ct.dtype)
        turn(ct, bit_ref, 0, own)
        for m, (ref, i) in sources:
            turn(ct, bit_ref, m, c_refs[ref] if i is None else c_refs[ref].at[i])
        early, _ = chunk_ends(gid_ref, slots)
        fit((slot_ref, block_ref, gid_ref), tiles, ct, zacc, 0, early)

    smem = pl.BlockSpec(memory_space=pltpu.SMEM)
    vmem = pl.BlockSpec(memory_space=pltpu.VMEM)
    return pl.pallas_call(
        kernel,
        out_shape=jax.ShapeDtypeStruct((AB_DEV, nocc, auxb * nocc), jnp.float32),
        in_specs=[smem] * 4 + [vmem] * (2 + n_in),
        out_specs=vmem,
        scratch_shapes=[pltpu.VMEM((n_aux + 1, nocc, blk), jnp.bfloat16)],
        compiler_params=pltpu.CompilerParams(vmem_limit_bytes=20 * 1024 * 1024),
        cost_estimate=pl.CostEstimate(
            flops=2 * tiles_array.size * nocc, bytes_accessed=tiles_array.size, transcendentals=0
        ),
        name="begin",
    )(*lists, bit, tiles_array, own_array, *shards)


def put(bit_ref, acc, m, out_ref, place):
    blk, nocc = acc.shape[1:]
    out_ref[place, :blk, :] = acc[m].astype(out_ref.dtype)
    out_ref[place, blk:, :] = jnp.full((TAIL, nocc), bit_ref[m], jnp.int32).astype(
        jnp.float32
    ).astype(out_ref.dtype)


def clear_and_fit(n_aux, ct, acc):
    ct[n_aux] = jnp.zeros(ct.shape[1:], ct.dtype)
    acc[...] = jnp.zeros(acc.shape, acc.dtype)


def round_fitted(zacc, zb):
    groups, nocc, wide = zacc.shape
    for g in range(groups):
        for p in range(wide // nocc):
            part = zacc[g, :, p * nocc : (p + 1) * nocc].astype(zb.dtype)
            zb[g, p * nocc : (p + 1) * nocc, :] = part.T


def first_part(n_aux, fit_lists, lists, bit, tiles_array, partial_fit, shards, sources):
    slots, auxb, blk, nocc = tiles_array.shape
    n_in = len(shards)

    def kernel(*refs):
        fit_refs, refs = refs[:3], refs[3:]
        list_refs, bit_ref, tiles, partial_ref = refs[:3], refs[3], refs[4], refs[5]
        c_refs, out_refs = refs[6 : 6 + n_in], refs[6 + n_in : -4]
        zb, ct, zacc, acc = refs[-4:]
        clear_and_fit(n_aux, ct, acc)
        zacc[...] = partial_ref[...]
        for m, (ref, i) in sources:
            turn(ct, bit_ref, m, c_refs[ref] if i is None else c_refs[ref].at[i])
        fit(fit_refs, tiles, ct, zacc, *chunk_ends(fit_refs[2], slots))
        round_fitted(zacc, zb)
        far, _ = chunk_ends(list_refs[2], slots)
        apply_fitted(list_refs, tiles, zb, acc, 0, far)
        for m in range(n_aux // 2, n_aux):
            put(bit_ref, acc, m, out_refs[m % PLANE], (m - n_aux // 2) // PLANE)

    smem = pl.BlockSpec(memory_space=pltpu.SMEM)
    vmem = pl.BlockSpec(memory_space=pltpu.VMEM)
    shape = (n_aux // PLANE // 2, blk + TAIL, nocc)
    out_shape = [jax.ShapeDtypeStruct(shape, jnp.bfloat16)] * PLANE
    out_shape = out_shape + [jax.ShapeDtypeStruct((AB_DEV, auxb * nocc, nocc), jnp.bfloat16)]
    return pl.pallas_call(
        kernel,
        out_shape=out_shape,
        in_specs=[smem] * 7 + [vmem] * (2 + n_in),
        out_specs=[vmem] * len(out_shape),
        scratch_shapes=[
            pltpu.VMEM((n_aux + 1, nocc, blk), jnp.bfloat16),
            pltpu.VMEM((AB_DEV, nocc, auxb * nocc), jnp.float32),
            pltpu.VMEM((n_aux + 1, blk, nocc), jnp.float32),
        ],
        compiler_params=pltpu.CompilerParams(vmem_limit_bytes=20 * 1024 * 1024),
        cost_estimate=pl.CostEstimate(
            flops=3 * tiles_array.size * nocc, bytes_accessed=tiles_array.size, transcendentals=0
        ),
        name="first_part",
    )(*fit_lists, *lists, bit, tiles_array, partial_fit, *shards)


def second_part(n_aux, lists, bit, tiles_array, fitted):
    slots, auxb, blk, nocc = tiles_array.shape

    def kernel(slot_ref, block_ref, gid_ref, bit_ref, tiles, zb, *refs):
        out_refs, acc = refs[:-1], refs[-1]
        acc[...] = jnp.zeros(acc.shape, acc.dtype)
        apply_fitted(
            (slot_ref, block_ref, gid_ref), tiles, zb, acc, *chunk_ends(gid_ref, slots)
        )
        for m in range(n_aux // 2):
            put(bit_ref, acc, m, out_refs[m % PLANE], m // PLANE)

    smem = pl.BlockSpec(memory_space=pltpu.SMEM)
    vmem = pl.BlockSpec(memory_space=pltpu.VMEM)
    shape = (n_aux // PLANE // 2, blk + TAIL, nocc)
    return pl.pallas_call(
        kernel,
        out_shape=[jax.ShapeDtypeStruct(shape, jnp.bfloat16)] * PLANE,
        in_specs=[smem] * 4 + [vmem, vmem],
        out_specs=[vmem] * PLANE,
        scratch_shapes=[pltpu.VMEM((n_aux + 1, blk, nocc), jnp.float32)],
        compiler_params=pltpu.CompilerParams(vmem_limit_bytes=20 * 1024 * 1024),
        cost_estimate=pl.CostEstimate(
            flops=10**10, bytes_accessed=tiles_array.size, transcendentals=0
        ),
        name="second_part",
    )(*lists, bit, tiles_array, fitted)


def all_in_one(n_aux, lists, bit, tiles_array, whole):
    slots, auxb, blk, nocc = tiles_array.shape

    def kernel(slot_ref, block_ref, gid_ref, bit_ref, tiles, c_ref, out_ref, ct, zacc, zb, acc):
        lists = (slot_ref, block_ref, gid_ref)
        clear_and_fit(n_aux, ct, acc)
        zacc[...] = jnp.zeros(zacc.shape, zacc.dtype)

        @pl.loop(0, n_aux)
        def _(m):
            turn(ct, bit_ref, m, c_ref.at[m])

        _, total = chunk_ends(gid_ref, slots)
        fit(lists, tiles, ct, zacc, 0, total)
        round_fitted(zacc, zb)
        apply_fitted(lists, tiles, zb, acc, 0, total)

        @pl.loop(0, n_aux)
        def _(m):
            put(bit_ref, acc, m, out_ref, m)

    smem = pl.BlockSpec(memory_space=pltpu.SMEM)
    vmem = pl.BlockSpec(memory_space=pltpu.VMEM)
    return pl.pallas_call(
        kernel,
        out_shape=jax.ShapeDtypeStruct((n_aux, blk + TAIL, nocc), jnp.bfloat16),
        in_specs=[smem] * 4 + [vmem] * 2,
        out_specs=vmem,
        scratch_shapes=[
            pltpu.VMEM((n_aux + 1, nocc, blk), jnp.bfloat16),
            pltpu.VMEM((AB_DEV, nocc, auxb * nocc), jnp.float32),
            pltpu.VMEM((AB_DEV, auxb * nocc, nocc), jnp.bfloat16),
            pltpu.VMEM((n_aux + 1, blk, nocc), jnp.float32),
        ],
        compiler_params=pltpu.CompilerParams(vmem_limit_bytes=46 * 1024 * 1024),
        name="all_in_one",
    )(*lists, bit, tiles_array, whole)


def merge(arrays, after, cost):
    def kernel(*refs):
        for i, ref in enumerate(refs[: len(arrays)]):
            refs[-1][i] = ref[...]

    vmem = pl.BlockSpec(memory_space=pltpu.VMEM)
    return pl.pallas_call(
        kernel,
        out_shape=jax.ShapeDtypeStruct((len(arrays),) + arrays[0].shape, arrays[0].dtype),
        in_specs=[vmem] * len(arrays) + [pl.BlockSpec(memory_space=pl.ANY)] * len(after),
        out_specs=vmem,
        compiler_params=pltpu.CompilerParams(vmem_limit_bytes=4 * 1024 * 1024),
        cost_estimate=pl.CostEstimate(flops=cost, bytes_accessed=cost // 1000, transcendentals=0),
        name="merge",
    )(*arrays, *after)


def spread(parts, after, dtypes, blk, bb_dev):
    count, rows, nocc = parts[0].shape

    def kernel(*refs):
        sources, targets = refs[: len(parts)], refs[len(parts) + len(after) :]
        for i in range(count):
            sums = [jnp.zeros((blk, nocc), jnp.float32) for _ in range(bb_dev)]
            for source in sources:
                value = source[i, :blk, :].astype(jnp.float32)
                which = source[i, blk:, :][:1].astype(jnp.float32)
                for b in range(bb_dev):
                    sums[b] = sums[b] + jnp.where(which == b, value, 0.0)
            for b in range(bb_dev):
                targets[i][b * blk : (b + 1) * blk, :] = sums[b].astype(targets[i].dtype)

    vmem = pl.BlockSpec(memory_space=pltpu.VMEM)
    return pl.pallas_call(
        kernel,
        out_shape=[jax.ShapeDtypeStruct((bb_dev * blk, nocc), dtype) for dtype in dtypes],
        in_specs=[vmem] * len(parts) + [pl.BlockSpec(memory_space=pl.ANY)] * len(after),
        out_specs=[vmem] * count,
        compiler_params=pltpu.CompilerParams(vmem_limit_bytes=4 * 1024 * 1024),
        cost_estimate=pl.CostEstimate(
            flops=SPREAD_COST, bytes_accessed=SPREAD_COST // 1000, transcendentals=0
        ),
        name="spread",
    )(*parts, *after)


def total_of(arrays, dtype, cost):
    def kernel(*refs):
        value = refs[0][...].astype(jnp.float32)
        for ref in refs[1:-1]:
            value = value + ref[...].astype(jnp.float32)
        refs[-1][...] = value.astype(refs[-1].dtype)

    vmem = pl.BlockSpec(memory_space=pltpu.VMEM)
    return pl.pallas_call(
        kernel,
        out_shape=jax.ShapeDtypeStruct(arrays[0].shape, dtype),
        in_specs=[vmem] * len(arrays),
        out_specs=vmem,
        compiler_params=pltpu.CompilerParams(vmem_limit_bytes=4 * 1024 * 1024),
        cost_estimate=pl.CostEstimate(flops=cost, bytes_accessed=cost // 1000, transcendentals=0),
        name="total_of",
    )(*arrays)


def owner_sum(parts, blk, bb_dev):
    n_aux, rows, nocc = parts.shape

    def kernel(parts_ref, out_ref):
        sums = [jnp.zeros((blk, nocc), jnp.float32) for _ in range(bb_dev)]
        for s in range(n_aux):
            value = parts_ref[s, :blk, :].astype(jnp.float32)
            which = parts_ref[s, blk:, :][:1].astype(jnp.float32)
            for b in range(bb_dev):
                sums[b] = sums[b] + jnp.where(which == b, value, 0.0)
        for b in range(bb_dev):
            out_ref[b * blk : (b + 1) * blk, :] = sums[b].astype(out_ref.dtype)

    vmem = pl.BlockSpec(memory_space=pltpu.VMEM)
    return pl.pallas_call(
        kernel,
        out_shape=jax.ShapeDtypeStruct((bb_dev * blk, nocc), jnp.bfloat16),
        in_specs=[vmem],
        out_specs=vmem,
        name="owner_sum",
    )(parts)


def on_device(tiles, c_orbitals, basis_order, tile_block, tile_aux, live):
    blk, nocc = tiles.shape[2:]
    n_aux = lax.axis_size("aux")
    bb_dev = basis_order.shape[0] // n_aux
    direct = n_aux == DIRECT

    def swap(array, m):
        return lax.ppermute(array, "aux", [(i, i ^ m) for i in range(n_aux)])

    base = lax.axis_index("aux").astype(jnp.int32) if direct else jnp.int32(0)
    alive = lax.iota(jnp.int32, tile_block.shape[0]) < live[0]
    where_to, which = owners_of(tile_block, basis_order, base, bb_dev)
    bit = bits_of(where_to, which, alive, n_aux)
    if not direct:
        lists = chunk_lists(where_to, where_to < 0, alive, tile_aux, n_aux)
        whole = lax.all_gather(c_orbitals, "aux", axis=0, tiled=True)
        whole = whole.reshape(n_aux, bb_dev * blk, nocc)
        parts = all_in_one(n_aux, lists, bit, tiles, whole)
        moved = lax.all_to_all(parts, "aux", 0, 0, tiled=True)
        return owner_sum(moved, blk, bb_dev)

    depth = n_aux // PLANE
    half = depth // 2
    last = (where_to >= PLANE) & (where_to % PLANE >= 2)
    fit_lists = chunk_lists(where_to, last, alive, tile_aux, n_aux)
    lists = chunk_lists(where_to, where_to < n_aux // 2, alive, tile_aux, n_aux)
    column = [c_orbitals] + [None] * (depth - 1)
    for dz in range(depth - 1, 0, -1):
        column[dz] = swap(c_orbitals, dz * PLANE)
    beside = swap(c_orbitals, 2)
    across = swap(c_orbitals, 1)
    early = merge(column[1:] + [beside], [], SPREAD_COST)
    late = [swap(array, 2) for array in column[1:]]
    early_from = [(1, (2, None)), (2, (0, depth - 1)), (3, (1, depth - 1))]
    late_from = []
    for dz in range(1, depth):
        for core in range(2):
            early_from.append((dz * PLANE + core, (core, dz - 1)))
            late_from.append((dz * PLANE + 2 + core, (core, dz - 1)))
    partial_fit = begin(
        n_aux,
        fit_lists,
        bit,
        tiles,
        c_orbitals,
        [early, swap(early, 1), across],
        early_from,
    )
    late = merge(late, [partial_fit], 0)
    *far, fitted = first_part(
        n_aux, fit_lists, lists, bit, tiles, partial_fit, [late, swap(late, 1)], late_from
    )
    far = [far[0]] + [swap(far[r], r) for r in range(1, PLANE)]
    near = second_part(n_aux, lists, bit, tiles, fitted)
    near = [near[0]] + [swap(near[r], r) for r in range(1, PLANE)]
    far = spread(far, [], [jnp.bfloat16] * half, blk, bb_dev)
    near = spread(
        near, [far[0]], [jnp.float32] + [jnp.bfloat16] * (half - 1), blk, bb_dev
    )
    far = [swap(far[i], (half + i) * PLANE) for i in range(half)]
    far = total_of(far, jnp.float32, SPREAD_COST)
    near = [near[0]] + [swap(near[dz], dz * PLANE) for dz in range(1, half)]
    return total_of(near + [far], jnp.bfloat16, 0)


def solution(mesh):
    return jax.shard_map(
        on_device,
        mesh=mesh,
        in_specs=(
            P(("grp", "aux"), None, None, None),
            P(("grp", "aux"), None),
            P("grp"),
            P(("grp", "aux")),
            P(("grp", "aux")),
            P(("grp", "aux")),
        ),
        out_specs=P(("grp", "aux"), None),
        check_vma=False,
    )
```

```python
import functools

import jax
import jax.numpy as jnp
from jax import lax
from jax.experimental import pallas as pl
from jax.experimental.pallas import tpu as pltpu
from jax.sharding import PartitionSpec as P

AB_DEV = 8
CHUNK = 4
UNROLL = 2
TAIL = 16
PLANE = 4
SPREAD_COST = 10**10
DIRECT = 16


def pack_slots(tile_block, tile_aux, live, basis_order, base, bb_dev):
    nbb = basis_order.shape[0]
    position = jnp.sum(
        jnp.where(
            basis_order[None, :] == tile_block[:, None], lax.iota(jnp.int32, nbb)[None, :], 0
        ),
        axis=1,
    )
    owner = jnp.bitwise_xor(position // bb_dev, base)
    alive = (lax.iota(jnp.int32, tile_block.shape[0]) < live[0]).astype(jnp.int32)
    return ((owner * bb_dev + position % bb_dev) * AB_DEV + tile_aux) * 2 + alive


def unpack_slots(packed, bb_dev):
    rest = packed // 2
    tile_aux = rest % AB_DEV
    rest = rest // AB_DEV
    return rest // bb_dev, rest % bb_dev, tile_aux, packed % 2 == 1


def chunk_lists(where_to, later, alive, tile_aux, n_aux):
    slots = where_to.shape[0]
    keys = 2 * AB_DEV
    chunks = slots // CHUNK + keys
    t = lax.iota(jnp.int32, slots)
    group = jnp.where(alive, tile_aux + jnp.where(later, AB_DEV, 0), keys)
    ids = lax.iota(jnp.int32, keys)
    counts = jnp.sum((group[None, :] == ids[:, None]).astype(jnp.int32), axis=1)
    need = (counts + CHUNK - 1) // CHUNK
    ends = jnp.sum(jnp.where(ids[None, :] <= ids[:, None], need[None, :], 0), axis=1)
    rank = jnp.sum(
        ((group[None, :] == group[:, None]) & (t[None, :] < t[:, None])).astype(jnp.int32), axis=1
    )
    start = jnp.sum(jnp.where(group[:, None] > ids[None, :], need[None, :], 0), axis=1)
    place = jnp.where(alive, start * CHUNK + rank, -1)
    q = lax.iota(jnp.int32, chunks * CHUNK)
    hit = place[None, :] == q[:, None]
    lead = place[None, :] == (q // CHUNK * CHUNK)[:, None]
    valid = jnp.any(hit, axis=1)
    slot = jnp.sum(jnp.where(hit, t[None, :], 0), axis=1)
    slot = jnp.where(valid, slot, jnp.sum(jnp.where(lead, t[None, :], 0), axis=1))
    block = jnp.where(valid, jnp.sum(jnp.where(hit, where_to[None, :], 0), axis=1), n_aux)
    gid = jnp.sum(
        (lax.iota(jnp.int32, chunks)[:, None] >= ends[None, :]).astype(jnp.int32), axis=1
    )
    return slot, block, jnp.concatenate([gid % AB_DEV, ends])


def bits_of(where_to, which, alive, n_aux):
    return jnp.max(
        jnp.where(
            (where_to[None, :] == lax.iota(jnp.int32, n_aux)[:, None]) & alive[None, :],
            which[None, :],
            0,
        ),
        axis=1,
    )


def slab(tiles, slot):
    return jnp.concatenate([tiles[slot, p] for p in range(tiles.shape[1])], axis=1)


def chunk_ends(gid_ref, slots):
    chunks = slots // CHUNK + 2 * AB_DEV
    return gid_ref[chunks + AB_DEV - 1], gid_ref[chunks + 2 * AB_DEV - 1]


def turn(ct, bit_ref, m, source):
    blk = ct.shape[2]
    row = pl.multiple_of(bit_ref[m] * blk, blk)
    ct[m] = source[pl.ds(row, blk), :].T


def fit(lists, tiles, ct, zacc, low, high):
    slot_ref, block_ref, gid_ref = lists

    @pl.loop(0, (high - low + UNROLL - 1) // UNROLL)
    def _(step):
        for chunk in [low + step * UNROLL + u for u in range(UNROLL)]:
            keep = jnp.where(chunk < high, 0, ct.shape[0] - 1)
            spots = [chunk * CHUNK + i for i in range(CHUNK)]
            left = jnp.concatenate(
                [ct[jnp.maximum(block_ref[pos], keep)] for pos in spots], axis=1
            )
            right = jnp.concatenate([slab(tiles, slot_ref[pos]) for pos in spots], axis=0)
            zacc[gid_ref[chunk]] += jnp.dot(left, right, preferred_element_type=jnp.float32)


def apply_fitted(lists, tiles, zb, acc, low, high):
    slot_ref, block_ref, gid_ref = lists
    blk = acc.shape[1]

    @pl.loop(0, (high - low + UNROLL - 1) // UNROLL)
    def _(step):
        for chunk in [low + step * UNROLL + u for u in range(UNROLL)]:
            spots = [chunk * CHUNK + i for i in range(CHUNK)]
            left = jnp.concatenate([slab(tiles, slot_ref[pos]) for pos in spots], axis=0)
            value = jnp.dot(left, zb[gid_ref[chunk]], preferred_element_type=jnp.float32)
            for i, pos in enumerate(spots):
                acc[block_ref[pos]] += value[i * blk : (i + 1) * blk]


def begin(n_aux, lists, bit, packed, tiles_array, own_array, shards, sources):
    slots, auxb, blk, nocc = tiles_array.shape
    n_in = len(shards)

    def kernel(slot_ref, block_ref, gid_ref, bit_ref, packed_ref, tiles, own, *refs):
        c_refs, (zacc, passed, ct) = refs[:n_in], refs[n_in:]
        passed[...] = packed_ref[...]
        zacc[...] = jnp.zeros(zacc.shape, zacc.dtype)
        ct[n_aux] = jnp.zeros((nocc, blk), ct.dtype)
        turn(ct, bit_ref, 0, own)
        for m, (ref, i) in sources:
            turn(ct, bit_ref, m, c_refs[ref] if i is None else c_refs[ref].at[i])
        early, _ = chunk_ends(gid_ref, slots)
        fit((slot_ref, block_ref, gid_ref), tiles, ct, zacc, 0, early)

    smem = pl.BlockSpec(memory_space=pltpu.SMEM)
    vmem = pl.BlockSpec(memory_space=pltpu.VMEM)
    return pl.pallas_call(
        kernel,
        out_shape=[
            jax.ShapeDtypeStruct((AB_DEV, nocc, auxb * nocc), jnp.float32),
            jax.ShapeDtypeStruct(packed.shape, packed.dtype),
        ],
        in_specs=[smem] * 4 + [vmem] * (3 + n_in),
        out_specs=[vmem] * 2,
        scratch_shapes=[pltpu.VMEM((n_aux + 1, nocc, blk), jnp.bfloat16)],
        compiler_params=pltpu.CompilerParams(vmem_limit_bytes=20 * 1024 * 1024),
        cost_estimate=pl.CostEstimate(
            flops=2 * tiles_array.size * nocc, bytes_accessed=tiles_array.size, transcendentals=0
        ),
        name="begin",
    )(*lists, bit, packed, tiles_array, own_array, *shards)


def put(bit_ref, acc, m, out_ref, place):
    blk, nocc = acc.shape[1:]
    out_ref[place, :blk, :] = acc[m].astype(out_ref.dtype)
    out_ref[place, blk:, :] = jnp.full((TAIL, nocc), bit_ref[m], jnp.int32).astype(
        jnp.float32
    ).astype(out_ref.dtype)


def clear(n_aux, ct, acc):
    ct[n_aux] = jnp.zeros(ct.shape[1:], ct.dtype)
    acc[...] = jnp.zeros(acc.shape, acc.dtype)


def round_fitted(zacc, zb):
    groups, nocc, wide = zacc.shape
    for g in range(groups):
        for p in range(wide // nocc):
            part = zacc[g, :, p * nocc : (p + 1) * nocc].astype(zb.dtype)
            zb[g, p * nocc : (p + 1) * nocc, :] = part.T


def first_part(n_aux, fit_lists, lists, bit, tiles_array, partial_fit, shards, sources):
    slots, auxb, blk, nocc = tiles_array.shape
    n_in = len(shards)

    def kernel(*refs):
        fit_refs, refs = refs[:3], refs[3:]
        list_refs, bit_ref, tiles = refs[:3], refs[3], refs[4]
        c_refs, out_refs = refs[6 : 6 + n_in], refs[6 + n_in : -4]
        zb, zacc, ct, acc = refs[-4:]
        clear(n_aux, ct, acc)
        for m, (ref, i) in sources:
            turn(ct, bit_ref, m, c_refs[ref] if i is None else c_refs[ref].at[i])
        fit(fit_refs, tiles, ct, zacc, *chunk_ends(fit_refs[2], slots))
        round_fitted(zacc, zb)
        far, _ = chunk_ends(list_refs[2], slots)
        apply_fitted(list_refs, tiles, zb, acc, 0, far)
        for m in range(n_aux // 2, n_aux):
            put(bit_ref, acc, m, out_refs[m % PLANE], (m - n_aux // 2) // PLANE)

    smem = pl.BlockSpec(memory_space=pltpu.SMEM)
    vmem = pl.BlockSpec(memory_space=pltpu.VMEM)
    shape = (n_aux // PLANE // 2, blk + TAIL, nocc)
    out_shape = [jax.ShapeDtypeStruct(shape, jnp.bfloat16)] * PLANE
    out_shape = out_shape + [
        jax.ShapeDtypeStruct((AB_DEV, auxb * nocc, nocc), jnp.bfloat16),
        jax.ShapeDtypeStruct(partial_fit.shape, partial_fit.dtype),
    ]
    return pl.pallas_call(
        kernel,
        out_shape=out_shape,
        in_specs=[smem] * 7 + [vmem] * (2 + n_in),
        out_specs=[vmem] * len(out_shape),
        scratch_shapes=[
            pltpu.VMEM((n_aux + 1, nocc, blk), jnp.bfloat16),
            pltpu.VMEM((n_aux + 1, blk, nocc), jnp.float32),
        ],
        input_output_aliases={8: PLANE + 1},
        compiler_params=pltpu.CompilerParams(vmem_limit_bytes=20 * 1024 * 1024),
        cost_estimate=pl.CostEstimate(
            flops=3 * tiles_array.size * nocc, bytes_accessed=tiles_array.size, transcendentals=0
        ),
        name="first_part",
    )(*fit_lists, *lists, bit, tiles_array, partial_fit, *shards)


def second_part(n_aux, lists, bit, tiles_array, fitted):
    slots, auxb, blk, nocc = tiles_array.shape

    def kernel(slot_ref, block_ref, gid_ref, bit_ref, tiles, zb, *refs):
        out_refs, acc = refs[:-1], refs[-1]
        acc[...] = jnp.zeros(acc.shape, acc.dtype)
        apply_fitted(
            (slot_ref, block_ref, gid_ref), tiles, zb, acc, *chunk_ends(gid_ref, slots)
        )
        for m in range(n_aux // 2):
            put(bit_ref, acc, m, out_refs[m % PLANE], m // PLANE)

    smem = pl.BlockSpec(memory_space=pltpu.SMEM)
    vmem = pl.BlockSpec(memory_space=pltpu.VMEM)
    shape = (n_aux // PLANE // 2, blk + TAIL, nocc)
    return pl.pallas_call(
        kernel,
        out_shape=[jax.ShapeDtypeStruct(shape, jnp.bfloat16)] * PLANE,
        in_specs=[smem] * 4 + [vmem, vmem],
        out_specs=[vmem] * PLANE,
        scratch_shapes=[pltpu.VMEM((n_aux + 1, blk, nocc), jnp.float32)],
        compiler_params=pltpu.CompilerParams(vmem_limit_bytes=20 * 1024 * 1024),
        cost_estimate=pl.CostEstimate(
            flops=10**10, bytes_accessed=tiles_array.size, transcendentals=0
        ),
        name="second_part",
    )(*lists, bit, tiles_array, fitted)


def all_in_one(n_aux, lists, bit, tiles_array, whole):
    slots, auxb, blk, nocc = tiles_array.shape

    def kernel(slot_ref, block_ref, gid_ref, bit_ref, tiles, c_ref, out_ref, ct, zacc, zb, acc):
        lists = (slot_ref, block_ref, gid_ref)
        clear(n_aux, ct, acc)
        zacc[...] = jnp.zeros(zacc.shape, zacc.dtype)

        @pl.loop(0, n_aux)
        def _(m):
            turn(ct, bit_ref, m, c_ref.at[m])

        _, total = chunk_ends(gid_ref, slots)
        fit(lists, tiles, ct, zacc, 0, total)
        round_fitted(zacc, zb)
        apply_fitted(lists, tiles, zb, acc, 0, total)

        @pl.loop(0, n_aux)
        def _(m):
            put(bit_ref, acc, m, out_ref, m)

    smem = pl.BlockSpec(memory_space=pltpu.SMEM)
    vmem = pl.BlockSpec(memory_space=pltpu.VMEM)
    return pl.pallas_call(
        kernel,
        out_shape=jax.ShapeDtypeStruct((n_aux, blk + TAIL, nocc), jnp.bfloat16),
        in_specs=[smem] * 4 + [vmem] * 2,
        out_specs=vmem,
        scratch_shapes=[
            pltpu.VMEM((n_aux + 1, nocc, blk), jnp.bfloat16),
            pltpu.VMEM((AB_DEV, nocc, auxb * nocc), jnp.float32),
            pltpu.VMEM((AB_DEV, auxb * nocc, nocc), jnp.bfloat16),
            pltpu.VMEM((n_aux + 1, blk, nocc), jnp.float32),
        ],
        compiler_params=pltpu.CompilerParams(vmem_limit_bytes=46 * 1024 * 1024),
        name="all_in_one",
    )(*lists, bit, tiles_array, whole)


def gate(array, after):
    def kernel(source, _, target):
        target[...] = source[...]

    vmem = pl.BlockSpec(memory_space=pltpu.VMEM)
    return pl.pallas_call(
        kernel,
        out_shape=jax.ShapeDtypeStruct(array.shape, array.dtype),
        in_specs=[vmem, pl.BlockSpec(memory_space=pl.ANY)],
        out_specs=vmem,
        compiler_params=pltpu.CompilerParams(vmem_limit_bytes=4 * 1024 * 1024),
        name="gate",
    )(array, after)


def merge(arrays, after, cost):
    def kernel(*refs):
        for i, ref in enumerate(refs[: len(arrays)]):
            refs[-1][i] = ref[...]

    vmem = pl.BlockSpec(memory_space=pltpu.VMEM)
    return pl.pallas_call(
        kernel,
        out_shape=jax.ShapeDtypeStruct((len(arrays),) + arrays[0].shape, arrays[0].dtype),
        in_specs=[vmem] * len(arrays) + [pl.BlockSpec(memory_space=pl.ANY)] * len(after),
        out_specs=vmem,
        compiler_params=pltpu.CompilerParams(vmem_limit_bytes=4 * 1024 * 1024),
        cost_estimate=pl.CostEstimate(flops=cost, bytes_accessed=cost // 1000, transcendentals=0),
        name="merge",
    )(*arrays, *after)


def spread(parts, after, dtypes, blk, bb_dev):
    count, rows, nocc = parts[0].shape

    def kernel(*refs):
        sources, targets = refs[: len(parts)], refs[len(parts) + len(after) :]
        for i in range(count):
            sums = [jnp.zeros((blk, nocc), jnp.float32) for _ in range(bb_dev)]
            for source in sources:
                value = source[i, :blk, :].astype(jnp.float32)
                which = source[i, blk:, :][:1].astype(jnp.float32)
                for b in range(bb_dev):
                    sums[b] = sums[b] + jnp.where(which == b, value, 0.0)
            for b in range(bb_dev):
                targets[i][b * blk : (b + 1) * blk, :] = sums[b].astype(targets[i].dtype)

    vmem = pl.BlockSpec(memory_space=pltpu.VMEM)
    return pl.pallas_call(
        kernel,
        out_shape=[jax.ShapeDtypeStruct((bb_dev * blk, nocc), dtype) for dtype in dtypes],
        in_specs=[vmem] * len(parts) + [pl.BlockSpec(memory_space=pl.ANY)] * len(after),
        out_specs=[vmem] * count,
        compiler_params=pltpu.CompilerParams(vmem_limit_bytes=4 * 1024 * 1024),
        cost_estimate=pl.CostEstimate(
            flops=SPREAD_COST, bytes_accessed=SPREAD_COST // 1000, transcendentals=0
        ),
        name="spread",
    )(*parts, *after)


def total_of(arrays, dtype, cost):
    def kernel(*refs):
        value = refs[0][...].astype(jnp.float32)
        for ref in refs[1:-1]:
            value = value + ref[...].astype(jnp.float32)
        refs[-1][...] = value.astype(refs[-1].dtype)

    vmem = pl.BlockSpec(memory_space=pltpu.VMEM)
    return pl.pallas_call(
        kernel,
        out_shape=jax.ShapeDtypeStruct(arrays[0].shape, dtype),
        in_specs=[vmem] * len(arrays),
        out_specs=vmem,
        compiler_params=pltpu.CompilerParams(vmem_limit_bytes=4 * 1024 * 1024),
        cost_estimate=pl.CostEstimate(flops=cost, bytes_accessed=cost // 1000, transcendentals=0),
        name="total_of",
    )(*arrays)


def owner_sum(parts, blk, bb_dev):
    n_aux, rows, nocc = parts.shape

    def kernel(parts_ref, out_ref):
        sums = [jnp.zeros((blk, nocc), jnp.float32) for _ in range(bb_dev)]
        for s in range(n_aux):
            value = parts_ref[s, :blk, :].astype(jnp.float32)
            which = parts_ref[s, blk:, :][:1].astype(jnp.float32)
            for b in range(bb_dev):
                sums[b] = sums[b] + jnp.where(which == b, value, 0.0)
        for b in range(bb_dev):
            out_ref[b * blk : (b + 1) * blk, :] = sums[b].astype(out_ref.dtype)

    vmem = pl.BlockSpec(memory_space=pltpu.VMEM)
    return pl.pallas_call(
        kernel,
        out_shape=jax.ShapeDtypeStruct((bb_dev * blk, nocc), jnp.bfloat16),
        in_specs=[vmem],
        out_specs=vmem,
        name="owner_sum",
    )(parts)


def on_device(tiles, c_orbitals, basis_order, tile_block, tile_aux, live):
    blk, nocc = tiles.shape[2:]
    n_aux = lax.axis_size("aux")
    bb_dev = basis_order.shape[0] // n_aux
    direct = n_aux == DIRECT

    def swap(array, m):
        return lax.ppermute(array, "aux", [(i, i ^ m) for i in range(n_aux)])

    base = lax.axis_index("aux").astype(jnp.int32) if direct else jnp.int32(0)
    packed = pack_slots(tile_block, tile_aux, live, basis_order, base, bb_dev)
    where_to, which, group, alive = unpack_slots(packed, bb_dev)
    bit = bits_of(where_to, which, alive, n_aux)
    if not direct:
        lists = chunk_lists(where_to, where_to < 0, alive, group, n_aux)
        whole = lax.all_gather(c_orbitals, "aux", axis=0, tiled=True)
        whole = whole.reshape(n_aux, bb_dev * blk, nocc)
        parts = all_in_one(n_aux, lists, bit, tiles, whole)
        moved = lax.all_to_all(parts, "aux", 0, 0, tiled=True)
        return owner_sum(moved, blk, bb_dev)

    depth = n_aux // PLANE
    half = depth // 2
    last = (where_to >= PLANE) & (where_to % PLANE >= 2)
    fit_lists = chunk_lists(where_to, last, alive, group, n_aux)
    column = [swap(c_orbitals, dz * PLANE) for dz in range(depth - 1, 0, -1)]
    beside = swap(c_orbitals, 2)
    across = swap(c_orbitals, 1)
    column = merge(column, [], SPREAD_COST)
    late = swap(column, 2)
    early = [column, swap(column, 1), across, beside, swap(beside, 1)]
    early_from = [(1, (2, None)), (2, (3, None)), (3, (4, None))]
    late_from = []
    for dz in range(1, depth):
        for core in range(2):
            early_from.append((dz * PLANE + core, (core, depth - 1 - dz)))
            late_from.append((dz * PLANE + 2 + core, (core, depth - 1 - dz)))
    partial_fit, packed = begin(
        n_aux, fit_lists, bit, packed, tiles, c_orbitals, early, early_from
    )
    late = gate(late, partial_fit)
    where_to, _, group, alive = unpack_slots(packed, bb_dev)
    lists = chunk_lists(where_to, where_to < n_aux // 2, alive, group, n_aux)
    *far, fitted, _ = first_part(
        n_aux, fit_lists, lists, bit, tiles, partial_fit, [late, swap(late, 1)], late_from
    )
    far = [far[0]] + [swap(far[r], r) for r in range(1, PLANE)]
    near = second_part(n_aux, lists, bit, tiles, fitted)
    near = [near[0]] + [swap(near[r], r) for r in range(1, PLANE)]
    far = spread(far, [], [jnp.bfloat16] * half, blk, bb_dev)
    near = spread(
        near, [far[0]], [jnp.float32] + [jnp.bfloat16] * (half - 1), blk, bb_dev
    )
    far = [swap(far[i], (half + i) * PLANE) for i in range(half)]
    far = total_of(far, jnp.float32, SPREAD_COST)
    near = [near[0]] + [swap(near[dz], dz * PLANE) for dz in range(1, half)]
    return total_of(near + [far], jnp.bfloat16, 0)


def solution(mesh):
    return jax.shard_map(
        on_device,
        mesh=mesh,
        in_specs=(
            P(("grp", "aux"), None, None, None),
            P(("grp", "aux"), None),
            P("grp"),
            P(("grp", "aux")),
            P(("grp", "aux")),
            P(("grp", "aux")),
        ),
        out_specs=P(("grp", "aux"), None),
        check_vma=False,
    )
```

```python
import functools

import jax
import jax.numpy as jnp
from jax import lax
from jax.experimental import pallas as pl
from jax.experimental.pallas import tpu as pltpu
from jax.sharding import PartitionSpec as P

AB_DEV = 8
CHUNK = 4
UNROLL = 2
TAIL = 16
PLANE = 4
SPREAD_COST = 10**10
DIRECT = 16


def pack_slots(tile_block, tile_aux, live, basis_order, base, bb_dev):
    nbb = basis_order.shape[0]
    position = jnp.sum(
        jnp.where(
            basis_order[None, :] == tile_block[:, None], lax.iota(jnp.int32, nbb)[None, :], 0
        ),
        axis=1,
    )
    owner = jnp.bitwise_xor(position // bb_dev, base)
    alive = (lax.iota(jnp.int32, tile_block.shape[0]) < live[0]).astype(jnp.int32)
    return ((owner * bb_dev + position % bb_dev) * AB_DEV + tile_aux) * 2 + alive


def unpack_slots(packed, bb_dev):
    rest = packed // 2
    tile_aux = rest % AB_DEV
    rest = rest // AB_DEV
    return rest // bb_dev, rest % bb_dev, tile_aux, packed % 2 == 1


def chunk_lists(where_to, later, alive, tile_aux, n_aux):
    slots = where_to.shape[0]
    keys = 2 * AB_DEV
    chunks = slots // CHUNK + keys
    t = lax.iota(jnp.int32, slots)
    group = jnp.where(alive, tile_aux + jnp.where(later, AB_DEV, 0), keys)
    ids = lax.iota(jnp.int32, keys)
    counts = jnp.sum((group[None, :] == ids[:, None]).astype(jnp.int32), axis=1)
    need = (counts + CHUNK - 1) // CHUNK
    ends = jnp.sum(jnp.where(ids[None, :] <= ids[:, None], need[None, :], 0), axis=1)
    rank = jnp.sum(
        ((group[None, :] == group[:, None]) & (t[None, :] < t[:, None])).astype(jnp.int32), axis=1
    )
    start = jnp.sum(jnp.where(group[:, None] > ids[None, :], need[None, :], 0), axis=1)
    place = jnp.where(alive, start * CHUNK + rank, -1)
    q = lax.iota(jnp.int32, chunks * CHUNK)
    hit = place[None, :] == q[:, None]
    lead = place[None, :] == (q // CHUNK * CHUNK)[:, None]
    valid = jnp.any(hit, axis=1)
    slot = jnp.sum(jnp.where(hit, t[None, :], 0), axis=1)
    slot = jnp.where(valid, slot, jnp.sum(jnp.where(lead, t[None, :], 0), axis=1))
    block = jnp.where(valid, jnp.sum(jnp.where(hit, where_to[None, :], 0), axis=1), n_aux)
    gid = jnp.sum(
        (lax.iota(jnp.int32, chunks)[:, None] >= ends[None, :]).astype(jnp.int32), axis=1
    )
    return slot, block, jnp.concatenate([gid % AB_DEV, ends])


def bits_of(where_to, which, alive, n_aux):
    return jnp.max(
        jnp.where(
            (where_to[None, :] == lax.iota(jnp.int32, n_aux)[:, None]) & alive[None, :],
            which[None, :],
            0,
        ),
        axis=1,
    )


def slab(tiles, slot):
    return jnp.concatenate([tiles[slot, p] for p in range(tiles.shape[1])], axis=1)


def chunk_ends(gid_ref, slots):
    chunks = slots // CHUNK + 2 * AB_DEV
    return gid_ref[chunks + AB_DEV - 1], gid_ref[chunks + 2 * AB_DEV - 1]


def turn(ct, bit_ref, m, source):
    blk = ct.shape[2]
    row = pl.multiple_of(bit_ref[m] * blk, blk)
    ct[m] = source[pl.ds(row, blk), :].T


def fit(lists, tiles, ct, zacc, low, high):
    slot_ref, block_ref, gid_ref = lists

    @pl.loop(0, (high - low + UNROLL - 1) // UNROLL)
    def _(step):
        for chunk in [low + step * UNROLL + u for u in range(UNROLL)]:
            keep = jnp.where(chunk < high, 0, ct.shape[0] - 1)
            spots = [chunk * CHUNK + i for i in range(CHUNK)]
            left = jnp.concatenate(
                [ct[jnp.maximum(block_ref[pos], keep)] for pos in spots], axis=1
            )
            right = jnp.concatenate([slab(tiles, slot_ref[pos]) for pos in spots], axis=0)
            zacc[gid_ref[chunk]] += jnp.dot(left, right, preferred_element_type=jnp.float32)


def apply_fitted(lists, tiles, zb, acc, low, high):
    slot_ref, block_ref, gid_ref = lists
    blk = acc.shape[1]

    @pl.loop(0, (high - low + UNROLL - 1) // UNROLL)
    def _(step):
        for chunk in [low + step * UNROLL + u for u in range(UNROLL)]:
            spots = [chunk * CHUNK + i for i in range(CHUNK)]
            left = jnp.concatenate([slab(tiles, slot_ref[pos]) for pos in spots], axis=0)
            value = lax.dot_general(
                left,
                zb[gid_ref[chunk]],
                (((1,), (1,)), ((), ())),
                preferred_element_type=jnp.float32,
            )
            for i, pos in enumerate(spots):
                acc[block_ref[pos]] += value[i * blk : (i + 1) * blk]


def begin(n_aux, lists, bit, packed, tiles_array, own_array, shards, sources):
    slots, auxb, blk, nocc = tiles_array.shape
    n_in = len(shards)

    def kernel(slot_ref, block_ref, gid_ref, bit_ref, packed_ref, tiles, own, *refs):
        c_refs, (zacc, passed, ct) = refs[:n_in], refs[n_in:]
        passed[...] = packed_ref[...]
        zacc[...] = jnp.zeros(zacc.shape, zacc.dtype)
        ct[n_aux] = jnp.zeros((nocc, blk), ct.dtype)
        turn(ct, bit_ref, 0, own)
        for m, (ref, i) in sources:
            turn(ct, bit_ref, m, c_refs[ref] if i is None else c_refs[ref].at[i])
        early, _ = chunk_ends(gid_ref, slots)
        fit((slot_ref, block_ref, gid_ref), tiles, ct, zacc, 0, early)

    smem = pl.BlockSpec(memory_space=pltpu.SMEM)
    vmem = pl.BlockSpec(memory_space=pltpu.VMEM)
    return pl.pallas_call(
        kernel,
        out_shape=[
            jax.ShapeDtypeStruct((AB_DEV, nocc, auxb * nocc), jnp.float32),
            jax.ShapeDtypeStruct(packed.shape, packed.dtype),
        ],
        in_specs=[smem] * 4 + [vmem] * (3 + n_in),
        out_specs=[vmem] * 2,
        scratch_shapes=[pltpu.VMEM((n_aux + 1, nocc, blk), jnp.bfloat16)],
        compiler_params=pltpu.CompilerParams(vmem_limit_bytes=20 * 1024 * 1024),
        cost_estimate=pl.CostEstimate(
            flops=2 * tiles_array.size * nocc, bytes_accessed=tiles_array.size, transcendentals=0
        ),
        name="begin",
    )(*lists, bit, packed, tiles_array, own_array, *shards)


def put(bit_ref, acc, m, out_ref, place):
    blk, nocc = acc.shape[1:]
    out_ref[place, :blk, :] = acc[m].astype(out_ref.dtype)
    out_ref[place, blk:, :] = jnp.full((TAIL, nocc), bit_ref[m], jnp.int32).astype(
        jnp.float32
    ).astype(out_ref.dtype)


def clear(n_aux, ct, acc):
    ct[n_aux] = jnp.zeros(ct.shape[1:], ct.dtype)
    acc[...] = jnp.zeros(acc.shape, acc.dtype)


def round_fitted(zacc, zb):
    for g in range(zacc.shape[0]):
        zb[g] = zacc[g].astype(zb.dtype)


def first_part(n_aux, fit_lists, lists, bit, tiles_array, partial_fit, shards, sources):
    slots, auxb, blk, nocc = tiles_array.shape
    n_in = len(shards)

    def kernel(*refs):
        fit_refs, refs = refs[:3], refs[3:]
        list_refs, bit_ref, tiles = refs[:3], refs[3], refs[4]
        c_refs, out_refs = refs[6 : 6 + n_in], refs[6 + n_in : -4]
        zb, zacc, ct, acc = refs[-4:]
        clear(n_aux, ct, acc)
        for m, (ref, i) in sources:
            turn(ct, bit_ref, m, c_refs[ref] if i is None else c_refs[ref].at[i])
        fit(fit_refs, tiles, ct, zacc, *chunk_ends(fit_refs[2], slots))
        round_fitted(zacc, zb)
        far, _ = chunk_ends(list_refs[2], slots)
        apply_fitted(list_refs, tiles, zb, acc, 0, far)
        for m in range(n_aux // 2, n_aux):
            put(bit_ref, acc, m, out_refs[m % PLANE], (m - n_aux // 2) // PLANE)

    smem = pl.BlockSpec(memory_space=pltpu.SMEM)
    vmem = pl.BlockSpec(memory_space=pltpu.VMEM)
    shape = (n_aux // PLANE // 2, blk + TAIL, nocc)
    out_shape = [jax.ShapeDtypeStruct(shape, jnp.bfloat16)] * PLANE
    out_shape = out_shape + [
        jax.ShapeDtypeStruct((AB_DEV, nocc, auxb * nocc), jnp.bfloat16),
        jax.ShapeDtypeStruct(partial_fit.shape, partial_fit.dtype),
    ]
    return pl.pallas_call(
        kernel,
        out_shape=out_shape,
        in_specs=[smem] * 7 + [vmem] * (2 + n_in),
        out_specs=[vmem] * len(out_shape),
        scratch_shapes=[
            pltpu.VMEM((n_aux + 1, nocc, blk), jnp.bfloat16),
            pltpu.VMEM((n_aux + 1, blk, nocc), jnp.float32),
        ],
        input_output_aliases={8: PLANE + 1},
        compiler_params=pltpu.CompilerParams(vmem_limit_bytes=20 * 1024 * 1024),
        cost_estimate=pl.CostEstimate(
            flops=3 * tiles_array.size * nocc, bytes_accessed=tiles_array.size, transcendentals=0
        ),
        name="first_part",
    )(*fit_lists, *lists, bit, tiles_array, partial_fit, *shards)


def second_part(n_aux, lists, bit, tiles_array, fitted):
    slots, auxb, blk, nocc = tiles_array.shape

    def kernel(slot_ref, block_ref, gid_ref, bit_ref, tiles, zb, *refs):
        out_refs, acc = refs[:-1], refs[-1]
        acc[...] = jnp.zeros(acc.shape, acc.dtype)
        apply_fitted(
            (slot_ref, block_ref, gid_ref), tiles, zb, acc, *chunk_ends(gid_ref, slots)
        )
        for m in range(n_aux // 2):
            put(bit_ref, acc, m, out_refs[m % PLANE], m // PLANE)

    smem = pl.BlockSpec(memory_space=pltpu.SMEM)
    vmem = pl.BlockSpec(memory_space=pltpu.VMEM)
    shape = (n_aux // PLANE // 2, blk + TAIL, nocc)
    return pl.pallas_call(
        kernel,
        out_shape=[jax.ShapeDtypeStruct(shape, jnp.bfloat16)] * PLANE,
        in_specs=[smem] * 4 + [vmem, vmem],
        out_specs=[vmem] * PLANE,
        scratch_shapes=[pltpu.VMEM((n_aux + 1, blk, nocc), jnp.float32)],
        compiler_params=pltpu.CompilerParams(vmem_limit_bytes=20 * 1024 * 1024),
        cost_estimate=pl.CostEstimate(
            flops=10**10, bytes_accessed=tiles_array.size, transcendentals=0
        ),
        name="second_part",
    )(*lists, bit, tiles_array, fitted)


def all_in_one(n_aux, lists, bit, tiles_array, whole):
    slots, auxb, blk, nocc = tiles_array.shape

    def kernel(slot_ref, block_ref, gid_ref, bit_ref, tiles, c_ref, out_ref, ct, zacc, zb, acc):
        lists = (slot_ref, block_ref, gid_ref)
        clear(n_aux, ct, acc)
        zacc[...] = jnp.zeros(zacc.shape, zacc.dtype)

        @pl.loop(0, n_aux)
        def _(m):
            turn(ct, bit_ref, m, c_ref.at[m])

        _, total = chunk_ends(gid_ref, slots)
        fit(lists, tiles, ct, zacc, 0, total)
        round_fitted(zacc, zb)
        apply_fitted(lists, tiles, zb, acc, 0, total)

        @pl.loop(0, n_aux)
        def _(m):
            put(bit_ref, acc, m, out_ref, m)

    smem = pl.BlockSpec(memory_space=pltpu.SMEM)
    vmem = pl.BlockSpec(memory_space=pltpu.VMEM)
    return pl.pallas_call(
        kernel,
        out_shape=jax.ShapeDtypeStruct((n_aux, blk + TAIL, nocc), jnp.bfloat16),
        in_specs=[smem] * 4 + [vmem] * 2,
        out_specs=vmem,
        scratch_shapes=[
            pltpu.VMEM((n_aux + 1, nocc, blk), jnp.bfloat16),
            pltpu.VMEM((AB_DEV, nocc, auxb * nocc), jnp.float32),
            pltpu.VMEM((AB_DEV, nocc, auxb * nocc), jnp.bfloat16),
            pltpu.VMEM((n_aux + 1, blk, nocc), jnp.float32),
        ],
        compiler_params=pltpu.CompilerParams(vmem_limit_bytes=46 * 1024 * 1024),
        name="all_in_one",
    )(*lists, bit, tiles_array, whole)


def gate(arrays, after):
    counts = [array.shape[0] if array.ndim == 3 else 1 for array in arrays]

    def kernel(*refs):
        target, place = refs[-1], 0
        for ref, count in zip(refs, counts):
            value = ref[...]
            target[place : place + count] = value.reshape((count,) + value.shape[-2:])
            place += count

    vmem = pl.BlockSpec(memory_space=pltpu.VMEM)
    return pl.pallas_call(
        kernel,
        out_shape=jax.ShapeDtypeStruct((sum(counts),) + arrays[0].shape[-2:], arrays[0].dtype),
        in_specs=[vmem] * len(arrays) + [pl.BlockSpec(memory_space=pl.ANY)],
        out_specs=vmem,
        compiler_params=pltpu.CompilerParams(vmem_limit_bytes=4 * 1024 * 1024),
        name="gate",
    )(*arrays, after)


def merge(arrays, after, cost):
    def kernel(*refs):
        for i, ref in enumerate(refs[: len(arrays)]):
            refs[-1][i] = ref[...]

    vmem = pl.BlockSpec(memory_space=pltpu.VMEM)
    return pl.pallas_call(
        kernel,
        out_shape=jax.ShapeDtypeStruct((len(arrays),) + arrays[0].shape, arrays[0].dtype),
        in_specs=[vmem] * len(arrays) + [pl.BlockSpec(memory_space=pl.ANY)] * len(after),
        out_specs=vmem,
        compiler_params=pltpu.CompilerParams(vmem_limit_bytes=4 * 1024 * 1024),
        cost_estimate=pl.CostEstimate(flops=cost, bytes_accessed=cost // 1000, transcendentals=0),
        name="merge",
    )(*arrays, *after)


def spread(parts, after, dtypes, blk, bb_dev):
    count, rows, nocc = parts[0].shape

    def kernel(*refs):
        sources, targets = refs[: len(parts)], refs[len(parts) + len(after) :]
        for i in range(count):
            sums = [jnp.zeros((blk, nocc), jnp.float32) for _ in range(bb_dev)]
            for source in sources:
                value = source[i, :blk, :].astype(jnp.float32)
                which = source[i, blk:, :][:1].astype(jnp.float32)
                for b in range(bb_dev):
                    sums[b] = sums[b] + jnp.where(which == b, value, 0.0)
            for b in range(bb_dev):
                targets[i][b * blk : (b + 1) * blk, :] = sums[b].astype(targets[i].dtype)

    vmem = pl.BlockSpec(memory_space=pltpu.VMEM)
    return pl.pallas_call(
        kernel,
        out_shape=[jax.ShapeDtypeStruct((bb_dev * blk, nocc), dtype) for dtype in dtypes],
        in_specs=[vmem] * len(parts) + [pl.BlockSpec(memory_space=pl.ANY)] * len(after),
        out_specs=[vmem] * count,
        compiler_params=pltpu.CompilerParams(vmem_limit_bytes=4 * 1024 * 1024),
        cost_estimate=pl.CostEstimate(
            flops=SPREAD_COST, bytes_accessed=SPREAD_COST // 1000, transcendentals=0
        ),
        name="spread",
    )(*parts, *after)


def total_of(arrays, dtype, cost):
    def kernel(*refs):
        value = refs[0][...].astype(jnp.float32)
        for ref in refs[1:-1]:
            value = value + ref[...].astype(jnp.float32)
        refs[-1][...] = value.astype(refs[-1].dtype)

    vmem = pl.BlockSpec(memory_space=pltpu.VMEM)
    return pl.pallas_call(
        kernel,
        out_shape=jax.ShapeDtypeStruct(arrays[0].shape, dtype),
        in_specs=[vmem] * len(arrays),
        out_specs=vmem,
        compiler_params=pltpu.CompilerParams(vmem_limit_bytes=4 * 1024 * 1024),
        cost_estimate=pl.CostEstimate(flops=cost, bytes_accessed=cost // 1000, transcendentals=0),
        name="total_of",
    )(*arrays)


def owner_sum(parts, blk, bb_dev):
    n_aux, rows, nocc = parts.shape

    def kernel(parts_ref, out_ref):
        sums = [jnp.zeros((blk, nocc), jnp.float32) for _ in range(bb_dev)]
        for s in range(n_aux):
            value = parts_ref[s, :blk, :].astype(jnp.float32)
            which = parts_ref[s, blk:, :][:1].astype(jnp.float32)
            for b in range(bb_dev):
                sums[b] = sums[b] + jnp.where(which == b, value, 0.0)
        for b in range(bb_dev):
            out_ref[b * blk : (b + 1) * blk, :] = sums[b].astype(out_ref.dtype)

    vmem = pl.BlockSpec(memory_space=pltpu.VMEM)
    return pl.pallas_call(
        kernel,
        out_shape=jax.ShapeDtypeStruct((bb_dev * blk, nocc), jnp.bfloat16),
        in_specs=[vmem],
        out_specs=vmem,
        name="owner_sum",
    )(parts)


def on_device(tiles, c_orbitals, basis_order, tile_block, tile_aux, live):
    blk, nocc = tiles.shape[2:]
    n_aux = lax.axis_size("aux")
    bb_dev = basis_order.shape[0] // n_aux
    direct = n_aux == DIRECT

    def swap(array, m):
        return lax.ppermute(array, "aux", [(i, i ^ m) for i in range(n_aux)])

    base = lax.axis_index("aux").astype(jnp.int32) if direct else jnp.int32(0)
    packed = pack_slots(tile_block, tile_aux, live, basis_order, base, bb_dev)
    where_to, which, group, alive = unpack_slots(packed, bb_dev)
    bit = bits_of(where_to, which, alive, n_aux)
    if not direct:
        lists = chunk_lists(where_to, where_to < 0, alive, group, n_aux)
        whole = lax.all_gather(c_orbitals, "aux", axis=0, tiled=True)
        whole = whole.reshape(n_aux, bb_dev * blk, nocc)
        parts = all_in_one(n_aux, lists, bit, tiles, whole)
        moved = lax.all_to_all(parts, "aux", 0, 0, tiled=True)
        return owner_sum(moved, blk, bb_dev)

    depth = n_aux // PLANE
    half = depth // 2
    side = where_to % PLANE >= 2
    last = (where_to >= 3 * PLANE) | ((where_to >= PLANE) & side)
    fit_lists = chunk_lists(where_to, last, alive, group, n_aux)
    two = swap(c_orbitals, 2 * PLANE)
    one = swap(c_orbitals, PLANE)
    beside = swap(c_orbitals, 2)
    across = swap(c_orbitals, 1)
    three = swap(two, PLANE)
    pair = merge([one, two], [], SPREAD_COST)
    pair_beside = swap(pair, 2)
    three_beside = swap(three, 2)
    early = [pair, swap(pair, 1), across, beside, swap(beside, 1)]
    early_from = [(1, (2, None)), (2, (3, None)), (3, (4, None))]
    late_from = []
    for core in range(2):
        early_from += [(PLANE + core, (core, 0)), (2 * PLANE + core, (core, 1))]
        late_from += [
            (PLANE + 2 + core, (core, 0)),
            (2 * PLANE + 2 + core, (core, 1)),
            (3 * PLANE + core, (core, 2)),
            (3 * PLANE + 2 + core, (core, 3)),
        ]
    partial_fit, packed = begin(
        n_aux, fit_lists, bit, packed, tiles, c_orbitals, early, early_from
    )
    late = gate([pair_beside, three, three_beside], partial_fit)
    where_to, _, group, alive = unpack_slots(packed, bb_dev)
    lists = chunk_lists(where_to, where_to < n_aux // 2, alive, group, n_aux)
    *far, fitted, _ = first_part(
        n_aux, fit_lists, lists, bit, tiles, partial_fit, [late, swap(late, 1)], late_from
    )
    far = [far[0]] + [swap(far[r], r) for r in range(1, PLANE)]
    near = second_part(n_aux, lists, bit, tiles, fitted)
    near = [near[0]] + [swap(near[r], r) for r in range(1, PLANE)]
    far = spread(far, [], [jnp.bfloat16] * half, blk, bb_dev)
    near = spread(
        near, [far[0]], [jnp.float32] + [jnp.bfloat16] * (half - 1), blk, bb_dev
    )
    far = [swap(far[i], (half + i) * PLANE) for i in range(half)]
    far = total_of(far, jnp.float32, SPREAD_COST)
    near = [near[0]] + [swap(near[dz], dz * PLANE) for dz in range(1, half)]
    return total_of(near + [far], jnp.bfloat16, 0)


def solution(mesh):
    return jax.shard_map(
        on_device,
        mesh=mesh,
        in_specs=(
            P(("grp", "aux"), None, None, None),
            P(("grp", "aux"), None),
            P("grp"),
            P(("grp", "aux")),
            P(("grp", "aux")),
            P(("grp", "aux")),
        ),
        out_specs=P(("grp", "aux"), None),
        check_vma=False,
    )
```

```python
import functools

import jax
import jax.numpy as jnp
from jax import lax
from jax.experimental import pallas as pl
from jax.experimental.pallas import tpu as pltpu
from jax.sharding import PartitionSpec as P

AB_DEV = 8
CHUNK = 4
UNROLL = 2
TAIL = 16
PLANE = 4
SPREAD_COST = 10**10
DIRECT = 16


def pack_slots(tile_block, tile_aux, live, basis_order, base, bb_dev):
    nbb = basis_order.shape[0]
    position = jnp.sum(
        jnp.where(
            basis_order[None, :] == tile_block[:, None], lax.iota(jnp.int32, nbb)[None, :], 0
        ),
        axis=1,
    )
    owner = jnp.bitwise_xor(position // bb_dev, base)
    alive = (lax.iota(jnp.int32, tile_block.shape[0]) < live[0]).astype(jnp.int32)
    return ((owner * bb_dev + position % bb_dev) * AB_DEV + tile_aux) * 2 + alive


def unpack_slots(packed, bb_dev):
    rest = packed // 2
    tile_aux = rest % AB_DEV
    rest = rest // AB_DEV
    return rest // bb_dev, rest % bb_dev, tile_aux, packed % 2 == 1


def chunk_lists(where_to, later, alive, tile_aux, n_aux):
    slots = where_to.shape[0]
    keys = 2 * AB_DEV
    chunks = slots // CHUNK + keys
    t = lax.iota(jnp.int32, slots)
    group = jnp.where(alive, tile_aux + jnp.where(later, AB_DEV, 0), keys)
    ids = lax.iota(jnp.int32, keys)
    counts = jnp.sum((group[None, :] == ids[:, None]).astype(jnp.int32), axis=1)
    need = (counts + CHUNK - 1) // CHUNK
    ends = jnp.sum(jnp.where(ids[None, :] <= ids[:, None], need[None, :], 0), axis=1)
    rank = jnp.sum(
        ((group[None, :] == group[:, None]) & (t[None, :] < t[:, None])).astype(jnp.int32), axis=1
    )
    start = jnp.sum(jnp.where(group[:, None] > ids[None, :], need[None, :], 0), axis=1)
    place = jnp.where(alive, start * CHUNK + rank, -1)
    q = lax.iota(jnp.int32, chunks * CHUNK)
    hit = place[None, :] == q[:, None]
    lead = place[None, :] == (q // CHUNK * CHUNK)[:, None]
    valid = jnp.any(hit, axis=1)
    slot = jnp.sum(jnp.where(hit, t[None, :], 0), axis=1)
    slot = jnp.where(valid, slot, jnp.sum(jnp.where(lead, t[None, :], 0), axis=1))
    block = jnp.where(valid, jnp.sum(jnp.where(hit, where_to[None, :], 0), axis=1), n_aux)
    gid = jnp.sum(
        (lax.iota(jnp.int32, chunks)[:, None] >= ends[None, :]).astype(jnp.int32), axis=1
    )
    return slot, block, jnp.concatenate([gid % AB_DEV, ends])


def bits_of(where_to, which, alive, n_aux):
    return jnp.max(
        jnp.where(
            (where_to[None, :] == lax.iota(jnp.int32, n_aux)[:, None]) & alive[None, :],
            which[None, :],
            0,
        ),
        axis=1,
    )


def slab(tiles, slot):
    return jnp.concatenate([tiles[slot, p] for p in range(tiles.shape[1])], axis=1)


def chunk_ends(gid_ref, slots):
    chunks = slots // CHUNK + 2 * AB_DEV
    return gid_ref[chunks + AB_DEV - 1], gid_ref[chunks + 2 * AB_DEV - 1]


def turn(ct, bit_ref, m, source):
    blk = ct.shape[2]
    row = pl.multiple_of(bit_ref[m] * blk, blk)
    ct[m] = source[pl.ds(row, blk), :].T


def fit(lists, tiles, ct, zacc, low, high):
    slot_ref, block_ref, gid_ref = lists

    @pl.loop(0, (high - low + UNROLL - 1) // UNROLL)
    def _(step):
        for chunk in [low + step * UNROLL + u for u in range(UNROLL)]:
            keep = jnp.where(chunk < high, 0, ct.shape[0] - 1)
            spots = [chunk * CHUNK + i for i in range(CHUNK)]
            left = jnp.concatenate(
                [ct[jnp.maximum(block_ref[pos], keep)] for pos in spots], axis=1
            )
            right = jnp.concatenate([slab(tiles, slot_ref[pos]) for pos in spots], axis=0)
            zacc[gid_ref[chunk]] += jnp.dot(left, right, preferred_element_type=jnp.float32)


def apply_fitted(lists, tiles, zb, acc, low, high):
    slot_ref, block_ref, gid_ref = lists
    blk = acc.shape[1]

    @pl.loop(0, (high - low + UNROLL - 1) // UNROLL)
    def _(step):
        for chunk in [low + step * UNROLL + u for u in range(UNROLL)]:
            spots = [chunk * CHUNK + i for i in range(CHUNK)]
            left = jnp.concatenate([slab(tiles, slot_ref[pos]) for pos in spots], axis=0)
            value = lax.dot_general(
                left,
                zb[gid_ref[chunk]],
                (((1,), (1,)), ((), ())),
                preferred_element_type=jnp.float32,
            )
            for i, pos in enumerate(spots):
                acc[block_ref[pos]] += value[i * blk : (i + 1) * blk]


def begin(n_aux, lists, bit, packed, tiles_array, own_array, shards, sources):
    slots, auxb, blk, nocc = tiles_array.shape
    n_in = len(shards)

    def kernel(slot_ref, block_ref, gid_ref, bit_ref, packed_ref, tiles, own, *refs):
        c_refs, (zacc, passed, ct) = refs[:n_in], refs[n_in:]
        passed[...] = packed_ref[...]
        zacc[...] = jnp.zeros(zacc.shape, zacc.dtype)
        ct[n_aux] = jnp.zeros((nocc, blk), ct.dtype)
        turn(ct, bit_ref, 0, own)
        for m, (ref, i) in sources:
            turn(ct, bit_ref, m, c_refs[ref] if i is None else c_refs[ref].at[i])
        early, _ = chunk_ends(gid_ref, slots)
        fit((slot_ref, block_ref, gid_ref), tiles, ct, zacc, 0, early)

    smem = pl.BlockSpec(memory_space=pltpu.SMEM)
    vmem = pl.BlockSpec(memory_space=pltpu.VMEM)
    return pl.pallas_call(
        kernel,
        out_shape=[
            jax.ShapeDtypeStruct((AB_DEV, nocc, auxb * nocc), jnp.float32),
            jax.ShapeDtypeStruct(packed.shape, packed.dtype),
        ],
        in_specs=[smem] * 4 + [vmem] * (3 + n_in),
        out_specs=[vmem] * 2,
        scratch_shapes=[pltpu.VMEM((n_aux + 1, nocc, blk), jnp.bfloat16)],
        compiler_params=pltpu.CompilerParams(vmem_limit_bytes=20 * 1024 * 1024),
        cost_estimate=pl.CostEstimate(
            flops=2 * tiles_array.size * nocc, bytes_accessed=tiles_array.size, transcendentals=0
        ),
        name="begin",
    )(*lists, bit, packed, tiles_array, own_array, *shards)


def put(bit_ref, acc, m, out_ref, place):
    blk, nocc = acc.shape[1:]
    out_ref[place, :blk, :] = acc[m].astype(out_ref.dtype)
    out_ref[place, blk:, :] = jnp.full((TAIL, nocc), bit_ref[m], jnp.int32).astype(
        jnp.float32
    ).astype(out_ref.dtype)


def clear(n_aux, ct, acc):
    ct[n_aux] = jnp.zeros(ct.shape[1:], ct.dtype)
    acc[...] = jnp.zeros(acc.shape, acc.dtype)


def round_fitted(zacc, zb):
    for g in range(zacc.shape[0]):
        zb[g] = zacc[g].astype(zb.dtype)


def first_part(n_aux, fit_lists, lists, bit, tiles_array, partial_fit, shards, sources):
    slots, auxb, blk, nocc = tiles_array.shape
    n_in = len(shards)

    def kernel(*refs):
        fit_refs, refs = refs[:3], refs[3:]
        list_refs, bit_ref, tiles = refs[:3], refs[3], refs[4]
        c_refs, out_refs = refs[6 : 6 + n_in], refs[6 + n_in : -4]
        zb, zacc, ct, acc = refs[-4:]
        clear(n_aux, ct, acc)
        for m, (ref, i) in sources:
            turn(ct, bit_ref, m, c_refs[ref] if i is None else c_refs[ref].at[i])
        fit(fit_refs, tiles, ct, zacc, *chunk_ends(fit_refs[2], slots))
        round_fitted(zacc, zb)
        far, _ = chunk_ends(list_refs[2], slots)
        apply_fitted(list_refs, tiles, zb, acc, 0, far)
        for m in range(PLANE, n_aux):
            put(bit_ref, acc, m, out_refs[m % PLANE], m // PLANE - 1)

    smem = pl.BlockSpec(memory_space=pltpu.SMEM)
    vmem = pl.BlockSpec(memory_space=pltpu.VMEM)
    shape = (n_aux // PLANE - 1, blk + TAIL, nocc)
    out_shape = [jax.ShapeDtypeStruct(shape, jnp.bfloat16)] * PLANE
    out_shape = out_shape + [
        jax.ShapeDtypeStruct((AB_DEV, nocc, auxb * nocc), jnp.bfloat16),
        jax.ShapeDtypeStruct(partial_fit.shape, partial_fit.dtype),
    ]
    return pl.pallas_call(
        kernel,
        out_shape=out_shape,
        in_specs=[smem] * 7 + [vmem] * (2 + n_in),
        out_specs=[vmem] * len(out_shape),
        scratch_shapes=[
            pltpu.VMEM((n_aux + 1, nocc, blk), jnp.bfloat16),
            pltpu.VMEM((n_aux + 1, blk, nocc), jnp.float32),
        ],
        input_output_aliases={8: PLANE + 1},
        compiler_params=pltpu.CompilerParams(vmem_limit_bytes=20 * 1024 * 1024),
        cost_estimate=pl.CostEstimate(
            flops=3 * tiles_array.size * nocc, bytes_accessed=tiles_array.size, transcendentals=0
        ),
        name="first_part",
    )(*fit_lists, *lists, bit, tiles_array, partial_fit, *shards)


def second_part(n_aux, lists, bit, tiles_array, fitted):
    slots, auxb, blk, nocc = tiles_array.shape

    def kernel(slot_ref, block_ref, gid_ref, bit_ref, tiles, zb, *refs):
        out_refs, acc = refs[:-1], refs[-1]
        acc[...] = jnp.zeros(acc.shape, acc.dtype)
        apply_fitted(
            (slot_ref, block_ref, gid_ref), tiles, zb, acc, *chunk_ends(gid_ref, slots)
        )
        for m in range(PLANE):
            put(bit_ref, acc, m, out_refs[m], 0)

    smem = pl.BlockSpec(memory_space=pltpu.SMEM)
    vmem = pl.BlockSpec(memory_space=pltpu.VMEM)
    shape = (1, blk + TAIL, nocc)
    return pl.pallas_call(
        kernel,
        out_shape=[jax.ShapeDtypeStruct(shape, jnp.bfloat16)] * PLANE,
        in_specs=[smem] * 4 + [vmem, vmem],
        out_specs=[vmem] * PLANE,
        scratch_shapes=[pltpu.VMEM((n_aux + 1, blk, nocc), jnp.float32)],
        compiler_params=pltpu.CompilerParams(vmem_limit_bytes=20 * 1024 * 1024),
        cost_estimate=pl.CostEstimate(
            flops=10**10, bytes_accessed=tiles_array.size, transcendentals=0
        ),
        name="second_part",
    )(*lists, bit, tiles_array, fitted)


def all_in_one(n_aux, lists, bit, tiles_array, whole):
    slots, auxb, blk, nocc = tiles_array.shape

    def kernel(slot_ref, block_ref, gid_ref, bit_ref, tiles, c_ref, out_ref, ct, zacc, zb, acc):
        lists = (slot_ref, block_ref, gid_ref)
        clear(n_aux, ct, acc)
        zacc[...] = jnp.zeros(zacc.shape, zacc.dtype)

        @pl.loop(0, n_aux)
        def _(m):
            turn(ct, bit_ref, m, c_ref.at[m])

        _, total = chunk_ends(gid_ref, slots)
        fit(lists, tiles, ct, zacc, 0, total)
        round_fitted(zacc, zb)
        apply_fitted(lists, tiles, zb, acc, 0, total)

        @pl.loop(0, n_aux)
        def _(m):
            put(bit_ref, acc, m, out_ref, m)

    smem = pl.BlockSpec(memory_space=pltpu.SMEM)
    vmem = pl.BlockSpec(memory_space=pltpu.VMEM)
    return pl.pallas_call(
        kernel,
        out_shape=jax.ShapeDtypeStruct((n_aux, blk + TAIL, nocc), jnp.bfloat16),
        in_specs=[smem] * 4 + [vmem] * 2,
        out_specs=vmem,
        scratch_shapes=[
            pltpu.VMEM((n_aux + 1, nocc, blk), jnp.bfloat16),
            pltpu.VMEM((AB_DEV, nocc, auxb * nocc), jnp.float32),
            pltpu.VMEM((AB_DEV, nocc, auxb * nocc), jnp.bfloat16),
            pltpu.VMEM((n_aux + 1, blk, nocc), jnp.float32),
        ],
        compiler_params=pltpu.CompilerParams(vmem_limit_bytes=46 * 1024 * 1024),
        name="all_in_one",
    )(*lists, bit, tiles_array, whole)


def gate(arrays, after):
    counts = [array.shape[0] if array.ndim == 3 else 1 for array in arrays]

    def kernel(*refs):
        target, place = refs[-1], 0
        for ref, count in zip(refs, counts):
            value = ref[...]
            target[place : place + count] = value.reshape((count,) + value.shape[-2:])
            place += count

    vmem = pl.BlockSpec(memory_space=pltpu.VMEM)
    return pl.pallas_call(
        kernel,
        out_shape=jax.ShapeDtypeStruct((sum(counts),) + arrays[0].shape[-2:], arrays[0].dtype),
        in_specs=[vmem] * len(arrays) + [pl.BlockSpec(memory_space=pl.ANY)],
        out_specs=vmem,
        compiler_params=pltpu.CompilerParams(vmem_limit_bytes=4 * 1024 * 1024),
        name="gate",
    )(*arrays, after)


def merge(arrays, after, cost):
    def kernel(*refs):
        for i, ref in enumerate(refs[: len(arrays)]):
            refs[-1][i] = ref[...]

    vmem = pl.BlockSpec(memory_space=pltpu.VMEM)
    return pl.pallas_call(
        kernel,
        out_shape=jax.ShapeDtypeStruct((len(arrays),) + arrays[0].shape, arrays[0].dtype),
        in_specs=[vmem] * len(arrays) + [pl.BlockSpec(memory_space=pl.ANY)] * len(after),
        out_specs=vmem,
        compiler_params=pltpu.CompilerParams(vmem_limit_bytes=4 * 1024 * 1024),
        cost_estimate=pl.CostEstimate(flops=cost, bytes_accessed=cost // 1000, transcendentals=0),
        name="merge",
    )(*arrays, *after)


def placed_sum(sources, i, blk, bb_dev):
    nocc = sources[0].shape[2]
    sums = [jnp.zeros((blk, nocc), jnp.float32) for _ in range(bb_dev)]
    for source in sources:
        value = source[i, :blk, :].astype(jnp.float32)
        which = source[i, blk:, :][:1].astype(jnp.float32)
        for b in range(bb_dev):
            sums[b] = sums[b] + jnp.where(which == b, value, 0.0)
    return sums


def spread(parts, blk, bb_dev):
    count, rows, nocc = parts[0].shape

    def kernel(*refs):
        sources, targets = refs[: len(parts)], refs[len(parts) :]
        for i in range(count):
            for b, value in enumerate(placed_sum(sources, i, blk, bb_dev)):
                targets[i][b * blk : (b + 1) * blk, :] = value.astype(targets[i].dtype)

    vmem = pl.BlockSpec(memory_space=pltpu.VMEM)
    return pl.pallas_call(
        kernel,
        out_shape=[jax.ShapeDtypeStruct((bb_dev * blk, nocc), jnp.bfloat16)] * count,
        in_specs=[vmem] * len(parts),
        out_specs=[vmem] * count,
        compiler_params=pltpu.CompilerParams(vmem_limit_bytes=4 * 1024 * 1024),
        cost_estimate=pl.CostEstimate(
            flops=SPREAD_COST, bytes_accessed=SPREAD_COST // 1000, transcendentals=0
        ),
        name="spread",
    )(*parts)


def total_of(parts, arrays, blk, bb_dev):
    nocc = parts[0].shape[2]

    def kernel(*refs):
        sources, others, target = refs[: len(parts)], refs[len(parts) : -1], refs[-1]
        for b, value in enumerate(placed_sum(sources, 0, blk, bb_dev)):
            for other in others:
                value = value + other[b * blk : (b + 1) * blk, :].astype(jnp.float32)
            target[b * blk : (b + 1) * blk, :] = value.astype(target.dtype)

    vmem = pl.BlockSpec(memory_space=pltpu.VMEM)
    return pl.pallas_call(
        kernel,
        out_shape=jax.ShapeDtypeStruct((bb_dev * blk, nocc), jnp.bfloat16),
        in_specs=[vmem] * (len(parts) + len(arrays)),
        out_specs=vmem,
        compiler_params=pltpu.CompilerParams(vmem_limit_bytes=4 * 1024 * 1024),
        name="total_of",
    )(*parts, *arrays)


def owner_sum(parts, blk, bb_dev):
    n_aux, rows, nocc = parts.shape

    def kernel(parts_ref, out_ref):
        sums = [jnp.zeros((blk, nocc), jnp.float32) for _ in range(bb_dev)]
        for s in range(n_aux):
            value = parts_ref[s, :blk, :].astype(jnp.float32)
            which = parts_ref[s, blk:, :][:1].astype(jnp.float32)
            for b in range(bb_dev):
                sums[b] = sums[b] + jnp.where(which == b, value, 0.0)
        for b in range(bb_dev):
            out_ref[b * blk : (b + 1) * blk, :] = sums[b].astype(out_ref.dtype)

    vmem = pl.BlockSpec(memory_space=pltpu.VMEM)
    return pl.pallas_call(
        kernel,
        out_shape=jax.ShapeDtypeStruct((bb_dev * blk, nocc), jnp.bfloat16),
        in_specs=[vmem],
        out_specs=vmem,
        name="owner_sum",
    )(parts)


def on_device(tiles, c_orbitals, basis_order, tile_block, tile_aux, live):
    blk, nocc = tiles.shape[2:]
    n_aux = lax.axis_size("aux")
    bb_dev = basis_order.shape[0] // n_aux
    direct = n_aux == DIRECT

    def swap(array, m):
        return lax.ppermute(array, "aux", [(i, i ^ m) for i in range(n_aux)])

    base = lax.axis_index("aux").astype(jnp.int32) if direct else jnp.int32(0)
    packed = pack_slots(tile_block, tile_aux, live, basis_order, base, bb_dev)
    where_to, which, group, alive = unpack_slots(packed, bb_dev)
    bit = bits_of(where_to, which, alive, n_aux)
    if not direct:
        lists = chunk_lists(where_to, where_to < 0, alive, group, n_aux)
        whole = lax.all_gather(c_orbitals, "aux", axis=0, tiled=True)
        whole = whole.reshape(n_aux, bb_dev * blk, nocc)
        parts = all_in_one(n_aux, lists, bit, tiles, whole)
        moved = lax.all_to_all(parts, "aux", 0, 0, tiled=True)
        return owner_sum(moved, blk, bb_dev)

    depth = n_aux // PLANE
    side = where_to % PLANE >= 2
    last = (where_to >= 3 * PLANE) | ((where_to >= PLANE) & side)
    fit_lists = chunk_lists(where_to, last, alive, group, n_aux)
    two = swap(c_orbitals, 2 * PLANE)
    one = swap(c_orbitals, PLANE)
    beside = swap(c_orbitals, 2)
    across = swap(c_orbitals, 1)
    three = swap(c_orbitals, 3 * PLANE)
    pair = merge([one, two], [], SPREAD_COST)
    pair_beside = swap(pair, 2)
    three_beside = swap(three, 2)
    early = [pair, swap(pair, 1), across, beside, swap(beside, 1)]
    early_from = [(1, (2, None)), (2, (3, None)), (3, (4, None))]
    late_from = []
    for core in range(2):
        early_from += [(PLANE + core, (core, 0)), (2 * PLANE + core, (core, 1))]
        late_from += [
            (PLANE + 2 + core, (core, 0)),
            (2 * PLANE + 2 + core, (core, 1)),
            (3 * PLANE + core, (core, 2)),
            (3 * PLANE + 2 + core, (core, 3)),
        ]
    partial_fit, packed = begin(
        n_aux, fit_lists, bit, packed, tiles, c_orbitals, early, early_from
    )
    late = gate([pair_beside, three, three_beside], partial_fit)
    where_to, _, group, alive = unpack_slots(packed, bb_dev)
    lists = chunk_lists(where_to, where_to < PLANE, alive, group, n_aux)
    *far, fitted, _ = first_part(
        n_aux, fit_lists, lists, bit, tiles, partial_fit, [late, swap(late, 1)], late_from
    )
    far = [far[0]] + [swap(far[r], r) for r in range(1, PLANE)]
    near = second_part(n_aux, lists, bit, tiles, fitted)
    near = [near[0]] + [swap(near[r], r) for r in range(1, PLANE)]
    far = spread(far, blk, bb_dev)
    far = [swap(far[dz - 1], dz * PLANE) for dz in range(depth - 1, 0, -1)]
    return total_of(near, far, blk, bb_dev)


def solution(mesh):
    return jax.shard_map(
        on_device,
        mesh=mesh,
        in_specs=(
            P(("grp", "aux"), None, None, None),
            P(("grp", "aux"), None),
            P("grp"),
            P(("grp", "aux")),
            P(("grp", "aux")),
            P(("grp", "aux")),
        ),
        out_specs=P(("grp", "aux"), None),
        check_vma=False,
    )
```

```python
import functools

import jax
import jax.numpy as jnp
from jax import lax
from jax.experimental import pallas as pl
from jax.experimental.pallas import tpu as pltpu
from jax.sharding import PartitionSpec as P

AB_DEV = 8
CHUNK = 4
UNROLL = 4
TAIL = 16
PLANE = 4
SPREAD_COST = 10**10
DIRECT = 16


def pack_slots(tile_block, tile_aux, live, basis_order, base, bb_dev):
    nbb = basis_order.shape[0]
    position = jnp.sum(
        jnp.where(
            basis_order[None, :] == tile_block[:, None], lax.iota(jnp.int32, nbb)[None, :], 0
        ),
        axis=1,
    )
    owner = jnp.bitwise_xor(position // bb_dev, base)
    alive = (lax.iota(jnp.int32, tile_block.shape[0]) < live[0]).astype(jnp.int32)
    return ((owner * bb_dev + position % bb_dev) * AB_DEV + tile_aux) * 2 + alive


def unpack_slots(packed, bb_dev):
    rest = packed // 2
    tile_aux = rest % AB_DEV
    rest = rest // AB_DEV
    return rest // bb_dev, rest % bb_dev, tile_aux, packed % 2 == 1


def chunk_lists(where_to, later, alive, tile_aux, n_aux):
    slots = where_to.shape[0]
    keys = 2 * AB_DEV
    chunks = slots // CHUNK + keys
    t = lax.iota(jnp.int32, slots)
    group = jnp.where(alive, tile_aux + jnp.where(later, AB_DEV, 0), keys)
    ids = lax.iota(jnp.int32, keys)
    counts = jnp.sum((group[None, :] == ids[:, None]).astype(jnp.int32), axis=1)
    need = (counts + CHUNK - 1) // CHUNK
    ends = jnp.sum(jnp.where(ids[None, :] <= ids[:, None], need[None, :], 0), axis=1)
    rank = jnp.sum(
        ((group[None, :] == group[:, None]) & (t[None, :] < t[:, None])).astype(jnp.int32), axis=1
    )
    start = jnp.sum(jnp.where(group[:, None] > ids[None, :], need[None, :], 0), axis=1)
    place = jnp.where(alive, start * CHUNK + rank, -1)
    q = lax.iota(jnp.int32, chunks * CHUNK)
    hit = place[None, :] == q[:, None]
    lead = place[None, :] == (q // CHUNK * CHUNK)[:, None]
    valid = jnp.any(hit, axis=1)
    slot = jnp.sum(jnp.where(hit, t[None, :], 0), axis=1)
    slot = jnp.where(valid, slot, jnp.sum(jnp.where(lead, t[None, :], 0), axis=1))
    block = jnp.where(valid, jnp.sum(jnp.where(hit, where_to[None, :], 0), axis=1), n_aux)
    gid = jnp.sum(
        (lax.iota(jnp.int32, chunks)[:, None] >= ends[None, :]).astype(jnp.int32), axis=1
    )
    return slot, block, jnp.concatenate([gid % AB_DEV, ends])


def bits_of(where_to, which, alive, n_aux):
    return jnp.max(
        jnp.where(
            (where_to[None, :] == lax.iota(jnp.int32, n_aux)[:, None]) & alive[None, :],
            which[None, :],
            0,
        ),
        axis=1,
    )


def slab(tiles, slot):
    return jnp.concatenate([tiles[slot, p] for p in range(tiles.shape[1])], axis=1)


def chunk_ends(gid_ref, slots):
    chunks = slots // CHUNK + 2 * AB_DEV
    return gid_ref[chunks + AB_DEV - 1], gid_ref[chunks + 2 * AB_DEV - 1]


def turn(ct, bit_ref, m, source):
    blk = ct.shape[2]
    row = pl.multiple_of(bit_ref[m] * blk, blk)
    ct[m] = source[pl.ds(row, blk), :].T


def sweep(low, high, body):
    whole = (high - low) // UNROLL

    @pl.loop(0, whole)
    def _(step):
        body([low + step * UNROLL + u for u in range(UNROLL)])

    @pl.loop(low + whole * UNROLL, high)
    def _(chunk):
        body([chunk])


def fit(lists, tiles, ct, zacc, low, high):
    slot_ref, block_ref, gid_ref = lists

    def body(group):
        for chunk in group:
            spots = [chunk * CHUNK + i for i in range(CHUNK)]
            left = jnp.concatenate([ct[block_ref[pos]] for pos in spots], axis=1)
            right = jnp.concatenate([slab(tiles, slot_ref[pos]) for pos in spots], axis=0)
            zacc[gid_ref[chunk]] += jnp.dot(left, right, preferred_element_type=jnp.float32)

    sweep(low, high, body)


def apply_fitted(lists, tiles, zb, acc, low, high):
    slot_ref, block_ref, gid_ref = lists
    blk = acc.shape[1]

    def body(group):
        for chunk in group:
            spots = [chunk * CHUNK + i for i in range(CHUNK)]
            left = jnp.concatenate([slab(tiles, slot_ref[pos]) for pos in spots], axis=0)
            value = lax.dot_general(
                left,
                zb[gid_ref[chunk]],
                (((1,), (1,)), ((), ())),
                preferred_element_type=jnp.float32,
            )
            for i, pos in enumerate(spots):
                acc[block_ref[pos]] += value[i * blk : (i + 1) * blk]

    sweep(low, high, body)


def begin(n_aux, lists, bit, packed, tiles_array, own_array, shards, sources):
    slots, auxb, blk, nocc = tiles_array.shape
    n_in = len(shards)

    def kernel(slot_ref, block_ref, gid_ref, bit_ref, packed_ref, tiles, own, *refs):
        c_refs, (zacc, passed, ct) = refs[:n_in], refs[n_in:]
        passed[...] = packed_ref[...]
        zacc[...] = jnp.zeros(zacc.shape, zacc.dtype)
        ct[n_aux] = jnp.zeros((nocc, blk), ct.dtype)
        turn(ct, bit_ref, 0, own)
        for m, (ref, i) in sources:
            turn(ct, bit_ref, m, c_refs[ref] if i is None else c_refs[ref].at[i])
        early, _ = chunk_ends(gid_ref, slots)
        fit((slot_ref, block_ref, gid_ref), tiles, ct, zacc, 0, early)

    smem = pl.BlockSpec(memory_space=pltpu.SMEM)
    vmem = pl.BlockSpec(memory_space=pltpu.VMEM)
    return pl.pallas_call(
        kernel,
        out_shape=[
            jax.ShapeDtypeStruct((AB_DEV, nocc, auxb * nocc), jnp.float32),
            jax.ShapeDtypeStruct(packed.shape, packed.dtype),
        ],
        in_specs=[smem] * 4 + [vmem] * (3 + n_in),
        out_specs=[vmem] * 2,
        scratch_shapes=[pltpu.VMEM((n_aux + 1, nocc, blk), jnp.bfloat16)],
        compiler_params=pltpu.CompilerParams(vmem_limit_bytes=20 * 1024 * 1024),
        cost_estimate=pl.CostEstimate(
            flops=2 * tiles_array.size * nocc, bytes_accessed=tiles_array.size, transcendentals=0
        ),
        name="begin",
    )(*lists, bit, packed, tiles_array, own_array, *shards)


def put(bit_ref, acc, m, out_ref, place):
    blk, nocc = acc.shape[1:]
    out_ref[place, :blk, :] = acc[m].astype(out_ref.dtype)
    out_ref[place, blk:, :] = jnp.full((TAIL, nocc), bit_ref[m], jnp.int32).astype(
        jnp.float32
    ).astype(out_ref.dtype)


def clear(n_aux, ct, acc):
    ct[n_aux] = jnp.zeros(ct.shape[1:], ct.dtype)
    acc[...] = jnp.zeros(acc.shape, acc.dtype)


def round_fitted(zacc, zb):
    for g in range(zacc.shape[0]):
        zb[g] = zacc[g].astype(zb.dtype)


def first_part(n_aux, fit_lists, lists, bit, tiles_array, partial_fit, shards, sources):
    slots, auxb, blk, nocc = tiles_array.shape
    n_in = len(shards)

    def kernel(*refs):
        fit_refs, refs = refs[:3], refs[3:]
        list_refs, bit_ref, tiles = refs[:3], refs[3], refs[4]
        c_refs, out_refs = refs[6 : 6 + n_in], refs[6 + n_in : -4]
        zb, zacc, ct, acc = refs[-4:]
        clear(n_aux, ct, acc)
        for m, (ref, i) in sources:
            turn(ct, bit_ref, m, c_refs[ref] if i is None else c_refs[ref].at[i])
        fit(fit_refs, tiles, ct, zacc, *chunk_ends(fit_refs[2], slots))
        round_fitted(zacc, zb)
        far, _ = chunk_ends(list_refs[2], slots)
        apply_fitted(list_refs, tiles, zb, acc, 0, far)
        for m in range(PLANE, n_aux):
            put(bit_ref, acc, m, out_refs[m % PLANE], m // PLANE - 1)

    smem = pl.BlockSpec(memory_space=pltpu.SMEM)
    vmem = pl.BlockSpec(memory_space=pltpu.VMEM)
    shape = (n_aux // PLANE - 1, blk + TAIL, nocc)
    out_shape = [jax.ShapeDtypeStruct(shape, jnp.bfloat16)] * PLANE
    out_shape = out_shape + [
        jax.ShapeDtypeStruct((AB_DEV, nocc, auxb * nocc), jnp.bfloat16),
        jax.ShapeDtypeStruct(partial_fit.shape, partial_fit.dtype),
    ]
    return pl.pallas_call(
        kernel,
        out_shape=out_shape,
        in_specs=[smem] * 7 + [vmem] * (2 + n_in),
        out_specs=[vmem] * len(out_shape),
        scratch_shapes=[
            pltpu.VMEM((n_aux + 1, nocc, blk), jnp.bfloat16),
            pltpu.VMEM((n_aux + 1, blk, nocc), jnp.float32),
        ],
        input_output_aliases={8: PLANE + 1},
        compiler_params=pltpu.CompilerParams(vmem_limit_bytes=20 * 1024 * 1024),
        cost_estimate=pl.CostEstimate(
            flops=3 * tiles_array.size * nocc, bytes_accessed=tiles_array.size, transcendentals=0
        ),
        name="first_part",
    )(*fit_lists, *lists, bit, tiles_array, partial_fit, *shards)


def second_part(n_aux, lists, bit, tiles_array, fitted, after):
    slots, auxb, blk, nocc = tiles_array.shape

    def kernel(slot_ref, block_ref, gid_ref, bit_ref, tiles, zb, _, *refs):
        out_refs, acc = refs[:-1], refs[-1]
        acc[...] = jnp.zeros(acc.shape, acc.dtype)
        apply_fitted(
            (slot_ref, block_ref, gid_ref), tiles, zb, acc, *chunk_ends(gid_ref, slots)
        )
        for m in range(PLANE):
            put(bit_ref, acc, m, out_refs[m], 0)

    smem = pl.BlockSpec(memory_space=pltpu.SMEM)
    vmem = pl.BlockSpec(memory_space=pltpu.VMEM)
    shape = (1, blk + TAIL, nocc)
    return pl.pallas_call(
        kernel,
        out_shape=[jax.ShapeDtypeStruct(shape, jnp.bfloat16)] * PLANE,
        in_specs=[smem] * 4 + [vmem, vmem, pl.BlockSpec(memory_space=pl.ANY)],
        out_specs=[vmem] * PLANE,
        scratch_shapes=[pltpu.VMEM((n_aux + 1, blk, nocc), jnp.float32)],
        compiler_params=pltpu.CompilerParams(vmem_limit_bytes=20 * 1024 * 1024),
        cost_estimate=pl.CostEstimate(
            flops=10**10, bytes_accessed=tiles_array.size, transcendentals=0
        ),
        name="second_part",
    )(*lists, bit, tiles_array, fitted, after)


def all_in_one(n_aux, lists, bit, tiles_array, whole):
    slots, auxb, blk, nocc = tiles_array.shape

    def kernel(slot_ref, block_ref, gid_ref, bit_ref, tiles, c_ref, out_ref, ct, zacc, zb, acc):
        lists = (slot_ref, block_ref, gid_ref)
        clear(n_aux, ct, acc)
        zacc[...] = jnp.zeros(zacc.shape, zacc.dtype)

        @pl.loop(0, n_aux)
        def _(m):
            turn(ct, bit_ref, m, c_ref.at[m])

        _, total = chunk_ends(gid_ref, slots)
        fit(lists, tiles, ct, zacc, 0, total)
        round_fitted(zacc, zb)
        apply_fitted(lists, tiles, zb, acc, 0, total)

        @pl.loop(0, n_aux)
        def _(m):
            put(bit_ref, acc, m, out_ref, m)

    smem = pl.BlockSpec(memory_space=pltpu.SMEM)
    vmem = pl.BlockSpec(memory_space=pltpu.VMEM)
    return pl.pallas_call(
        kernel,
        out_shape=jax.ShapeDtypeStruct((n_aux, blk + TAIL, nocc), jnp.bfloat16),
        in_specs=[smem] * 4 + [vmem] * 2,
        out_specs=vmem,
        scratch_shapes=[
            pltpu.VMEM((n_aux + 1, nocc, blk), jnp.bfloat16),
            pltpu.VMEM((AB_DEV, nocc, auxb * nocc), jnp.float32),
            pltpu.VMEM((AB_DEV, nocc, auxb * nocc), jnp.bfloat16),
            pltpu.VMEM((n_aux + 1, blk, nocc), jnp.float32),
        ],
        compiler_params=pltpu.CompilerParams(vmem_limit_bytes=46 * 1024 * 1024),
        name="all_in_one",
    )(*lists, bit, tiles_array, whole)


def gate(arrays, after):
    counts = [array.shape[0] if array.ndim == 3 else 1 for array in arrays]

    def kernel(*refs):
        target, place = refs[-1], 0
        for ref, count in zip(refs, counts):
            value = ref[...]
            target[place : place + count] = value.reshape((count,) + value.shape[-2:])
            place += count

    vmem = pl.BlockSpec(memory_space=pltpu.VMEM)
    return pl.pallas_call(
        kernel,
        out_shape=jax.ShapeDtypeStruct((sum(counts),) + arrays[0].shape[-2:], arrays[0].dtype),
        in_specs=[vmem] * len(arrays) + [pl.BlockSpec(memory_space=pl.ANY)],
        out_specs=vmem,
        compiler_params=pltpu.CompilerParams(vmem_limit_bytes=4 * 1024 * 1024),
        name="gate",
    )(*arrays, after)


def merge(arrays, after, cost):
    def kernel(*refs):
        for i, ref in enumerate(refs[: len(arrays)]):
            refs[-1][i] = ref[...]

    vmem = pl.BlockSpec(memory_space=pltpu.VMEM)
    return pl.pallas_call(
        kernel,
        out_shape=jax.ShapeDtypeStruct((len(arrays),) + arrays[0].shape, arrays[0].dtype),
        in_specs=[vmem] * len(arrays) + [pl.BlockSpec(memory_space=pl.ANY)] * len(after),
        out_specs=vmem,
        compiler_params=pltpu.CompilerParams(vmem_limit_bytes=4 * 1024 * 1024),
        cost_estimate=pl.CostEstimate(flops=cost, bytes_accessed=cost // 1000, transcendentals=0),
        name="merge",
    )(*arrays, *after)


def placed_sum(sources, i, blk, bb_dev):
    nocc = sources[0].shape[2]
    sums = [jnp.zeros((blk, nocc), jnp.float32) for _ in range(bb_dev)]
    for source in sources:
        value = source[i, :blk, :].astype(jnp.float32)
        which = source[i, blk:, :][:1].astype(jnp.float32)
        for b in range(bb_dev):
            sums[b] = sums[b] + jnp.where(which == b, value, 0.0)
    return sums


def spread(parts, dtype, blk, bb_dev):
    count, rows, nocc = parts[0].shape

    def kernel(*refs):
        sources, targets = refs[: len(parts)], refs[len(parts) :]
        for i in range(count):
            for b, value in enumerate(placed_sum(sources, i, blk, bb_dev)):
                targets[i][b * blk : (b + 1) * blk, :] = value.astype(targets[i].dtype)

    vmem = pl.BlockSpec(memory_space=pltpu.VMEM)
    return pl.pallas_call(
        kernel,
        out_shape=[jax.ShapeDtypeStruct((bb_dev * blk, nocc), dtype)] * count,
        in_specs=[vmem] * len(parts),
        out_specs=[vmem] * count,
        compiler_params=pltpu.CompilerParams(vmem_limit_bytes=4 * 1024 * 1024),
        cost_estimate=pl.CostEstimate(
            flops=SPREAD_COST, bytes_accessed=SPREAD_COST // 1000, transcendentals=0
        ),
        name="spread",
    )(*parts)


def total_of(arrays):
    def kernel(*refs):
        value = refs[0][...].astype(jnp.float32)
        for ref in refs[1:-1]:
            value = value + ref[...].astype(jnp.float32)
        refs[-1][...] = value.astype(refs[-1].dtype)

    vmem = pl.BlockSpec(memory_space=pltpu.VMEM)
    return pl.pallas_call(
        kernel,
        out_shape=jax.ShapeDtypeStruct(arrays[0].shape, jnp.bfloat16),
        in_specs=[vmem] * len(arrays),
        out_specs=vmem,
        compiler_params=pltpu.CompilerParams(vmem_limit_bytes=4 * 1024 * 1024),
        name="total_of",
    )(*arrays)


def owner_sum(parts, blk, bb_dev):
    n_aux, rows, nocc = parts.shape

    def kernel(parts_ref, out_ref):
        sums = [jnp.zeros((blk, nocc), jnp.float32) for _ in range(bb_dev)]
        for s in range(n_aux):
            value = parts_ref[s, :blk, :].astype(jnp.float32)
            which = parts_ref[s, blk:, :][:1].astype(jnp.float32)
            for b in range(bb_dev):
                sums[b] = sums[b] + jnp.where(which == b, value, 0.0)
        for b in range(bb_dev):
            out_ref[b * blk : (b + 1) * blk, :] = sums[b].astype(out_ref.dtype)

    vmem = pl.BlockSpec(memory_space=pltpu.VMEM)
    return pl.pallas_call(
        kernel,
        out_shape=jax.ShapeDtypeStruct((bb_dev * blk, nocc), jnp.bfloat16),
        in_specs=[vmem],
        out_specs=vmem,
        name="owner_sum",
    )(parts)


def on_device(tiles, c_orbitals, basis_order, tile_block, tile_aux, live):
    blk, nocc = tiles.shape[2:]
    n_aux = lax.axis_size("aux")
    bb_dev = basis_order.shape[0] // n_aux
    direct = n_aux == DIRECT

    def swap(array, m):
        return lax.ppermute(array, "aux", [(i, i ^ m) for i in range(n_aux)])

    base = lax.axis_index("aux").astype(jnp.int32) if direct else jnp.int32(0)
    packed = pack_slots(tile_block, tile_aux, live, basis_order, base, bb_dev)
    where_to, which, group, alive = unpack_slots(packed, bb_dev)
    bit = bits_of(where_to, which, alive, n_aux)
    if not direct:
        lists = chunk_lists(where_to, where_to < 0, alive, group, n_aux)
        whole = lax.all_gather(c_orbitals, "aux", axis=0, tiled=True)
        whole = whole.reshape(n_aux, bb_dev * blk, nocc)
        parts = all_in_one(n_aux, lists, bit, tiles, whole)
        moved = lax.all_to_all(parts, "aux", 0, 0, tiled=True)
        return owner_sum(moved, blk, bb_dev)

    depth = n_aux // PLANE
    side = where_to % PLANE >= 2
    last = (where_to >= 3 * PLANE) | ((where_to >= PLANE) & side)
    fit_lists = chunk_lists(where_to, last, alive, group, n_aux)
    two = swap(c_orbitals, 2 * PLANE)
    one = swap(c_orbitals, PLANE)
    beside = swap(c_orbitals, 2)
    across = swap(c_orbitals, 1)
    three = swap(c_orbitals, 3 * PLANE)
    pair = merge([one, two], [], SPREAD_COST)
    pair_beside = swap(pair, 2)
    three_beside = swap(three, 2)
    early = [pair, swap(pair, 1), across, beside, swap(beside, 1)]
    early_from = [(1, (2, None)), (2, (3, None)), (3, (4, None))]
    late_from = []
    for core in range(2):
        early_from += [(PLANE + core, (core, 0)), (2 * PLANE + core, (core, 1))]
        late_from += [
            (PLANE + 2 + core, (core, 0)),
            (2 * PLANE + 2 + core, (core, 1)),
            (3 * PLANE + core, (core, 2)),
            (3 * PLANE + 2 + core, (core, 3)),
        ]
    partial_fit, packed = begin(
        n_aux, fit_lists, bit, packed, tiles, c_orbitals, early, early_from
    )
    late = gate([pair_beside, three, three_beside], partial_fit)
    where_to, _, group, alive = unpack_slots(packed, bb_dev)
    lists = chunk_lists(where_to, where_to < PLANE, alive, group, n_aux)
    *far, fitted, _ = first_part(
        n_aux, fit_lists, lists, bit, tiles, partial_fit, [late, swap(late, 1)], late_from
    )
    far = [far[0]] + [swap(far[r], r) for r in range(1, PLANE)]
    near = second_part(n_aux, lists, bit, tiles, fitted, far[1])
    near = [near[0]] + [swap(near[r], r) for r in range(1, PLANE)]
    far = spread(far, jnp.bfloat16, blk, bb_dev)
    far = [swap(far[dz - 1], dz * PLANE) for dz in range(depth - 1, 0, -1)]
    near = spread(near, jnp.float32, blk, bb_dev)
    return total_of(list(near) + far)


def solution(mesh):
    return jax.shard_map(
        on_device,
        mesh=mesh,
        in_specs=(
            P(("grp", "aux"), None, None, None),
            P(("grp", "aux"), None),
            P("grp"),
            P(("grp", "aux")),
            P(("grp", "aux")),
            P(("grp", "aux")),
        ),
        out_specs=P(("grp", "aux"), None),
        check_vma=False,
    )
```

```python
import functools

import jax
import jax.numpy as jnp
from jax import lax
from jax.experimental import pallas as pl
from jax.experimental.pallas import tpu as pltpu
from jax.sharding import PartitionSpec as P

AB_DEV = 8
CHUNK = 2
TURNS = (8, 2, 1)
TAIL = 16
PLANE = 4
SPREAD_COST = 10**10
DIRECT = 16


def pack_slots(tile_block, tile_aux, live, basis_order, base, bb_dev):
    slots, nbb = tile_block.shape[0], basis_order.shape[0]
    k = lax.broadcasted_iota(jnp.int32, (slots, nbb), 1)
    owner = jnp.bitwise_xor(k // bb_dev, base)
    alive = lax.broadcasted_iota(jnp.int32, (slots, nbb), 0) < live[None, :]
    value = ((owner * bb_dev + k % bb_dev) * AB_DEV + tile_aux[:, None]) * 2
    value = value + alive.astype(jnp.int32)
    return jnp.sum(
        jnp.where(basis_order[None, :] == tile_block[:, None], value, 0), axis=1
    )


def unpack_slots(packed, bb_dev):
    rest = packed // 2
    tile_aux = rest % AB_DEV
    rest = rest // AB_DEV
    return rest // bb_dev, rest % bb_dev, tile_aux, packed % 2 == 1


def chunk_lists(where_to, later, alive, tile_aux, n_aux):
    slots = where_to.shape[0]
    keys = 2 * AB_DEV
    chunks = slots // CHUNK + keys
    t = lax.iota(jnp.int32, slots)
    group = jnp.where(alive, tile_aux + jnp.where(later, AB_DEV, 0), keys)
    ids = lax.iota(jnp.int32, keys)
    counts = jnp.sum((group[None, :] == ids[:, None]).astype(jnp.int32), axis=1)
    need = (counts + CHUNK - 1) // CHUNK
    ends = jnp.sum(jnp.where(ids[None, :] <= ids[:, None], need[None, :], 0), axis=1)
    rank = jnp.sum(
        ((group[None, :] == group[:, None]) & (t[None, :] < t[:, None])).astype(jnp.int32), axis=1
    )
    start = jnp.sum(jnp.where(group[:, None] > ids[None, :], need[None, :], 0), axis=1)
    place = jnp.where(alive, start * CHUNK + rank, -1)
    q = lax.iota(jnp.int32, chunks * CHUNK)
    hit = place[None, :] == q[:, None]
    lead = place[None, :] == (q // CHUNK * CHUNK)[:, None]
    valid = jnp.any(hit, axis=1)
    slot = jnp.sum(jnp.where(hit, t[None, :], 0), axis=1)
    slot = jnp.where(valid, slot, jnp.sum(jnp.where(lead, t[None, :], 0), axis=1))
    block = jnp.where(valid, jnp.sum(jnp.where(hit, where_to[None, :], 0), axis=1), n_aux)
    gid = jnp.sum(
        (lax.iota(jnp.int32, chunks)[:, None] >= ends[None, :]).astype(jnp.int32), axis=1
    )
    return slot, block, jnp.concatenate([gid % AB_DEV, ends])


def bits_of(where_to, which, alive, n_aux):
    return jnp.max(
        jnp.where(
            (where_to[None, :] == lax.iota(jnp.int32, n_aux)[:, None]) & alive[None, :],
            which[None, :],
            0,
        ),
        axis=1,
    )


def slab(tiles, slot):
    return jnp.concatenate([tiles[slot, p] for p in range(tiles.shape[1])], axis=1)


def chunk_ends(gid_ref, slots):
    chunks = slots // CHUNK + 2 * AB_DEV
    return gid_ref[chunks + AB_DEV - 1], gid_ref[chunks + 2 * AB_DEV - 1]


def turn(ct, bit_ref, m, source):
    blk = ct.shape[2]
    row = pl.multiple_of(bit_ref[m] * blk, blk)
    ct[m] = source[pl.ds(row, blk), :].T


def sweep(low, high, body):
    for size in TURNS:
        whole = (high - low) // size

        @pl.loop(0, whole)
        def _(step, low=low, size=size):
            body([low + step * size + u for u in range(size)])

        low = low + whole * size


def fit(lists, tiles, ct, zacc, low, high):
    slot_ref, block_ref, gid_ref = lists

    def body(group):
        for chunk in group:
            spots = [chunk * CHUNK + i for i in range(CHUNK)]
            left = jnp.concatenate([ct[block_ref[pos]] for pos in spots], axis=1)
            right = jnp.concatenate([slab(tiles, slot_ref[pos]) for pos in spots], axis=0)
            zacc[gid_ref[chunk]] += jnp.dot(left, right, preferred_element_type=jnp.float32)

    sweep(low, high, body)


def apply_fitted(lists, tiles, zb, acc, low, high):
    slot_ref, block_ref, gid_ref = lists
    blk = acc.shape[1]

    def body(group):
        for chunk in group:
            spots = [chunk * CHUNK + i for i in range(CHUNK)]
            left = jnp.concatenate([slab(tiles, slot_ref[pos]) for pos in spots], axis=0)
            value = lax.dot_general(
                left,
                zb[gid_ref[chunk]],
                (((1,), (1,)), ((), ())),
                preferred_element_type=jnp.float32,
            )
            for i, pos in enumerate(spots):
                acc[block_ref[pos]] += value[i * blk : (i + 1) * blk]

    sweep(low, high, body)


def begin(n_aux, lists, bit, packed, tiles_array, own_array, shards, sources):
    slots, auxb, blk, nocc = tiles_array.shape
    n_in = len(shards)

    def kernel(slot_ref, block_ref, gid_ref, bit_ref, packed_ref, tiles, own, *refs):
        c_refs, (zacc, passed, ct) = refs[:n_in], refs[n_in:]
        passed[...] = packed_ref[...]
        zacc[...] = jnp.zeros(zacc.shape, zacc.dtype)
        ct[n_aux] = jnp.zeros((nocc, blk), ct.dtype)
        turn(ct, bit_ref, 0, own)
        for m, (ref, i) in sources:
            turn(ct, bit_ref, m, c_refs[ref] if i is None else c_refs[ref].at[i])
        early, _ = chunk_ends(gid_ref, slots)
        fit((slot_ref, block_ref, gid_ref), tiles, ct, zacc, 0, early)

    smem = pl.BlockSpec(memory_space=pltpu.SMEM)
    vmem = pl.BlockSpec(memory_space=pltpu.VMEM)
    return pl.pallas_call(
        kernel,
        out_shape=[
            jax.ShapeDtypeStruct((AB_DEV, nocc, auxb * nocc), jnp.float32),
            jax.ShapeDtypeStruct(packed.shape, packed.dtype),
        ],
        in_specs=[smem] * 4 + [vmem] * (3 + n_in),
        out_specs=[vmem] * 2,
        scratch_shapes=[pltpu.VMEM((n_aux + 1, nocc, blk), jnp.bfloat16)],
        compiler_params=pltpu.CompilerParams(vmem_limit_bytes=20 * 1024 * 1024),
        cost_estimate=pl.CostEstimate(
            flops=2 * tiles_array.size * nocc, bytes_accessed=tiles_array.size, transcendentals=0
        ),
        name="begin",
    )(*lists, bit, packed, tiles_array, own_array, *shards)


def put(bit_ref, acc, m, out_ref, place):
    blk, nocc = acc.shape[1:]
    out_ref[place, :blk, :] = acc[m].astype(out_ref.dtype)
    out_ref[place, blk:, :] = jnp.full((TAIL, nocc), bit_ref[m], jnp.int32).astype(
        jnp.float32
    ).astype(out_ref.dtype)


def clear(n_aux, ct, acc):
    ct[n_aux] = jnp.zeros(ct.shape[1:], ct.dtype)
    acc[...] = jnp.zeros(acc.shape, acc.dtype)


def round_fitted(zacc, zb):
    for g in range(zacc.shape[0]):
        zb[g] = zacc[g].astype(zb.dtype)


def first_part(n_aux, fit_lists, lists, bit, tiles_array, partial_fit, shards, sources):
    slots, auxb, blk, nocc = tiles_array.shape
    n_in = len(shards)

    def kernel(*refs):
        fit_refs, refs = refs[:3], refs[3:]
        list_refs, bit_ref, tiles = refs[:3], refs[3], refs[4]
        c_refs, out_refs = refs[6 : 6 + n_in], refs[6 + n_in : -4]
        zb, zacc, ct, acc = refs[-4:]
        clear(n_aux, ct, acc)
        for m, (ref, i) in sources:
            turn(ct, bit_ref, m, c_refs[ref] if i is None else c_refs[ref].at[i])
        fit(fit_refs, tiles, ct, zacc, *chunk_ends(fit_refs[2], slots))
        round_fitted(zacc, zb)
        far, _ = chunk_ends(list_refs[2], slots)
        apply_fitted(list_refs, tiles, zb, acc, 0, far)
        for m in range(PLANE, n_aux):
            put(bit_ref, acc, m, out_refs[m % PLANE], m // PLANE - 1)

    smem = pl.BlockSpec(memory_space=pltpu.SMEM)
    vmem = pl.BlockSpec(memory_space=pltpu.VMEM)
    shape = (n_aux // PLANE - 1, blk + TAIL, nocc)
    out_shape = [jax.ShapeDtypeStruct(shape, jnp.bfloat16)] * PLANE
    out_shape = out_shape + [
        jax.ShapeDtypeStruct((AB_DEV, nocc, auxb * nocc), jnp.bfloat16),
        jax.ShapeDtypeStruct(partial_fit.shape, partial_fit.dtype),
    ]
    return pl.pallas_call(
        kernel,
        out_shape=out_shape,
        in_specs=[smem] * 7 + [vmem] * (2 + n_in),
        out_specs=[vmem] * len(out_shape),
        scratch_shapes=[
            pltpu.VMEM((n_aux + 1, nocc, blk), jnp.bfloat16),
            pltpu.VMEM((n_aux + 1, blk, nocc), jnp.float32),
        ],
        input_output_aliases={8: PLANE + 1},
        compiler_params=pltpu.CompilerParams(vmem_limit_bytes=20 * 1024 * 1024),
        cost_estimate=pl.CostEstimate(
            flops=3 * tiles_array.size * nocc, bytes_accessed=tiles_array.size, transcendentals=0
        ),
        name="first_part",
    )(*fit_lists, *lists, bit, tiles_array, partial_fit, *shards)


def second_part(n_aux, lists, bit, tiles_array, fitted, after):
    slots, auxb, blk, nocc = tiles_array.shape

    def kernel(slot_ref, block_ref, gid_ref, bit_ref, tiles, zb, _, *refs):
        out_refs, acc = refs[:-1], refs[-1]
        acc[...] = jnp.zeros(acc.shape, acc.dtype)
        apply_fitted(
            (slot_ref, block_ref, gid_ref), tiles, zb, acc, *chunk_ends(gid_ref, slots)
        )
        for m in range(PLANE):
            put(bit_ref, acc, m, out_refs[m], 0)

    smem = pl.BlockSpec(memory_space=pltpu.SMEM)
    vmem = pl.BlockSpec(memory_space=pltpu.VMEM)
    shape = (1, blk + TAIL, nocc)
    return pl.pallas_call(
        kernel,
        out_shape=[jax.ShapeDtypeStruct(shape, jnp.bfloat16)] * PLANE,
        in_specs=[smem] * 4 + [vmem, vmem, pl.BlockSpec(memory_space=pl.ANY)],
        out_specs=[vmem] * PLANE,
        scratch_shapes=[pltpu.VMEM((n_aux + 1, blk, nocc), jnp.float32)],
        compiler_params=pltpu.CompilerParams(vmem_limit_bytes=20 * 1024 * 1024),
        cost_estimate=pl.CostEstimate(
            flops=10**10, bytes_accessed=tiles_array.size, transcendentals=0
        ),
        name="second_part",
    )(*lists, bit, tiles_array, fitted, after)


def all_in_one(n_aux, lists, bit, tiles_array, whole):
    slots, auxb, blk, nocc = tiles_array.shape

    def kernel(slot_ref, block_ref, gid_ref, bit_ref, tiles, c_ref, out_ref, ct, zacc, zb, acc):
        lists = (slot_ref, block_ref, gid_ref)
        clear(n_aux, ct, acc)
        zacc[...] = jnp.zeros(zacc.shape, zacc.dtype)

        @pl.loop(0, n_aux)
        def _(m):
            turn(ct, bit_ref, m, c_ref.at[m])

        _, total = chunk_ends(gid_ref, slots)
        fit(lists, tiles, ct, zacc, 0, total)
        round_fitted(zacc, zb)
        apply_fitted(lists, tiles, zb, acc, 0, total)

        @pl.loop(0, n_aux)
        def _(m):
            put(bit_ref, acc, m, out_ref, m)

    smem = pl.BlockSpec(memory_space=pltpu.SMEM)
    vmem = pl.BlockSpec(memory_space=pltpu.VMEM)
    return pl.pallas_call(
        kernel,
        out_shape=jax.ShapeDtypeStruct((n_aux, blk + TAIL, nocc), jnp.bfloat16),
        in_specs=[smem] * 4 + [vmem] * 2,
        out_specs=vmem,
        scratch_shapes=[
            pltpu.VMEM((n_aux + 1, nocc, blk), jnp.bfloat16),
            pltpu.VMEM((AB_DEV, nocc, auxb * nocc), jnp.float32),
            pltpu.VMEM((AB_DEV, nocc, auxb * nocc), jnp.bfloat16),
            pltpu.VMEM((n_aux + 1, blk, nocc), jnp.float32),
        ],
        compiler_params=pltpu.CompilerParams(vmem_limit_bytes=46 * 1024 * 1024),
        name="all_in_one",
    )(*lists, bit, tiles_array, whole)


def gate(arrays, after):
    counts = [array.shape[0] if array.ndim == 3 else 1 for array in arrays]

    def kernel(*refs):
        target, place = refs[-1], 0
        for ref, count in zip(refs, counts):
            value = ref[...]
            target[place : place + count] = value.reshape((count,) + value.shape[-2:])
            place += count

    vmem = pl.BlockSpec(memory_space=pltpu.VMEM)
    return pl.pallas_call(
        kernel,
        out_shape=jax.ShapeDtypeStruct((sum(counts),) + arrays[0].shape[-2:], arrays[0].dtype),
        in_specs=[vmem] * len(arrays) + [pl.BlockSpec(memory_space=pl.ANY)],
        out_specs=vmem,
        compiler_params=pltpu.CompilerParams(vmem_limit_bytes=4 * 1024 * 1024),
        name="gate",
    )(*arrays, after)


def merge(arrays, after, cost):
    def kernel(*refs):
        for i, ref in enumerate(refs[: len(arrays)]):
            refs[-1][i] = ref[...]

    vmem = pl.BlockSpec(memory_space=pltpu.VMEM)
    return pl.pallas_call(
        kernel,
        out_shape=jax.ShapeDtypeStruct((len(arrays),) + arrays[0].shape, arrays[0].dtype),
        in_specs=[vmem] * len(arrays) + [pl.BlockSpec(memory_space=pl.ANY)] * len(after),
        out_specs=vmem,
        compiler_params=pltpu.CompilerParams(vmem_limit_bytes=4 * 1024 * 1024),
        cost_estimate=pl.CostEstimate(flops=cost, bytes_accessed=cost // 1000, transcendentals=0),
        name="merge",
    )(*arrays, *after)


def placed_sum(sources, i, blk, bb_dev):
    nocc = sources[0].shape[2]
    sums = [jnp.zeros((blk, nocc), jnp.float32) for _ in range(bb_dev)]
    for source in sources:
        value = source[i, :blk, :].astype(jnp.float32)
        which = source[i, blk:, :][:1].astype(jnp.float32)
        for b in range(bb_dev):
            sums[b] = sums[b] + jnp.where(which == b, value, 0.0)
    return sums


def spread(parts, dtype, blk, bb_dev):
    count, rows, nocc = parts[0].shape

    def kernel(*refs):
        sources, targets = refs[: len(parts)], refs[len(parts) :]
        for i in range(count):
            for b, value in enumerate(placed_sum(sources, i, blk, bb_dev)):
                targets[i][b * blk : (b + 1) * blk, :] = value.astype(targets[i].dtype)

    vmem = pl.BlockSpec(memory_space=pltpu.VMEM)
    return pl.pallas_call(
        kernel,
        out_shape=[jax.ShapeDtypeStruct((bb_dev * blk, nocc), dtype)] * count,
        in_specs=[vmem] * len(parts),
        out_specs=[vmem] * count,
        compiler_params=pltpu.CompilerParams(vmem_limit_bytes=4 * 1024 * 1024),
        cost_estimate=pl.CostEstimate(
            flops=SPREAD_COST, bytes_accessed=SPREAD_COST // 1000, transcendentals=0
        ),
        name="spread",
    )(*parts)


def total_of(arrays):
    def kernel(*refs):
        value = refs[0][...].astype(jnp.float32)
        for ref in refs[1:-1]:
            value = value + ref[...].astype(jnp.float32)
        refs[-1][...] = value.astype(refs[-1].dtype)

    vmem = pl.BlockSpec(memory_space=pltpu.VMEM)
    return pl.pallas_call(
        kernel,
        out_shape=jax.ShapeDtypeStruct(arrays[0].shape, jnp.bfloat16),
        in_specs=[vmem] * len(arrays),
        out_specs=vmem,
        compiler_params=pltpu.CompilerParams(vmem_limit_bytes=4 * 1024 * 1024),
        name="total_of",
    )(*arrays)


def owner_sum(parts, blk, bb_dev):
    n_aux, rows, nocc = parts.shape

    def kernel(parts_ref, out_ref):
        sums = [jnp.zeros((blk, nocc), jnp.float32) for _ in range(bb_dev)]
        for s in range(n_aux):
            value = parts_ref[s, :blk, :].astype(jnp.float32)
            which = parts_ref[s, blk:, :][:1].astype(jnp.float32)
            for b in range(bb_dev):
                sums[b] = sums[b] + jnp.where(which == b, value, 0.0)
        for b in range(bb_dev):
            out_ref[b * blk : (b + 1) * blk, :] = sums[b].astype(out_ref.dtype)

    vmem = pl.BlockSpec(memory_space=pltpu.VMEM)
    return pl.pallas_call(
        kernel,
        out_shape=jax.ShapeDtypeStruct((bb_dev * blk, nocc), jnp.bfloat16),
        in_specs=[vmem],
        out_specs=vmem,
        name="owner_sum",
    )(parts)


def on_device(tiles, c_orbitals, basis_order, tile_block, tile_aux, live):
    blk, nocc = tiles.shape[2:]
    n_aux = lax.axis_size("aux")
    bb_dev = basis_order.shape[0] // n_aux
    direct = n_aux == DIRECT

    def swap(array, m):
        return lax.ppermute(array, "aux", [(i, i ^ m) for i in range(n_aux)])

    base = lax.axis_index("aux").astype(jnp.int32) if direct else jnp.int32(0)
    slots, nbb = tile_block.shape[0], basis_order.shape[0]
    index = lax.optimization_barrier(
        jnp.concatenate([tile_block, tile_aux, basis_order, live])
    )
    packed = pack_slots(
        index[:slots],
        index[slots : 2 * slots],
        index[2 * slots + nbb :],
        index[2 * slots : 2 * slots + nbb],
        base,
        bb_dev,
    )
    where_to, which, group, alive = unpack_slots(packed, bb_dev)
    bit = bits_of(where_to, which, alive, n_aux)
    if not direct:
        lists = chunk_lists(where_to, where_to < 0, alive, group, n_aux)
        whole = lax.all_gather(c_orbitals, "aux", axis=0, tiled=True)
        whole = whole.reshape(n_aux, bb_dev * blk, nocc)
        parts = all_in_one(n_aux, lists, bit, tiles, whole)
        moved = lax.all_to_all(parts, "aux", 0, 0, tiled=True)
        return owner_sum(moved, blk, bb_dev)

    depth = n_aux // PLANE
    side = where_to % PLANE >= 2
    last = (where_to >= 3 * PLANE) | ((where_to >= PLANE) & side)
    fit_lists = chunk_lists(where_to, last, alive, group, n_aux)
    two = swap(c_orbitals, 2 * PLANE)
    one = swap(c_orbitals, PLANE)
    beside = swap(c_orbitals, 2)
    across = swap(c_orbitals, 1)
    three = swap(c_orbitals, 3 * PLANE)
    pair = merge([one, two], [], SPREAD_COST)
    pair_beside = swap(pair, 2)
    three_beside = swap(three, 2)
    early = [pair, swap(pair, 1), across, beside, swap(beside, 1)]
    early_from = [(1, (2, None)), (2, (3, None)), (3, (4, None))]
    late_from = []
    for core in range(2):
        early_from += [(PLANE + core, (core, 0)), (2 * PLANE + core, (core, 1))]
        late_from += [
            (PLANE + 2 + core, (core, 0)),
            (2 * PLANE + 2 + core, (core, 1)),
            (3 * PLANE + core, (core, 2)),
            (3 * PLANE + 2 + core, (core, 3)),
        ]
    partial_fit, packed = begin(
        n_aux, fit_lists, bit, packed, tiles, c_orbitals, early, early_from
    )
    late = gate([pair_beside, three, three_beside], partial_fit)
    where_to, _, group, alive = unpack_slots(packed, bb_dev)
    lists = chunk_lists(where_to, where_to < PLANE, alive, group, n_aux)
    *far, fitted, _ = first_part(
        n_aux, fit_lists, lists, bit, tiles, partial_fit, [late, swap(late, 1)], late_from
    )
    far = [far[0]] + [swap(far[r], r) for r in range(1, PLANE)]
    near = second_part(n_aux, lists, bit, tiles, fitted, far[1])
    near = [near[0]] + [swap(near[r], r) for r in range(1, PLANE)]
    far = spread(far, jnp.bfloat16, blk, bb_dev)
    far = [swap(far[dz - 1], dz * PLANE) for dz in range(depth - 1, 0, -1)]
    near = spread(near, jnp.float32, blk, bb_dev)
    return total_of(list(near) + far)


def solution(mesh):
    return jax.shard_map(
        on_device,
        mesh=mesh,
        in_specs=(
            P(("grp", "aux"), None, None, None),
            P(("grp", "aux"), None),
            P("grp"),
            P(("grp", "aux")),
            P(("grp", "aux")),
            P(("grp", "aux")),
        ),
        out_specs=P(("grp", "aux"), None),
        check_vma=False,
    )
```

```python
import functools

import jax
import jax.numpy as jnp
from jax import lax
from jax.experimental import pallas as pl
from jax.experimental.pallas import tpu as pltpu
from jax.sharding import PartitionSpec as P

AB_DEV = 8
CHUNK = 2
TURNS = (8, 2, 1)
TAIL = 16
PLANE = 4
SPREAD_COST = 10**10
DIRECT = 16


def pack_slots(tile_block, tile_aux, live, basis_order, base, bb_dev):
    nbb = basis_order.shape[0]
    position = jnp.sum(
        jnp.where(
            basis_order[None, :] == tile_block[:, None], lax.iota(jnp.int32, nbb)[None, :], 0
        ),
        axis=1,
    )
    owner = jnp.bitwise_xor(position // bb_dev, base)
    alive = (lax.iota(jnp.int32, tile_block.shape[0]) < live[0]).astype(jnp.int32)
    return ((owner * bb_dev + position % bb_dev) * AB_DEV + tile_aux) * 2 + alive


def unpack_slots(packed, bb_dev):
    rest = packed // 2
    tile_aux = rest % AB_DEV
    rest = rest // AB_DEV
    return rest // bb_dev, rest % bb_dev, tile_aux, packed % 2 == 1


def chunk_lists(where_to, later, alive, tile_aux, n_aux):
    slots = where_to.shape[0]
    keys = 2 * AB_DEV
    chunks = slots // CHUNK + keys
    t = lax.iota(jnp.int32, slots)
    group = jnp.where(alive, tile_aux + jnp.where(later, AB_DEV, 0), keys)
    ids = lax.iota(jnp.int32, keys)
    counts = jnp.sum((group[None, :] == ids[:, None]).astype(jnp.int32), axis=1)
    need = (counts + CHUNK - 1) // CHUNK
    ends = jnp.sum(jnp.where(ids[None, :] <= ids[:, None], need[None, :], 0), axis=1)
    rank = jnp.sum(
        ((group[None, :] == group[:, None]) & (t[None, :] < t[:, None])).astype(jnp.int32), axis=1
    )
    start = jnp.sum(jnp.where(group[:, None] > ids[None, :], need[None, :], 0), axis=1)
    place = jnp.where(alive, start * CHUNK + rank, -1)
    q = lax.iota(jnp.int32, chunks * CHUNK)
    hit = place[None, :] == q[:, None]
    lead = place[None, :] == (q // CHUNK * CHUNK)[:, None]
    valid = jnp.any(hit, axis=1)
    slot = jnp.sum(jnp.where(hit, t[None, :], 0), axis=1)
    slot = jnp.where(valid, slot, jnp.sum(jnp.where(lead, t[None, :], 0), axis=1))
    block = jnp.where(valid, jnp.sum(jnp.where(hit, where_to[None, :], 0), axis=1), n_aux)
    gid = jnp.sum(
        (lax.iota(jnp.int32, chunks)[:, None] >= ends[None, :]).astype(jnp.int32), axis=1
    )
    return slot, block, jnp.concatenate([gid % AB_DEV, ends])


def bits_of(where_to, which, alive, n_aux):
    return jnp.max(
        jnp.where(
            (where_to[None, :] == lax.iota(jnp.int32, n_aux)[:, None]) & alive[None, :],
            which[None, :],
            0,
        ),
        axis=1,
    )


def slab(tiles, slot):
    return jnp.concatenate([tiles[slot, p] for p in range(tiles.shape[1])], axis=1)


def chunk_ends(gid_ref, slots):
    chunks = slots // CHUNK + 2 * AB_DEV
    return gid_ref[chunks + AB_DEV - 1], gid_ref[chunks + 2 * AB_DEV - 1]


def turn(ct, bit_ref, m, source):
    blk = ct.shape[2]
    row = pl.multiple_of(bit_ref[m] * blk, blk)
    ct[m] = source[pl.ds(row, blk), :].T


def sweep(low, high, body):
    for size in TURNS:
        whole = (high - low) // size

        @pl.loop(0, whole)
        def _(step, low=low, size=size):
            body([low + step * size + u for u in range(size)])

        low = low + whole * size


def fit(lists, tiles, ct, zacc, low, high):
    slot_ref, block_ref, gid_ref = lists

    def body(group):
        for chunk in group:
            spots = [chunk * CHUNK + i for i in range(CHUNK)]
            left = jnp.concatenate([ct[block_ref[pos]] for pos in spots], axis=1)
            right = jnp.concatenate([slab(tiles, slot_ref[pos]) for pos in spots], axis=0)
            zacc[gid_ref[chunk]] += jnp.dot(left, right, preferred_element_type=jnp.float32)

    sweep(low, high, body)


def apply_fitted(lists, tiles, zb, acc, low, high):
    slot_ref, block_ref, gid_ref = lists
    blk = acc.shape[1]

    def body(group):
        for chunk in group:
            spots = [chunk * CHUNK + i for i in range(CHUNK)]
            left = jnp.concatenate([slab(tiles, slot_ref[pos]) for pos in spots], axis=0)
            value = lax.dot_general(
                left,
                zb[gid_ref[chunk]],
                (((1,), (1,)), ((), ())),
                preferred_element_type=jnp.float32,
            )
            for i, pos in enumerate(spots):
                acc[block_ref[pos]] += value[i * blk : (i + 1) * blk]

    sweep(low, high, body)


def begin(n_aux, lists, bit, packed, tiles_array, own_array, shards, sources):
    slots, auxb, blk, nocc = tiles_array.shape
    n_in = len(shards)

    def kernel(slot_ref, block_ref, gid_ref, bit_ref, packed_ref, tiles, own, *refs):
        c_refs, (zacc, passed, ct) = refs[:n_in], refs[n_in:]
        passed[...] = packed_ref[...]
        zacc[...] = jnp.zeros(zacc.shape, zacc.dtype)
        ct[n_aux] = jnp.zeros((nocc, blk), ct.dtype)
        turn(ct, bit_ref, 0, own)
        for m, (ref, i) in sources:
            turn(ct, bit_ref, m, c_refs[ref] if i is None else c_refs[ref].at[i])
        early, _ = chunk_ends(gid_ref, slots)
        fit((slot_ref, block_ref, gid_ref), tiles, ct, zacc, 0, early)

    smem = pl.BlockSpec(memory_space=pltpu.SMEM)
    vmem = pl.BlockSpec(memory_space=pltpu.VMEM)
    return pl.pallas_call(
        kernel,
        out_shape=[
            jax.ShapeDtypeStruct((AB_DEV, nocc, auxb * nocc), jnp.float32),
            jax.ShapeDtypeStruct(packed.shape, packed.dtype),
        ],
        in_specs=[smem] * 4 + [vmem] * (3 + n_in),
        out_specs=[vmem] * 2,
        scratch_shapes=[pltpu.VMEM((n_aux + 1, nocc, blk), jnp.bfloat16)],
        compiler_params=pltpu.CompilerParams(vmem_limit_bytes=20 * 1024 * 1024),
        cost_estimate=pl.CostEstimate(
            flops=2 * tiles_array.size * nocc, bytes_accessed=tiles_array.size, transcendentals=0
        ),
        name="begin",
    )(*lists, bit, packed, tiles_array, own_array, *shards)


def put(bit_ref, acc, m, out_ref, place):
    blk, nocc = acc.shape[1:]
    out_ref[place, :blk, :] = acc[m].astype(out_ref.dtype)
    out_ref[place, blk:, :] = jnp.full((TAIL, nocc), bit_ref[m], jnp.int32).astype(
        jnp.float32
    ).astype(out_ref.dtype)


def clear(n_aux, ct, acc):
    ct[n_aux] = jnp.zeros(ct.shape[1:], ct.dtype)
    acc[...] = jnp.zeros(acc.shape, acc.dtype)


def round_fitted(zacc, zb):
    for g in range(zacc.shape[0]):
        zb[g] = zacc[g].astype(zb.dtype)


def first_part(n_aux, fit_lists, lists, bit, tiles_array, partial_fit, shards, sources):
    slots, auxb, blk, nocc = tiles_array.shape
    n_in = len(shards)

    def kernel(*refs):
        fit_refs, refs = refs[:3], refs[3:]
        list_refs, bit_ref, tiles = refs[:3], refs[3], refs[4]
        c_refs, out_refs = refs[6 : 6 + n_in], refs[6 + n_in : -4]
        zb, zacc, ct, acc = refs[-4:]
        clear(n_aux, ct, acc)
        for m, (ref, i) in sources:
            turn(ct, bit_ref, m, c_refs[ref] if i is None else c_refs[ref].at[i])
        fit(fit_refs, tiles, ct, zacc, *chunk_ends(fit_refs[2], slots))
        round_fitted(zacc, zb)
        far, _ = chunk_ends(list_refs[2], slots)
        apply_fitted(list_refs, tiles, zb, acc, 0, far)
        for m in range(PLANE, n_aux):
            put(bit_ref, acc, m, out_refs[m % PLANE], m // PLANE - 1)

    smem = pl.BlockSpec(memory_space=pltpu.SMEM)
    vmem = pl.BlockSpec(memory_space=pltpu.VMEM)
    shape = (n_aux // PLANE - 1, blk + TAIL, nocc)
    out_shape = [jax.ShapeDtypeStruct(shape, jnp.bfloat16)] * PLANE
    out_shape = out_shape + [
        jax.ShapeDtypeStruct((AB_DEV, nocc, auxb * nocc), jnp.bfloat16),
        jax.ShapeDtypeStruct(partial_fit.shape, partial_fit.dtype),
    ]
    return pl.pallas_call(
        kernel,
        out_shape=out_shape,
        in_specs=[smem] * 7 + [vmem] * (2 + n_in),
        out_specs=[vmem] * len(out_shape),
        scratch_shapes=[
            pltpu.VMEM((n_aux + 1, nocc, blk), jnp.bfloat16),
            pltpu.VMEM((n_aux + 1, blk, nocc), jnp.float32),
        ],
        input_output_aliases={8: PLANE + 1},
        compiler_params=pltpu.CompilerParams(vmem_limit_bytes=20 * 1024 * 1024),
        cost_estimate=pl.CostEstimate(
            flops=3 * tiles_array.size * nocc, bytes_accessed=tiles_array.size, transcendentals=0
        ),
        name="first_part",
    )(*fit_lists, *lists, bit, tiles_array, partial_fit, *shards)


def second_part(n_aux, lists, bit, tiles_array, fitted, after):
    slots, auxb, blk, nocc = tiles_array.shape

    def kernel(slot_ref, block_ref, gid_ref, bit_ref, tiles, zb, _, *refs):
        out_refs, acc = refs[:-1], refs[-1]
        acc[...] = jnp.zeros(acc.shape, acc.dtype)
        apply_fitted(
            (slot_ref, block_ref, gid_ref), tiles, zb, acc, *chunk_ends(gid_ref, slots)
        )
        for m in range(PLANE):
            put(bit_ref, acc, m, out_refs[m], 0)

    smem = pl.BlockSpec(memory_space=pltpu.SMEM)
    vmem = pl.BlockSpec(memory_space=pltpu.VMEM)
    shape = (1, blk + TAIL, nocc)
    return pl.pallas_call(
        kernel,
        out_shape=[jax.ShapeDtypeStruct(shape, jnp.bfloat16)] * PLANE,
        in_specs=[smem] * 4 + [vmem, vmem, pl.BlockSpec(memory_space=pl.ANY)],
        out_specs=[vmem] * PLANE,
        scratch_shapes=[pltpu.VMEM((n_aux + 1, blk, nocc), jnp.float32)],
        compiler_params=pltpu.CompilerParams(vmem_limit_bytes=20 * 1024 * 1024),
        cost_estimate=pl.CostEstimate(
            flops=10**10, bytes_accessed=tiles_array.size, transcendentals=0
        ),
        name="second_part",
    )(*lists, bit, tiles_array, fitted, after)


def all_in_one(n_aux, lists, bit, tiles_array, whole):
    slots, auxb, blk, nocc = tiles_array.shape

    def kernel(slot_ref, block_ref, gid_ref, bit_ref, tiles, c_ref, out_ref, ct, zacc, zb, acc):
        lists = (slot_ref, block_ref, gid_ref)
        clear(n_aux, ct, acc)
        zacc[...] = jnp.zeros(zacc.shape, zacc.dtype)

        @pl.loop(0, n_aux)
        def _(m):
            turn(ct, bit_ref, m, c_ref.at[m])

        _, total = chunk_ends(gid_ref, slots)
        fit(lists, tiles, ct, zacc, 0, total)
        round_fitted(zacc, zb)
        apply_fitted(lists, tiles, zb, acc, 0, total)

        @pl.loop(0, n_aux)
        def _(m):
            put(bit_ref, acc, m, out_ref, m)

    smem = pl.BlockSpec(memory_space=pltpu.SMEM)
    vmem = pl.BlockSpec(memory_space=pltpu.VMEM)
    return pl.pallas_call(
        kernel,
        out_shape=jax.ShapeDtypeStruct((n_aux, blk + TAIL, nocc), jnp.bfloat16),
        in_specs=[smem] * 4 + [vmem] * 2,
        out_specs=vmem,
        scratch_shapes=[
            pltpu.VMEM((n_aux + 1, nocc, blk), jnp.bfloat16),
            pltpu.VMEM((AB_DEV, nocc, auxb * nocc), jnp.float32),
            pltpu.VMEM((AB_DEV, nocc, auxb * nocc), jnp.bfloat16),
            pltpu.VMEM((n_aux + 1, blk, nocc), jnp.float32),
        ],
        compiler_params=pltpu.CompilerParams(vmem_limit_bytes=46 * 1024 * 1024),
        name="all_in_one",
    )(*lists, bit, tiles_array, whole)


def gate(arrays, after):
    counts = [array.shape[0] if array.ndim == 3 else 1 for array in arrays]

    def kernel(*refs):
        target, place = refs[-1], 0
        for ref, count in zip(refs, counts):
            value = ref[...]
            target[place : place + count] = value.reshape((count,) + value.shape[-2:])
            place += count

    vmem = pl.BlockSpec(memory_space=pltpu.VMEM)
    return pl.pallas_call(
        kernel,
        out_shape=jax.ShapeDtypeStruct((sum(counts),) + arrays[0].shape[-2:], arrays[0].dtype),
        in_specs=[vmem] * len(arrays) + [pl.BlockSpec(memory_space=pl.ANY)],
        out_specs=vmem,
        compiler_params=pltpu.CompilerParams(vmem_limit_bytes=4 * 1024 * 1024),
        name="gate",
    )(*arrays, after)


def merge(arrays, after, cost):
    def kernel(*refs):
        for i, ref in enumerate(refs[: len(arrays)]):
            refs[-1][i] = ref[...]

    vmem = pl.BlockSpec(memory_space=pltpu.VMEM)
    return pl.pallas_call(
        kernel,
        out_shape=jax.ShapeDtypeStruct((len(arrays),) + arrays[0].shape, arrays[0].dtype),
        in_specs=[vmem] * len(arrays) + [pl.BlockSpec(memory_space=pl.ANY)] * len(after),
        out_specs=vmem,
        compiler_params=pltpu.CompilerParams(vmem_limit_bytes=4 * 1024 * 1024),
        cost_estimate=pl.CostEstimate(flops=cost, bytes_accessed=cost // 1000, transcendentals=0),
        name="merge",
    )(*arrays, *after)


def placed_sum(sources, i, blk, bb_dev):
    nocc = sources[0].shape[2]
    sums = [jnp.zeros((blk, nocc), jnp.float32) for _ in range(bb_dev)]
    for source in sources:
        value = source[i, :blk, :].astype(jnp.float32)
        which = source[i, blk:, :][:1].astype(jnp.float32)
        for b in range(bb_dev):
            sums[b] = sums[b] + jnp.where(which == b, value, 0.0)
    return sums


def spread(parts, dtype, blk, bb_dev):
    count, rows, nocc = parts[0].shape

    def kernel(*refs):
        sources, targets = refs[: len(parts)], refs[len(parts) :]
        for i in range(count):
            for b, value in enumerate(placed_sum(sources, i, blk, bb_dev)):
                targets[i][b * blk : (b + 1) * blk, :] = value.astype(targets[i].dtype)

    vmem = pl.BlockSpec(memory_space=pltpu.VMEM)
    return pl.pallas_call(
        kernel,
        out_shape=[jax.ShapeDtypeStruct((bb_dev * blk, nocc), dtype)] * count,
        in_specs=[vmem] * len(parts),
        out_specs=[vmem] * count,
        compiler_params=pltpu.CompilerParams(vmem_limit_bytes=4 * 1024 * 1024),
        cost_estimate=pl.CostEstimate(
            flops=SPREAD_COST, bytes_accessed=SPREAD_COST // 1000, transcendentals=0
        ),
        name="spread",
    )(*parts)


def total_of(arrays):
    def kernel(*refs):
        value = refs[0][...].astype(jnp.float32)
        for ref in refs[1:-1]:
            value = value + ref[...].astype(jnp.float32)
        refs[-1][...] = value.astype(refs[-1].dtype)

    vmem = pl.BlockSpec(memory_space=pltpu.VMEM)
    return pl.pallas_call(
        kernel,
        out_shape=jax.ShapeDtypeStruct(arrays[0].shape, jnp.bfloat16),
        in_specs=[vmem] * len(arrays),
        out_specs=vmem,
        compiler_params=pltpu.CompilerParams(vmem_limit_bytes=4 * 1024 * 1024),
        name="total_of",
    )(*arrays)


def owner_sum(parts, blk, bb_dev):
    n_aux, rows, nocc = parts.shape

    def kernel(parts_ref, out_ref):
        sums = [jnp.zeros((blk, nocc), jnp.float32) for _ in range(bb_dev)]
        for s in range(n_aux):
            value = parts_ref[s, :blk, :].astype(jnp.float32)
            which = parts_ref[s, blk:, :][:1].astype(jnp.float32)
            for b in range(bb_dev):
                sums[b] = sums[b] + jnp.where(which == b, value, 0.0)
        for b in range(bb_dev):
            out_ref[b * blk : (b + 1) * blk, :] = sums[b].astype(out_ref.dtype)

    vmem = pl.BlockSpec(memory_space=pltpu.VMEM)
    return pl.pallas_call(
        kernel,
        out_shape=jax.ShapeDtypeStruct((bb_dev * blk, nocc), jnp.bfloat16),
        in_specs=[vmem],
        out_specs=vmem,
        name="owner_sum",
    )(parts)


def on_device(tiles, c_orbitals, basis_order, tile_block, tile_aux, live):
    blk, nocc = tiles.shape[2:]
    n_aux = lax.axis_size("aux")
    bb_dev = basis_order.shape[0] // n_aux
    direct = n_aux == DIRECT

    def swap(array, m):
        return lax.ppermute(array, "aux", [(i, i ^ m) for i in range(n_aux)])

    base = lax.axis_index("aux").astype(jnp.int32) if direct else jnp.int32(0)
    packed = pack_slots(tile_block, tile_aux, live, basis_order, base, bb_dev)
    where_to, which, group, alive = unpack_slots(packed, bb_dev)
    bit = bits_of(where_to, which, alive, n_aux)
    if not direct:
        lists = chunk_lists(where_to, where_to < 0, alive, group, n_aux)
        whole = lax.all_gather(c_orbitals, "aux", axis=0, tiled=True)
        whole = whole.reshape(n_aux, bb_dev * blk, nocc)
        parts = all_in_one(n_aux, lists, bit, tiles, whole)
        moved = lax.all_to_all(parts, "aux", 0, 0, tiled=True)
        return owner_sum(moved, blk, bb_dev)

    depth = n_aux // PLANE
    side = where_to % PLANE >= 2
    last = (where_to >= 3 * PLANE) | ((where_to >= PLANE) & side)
    fit_lists = chunk_lists(where_to, last, alive, group, n_aux)
    two = swap(c_orbitals, 2 * PLANE)
    one = swap(c_orbitals, PLANE)
    beside = swap(c_orbitals, 2)
    across = swap(c_orbitals, 1)
    three = swap(c_orbitals, 3 * PLANE)
    pair = merge([one, two], [], SPREAD_COST)
    pair_beside = swap(pair, 2)
    three_beside = swap(three, 2)
    early = [pair, swap(pair, 1), across, beside, swap(beside, 1)]
    early_from = [(1, (2, None)), (2, (3, None)), (3, (4, None))]
    late_from = []
    for core in range(2):
        early_from += [(PLANE + core, (core, 0)), (2 * PLANE + core, (core, 1))]
        late_from += [
            (PLANE + 2 + core, (core, 0)),
            (2 * PLANE + 2 + core, (core, 1)),
            (3 * PLANE + core, (core, 2)),
            (3 * PLANE + 2 + core, (core, 3)),
        ]
    partial_fit, packed = begin(
        n_aux, fit_lists, bit, packed, tiles, c_orbitals, early, early_from
    )
    late = gate([pair_beside, three, three_beside], partial_fit)
    where_to, _, group, alive = unpack_slots(packed, bb_dev)
    lists = chunk_lists(where_to, where_to < PLANE, alive, group, n_aux)
    *far, fitted, _ = first_part(
        n_aux, fit_lists, lists, bit, tiles, partial_fit, [late, swap(late, 1)], late_from
    )
    far = [far[0]] + [swap(far[r], r) for r in range(1, PLANE)]
    near = second_part(n_aux, lists, bit, tiles, fitted, far[1])
    near = [near[0]] + [swap(near[r], r) for r in range(1, PLANE)]
    far = spread(far, jnp.bfloat16, blk, bb_dev)
    far = [swap(far[dz - 1], dz * PLANE) for dz in range(depth - 1, 0, -1)]
    near = spread(near, jnp.float32, blk, bb_dev)
    return total_of(list(near) + far)


def solution(mesh):
    return jax.shard_map(
        on_device,
        mesh=mesh,
        in_specs=(
            P(("grp", "aux"), None, None, None),
            P(("grp", "aux"), None),
            P("grp"),
            P(("grp", "aux")),
            P(("grp", "aux")),
            P(("grp", "aux")),
        ),
        out_specs=P(("grp", "aux"), None),
        check_vma=False,
    )
```

```python
import functools

import jax
import jax.numpy as jnp
from jax import lax
from jax.experimental import pallas as pl
from jax.experimental.pallas import tpu as pltpu
from jax.sharding import PartitionSpec as P

AB_DEV = 8
CHUNK = 2
TURNS = (8, 2, 1)
TAIL = 16
PLANE = 4
SPREAD_COST = 10**10
DIRECT = 16


def pack_slots(tile_block, tile_aux, live, basis_order, base, bb_dev):
    slots, nbb = tile_block.shape[0], basis_order.shape[0]
    k = lax.iota(jnp.int32, nbb)
    owner = jnp.bitwise_xor(k // bb_dev, base)
    value = (owner * bb_dev + k % bb_dev)[None, :] * AB_DEV + tile_aux[:, None]
    value = jnp.where(basis_order[None, :] == tile_block[:, None], value * 2, 0)
    alive = jnp.pad(live, (0, nbb - 1))[None, :] > lax.iota(jnp.int32, slots)[:, None]
    return jnp.sum(value + alive.astype(jnp.int32), axis=1)


def unpack_slots(packed, bb_dev):
    rest = packed // 2
    tile_aux = rest % AB_DEV
    rest = rest // AB_DEV
    return rest // bb_dev, rest % bb_dev, tile_aux, packed % 2 == 1


def chunk_lists(where_to, later, alive, tile_aux, n_aux):
    slots = where_to.shape[0]
    keys = 2 * AB_DEV
    chunks = slots // CHUNK + keys
    t = lax.iota(jnp.int32, slots)
    group = jnp.where(alive, tile_aux + jnp.where(later, AB_DEV, 0), keys)
    ids = lax.iota(jnp.int32, keys)
    counts = jnp.sum((group[None, :] == ids[:, None]).astype(jnp.int32), axis=1)
    need = (counts + CHUNK - 1) // CHUNK
    ends = jnp.sum(jnp.where(ids[None, :] <= ids[:, None], need[None, :], 0), axis=1)
    rank = jnp.sum(
        ((group[None, :] == group[:, None]) & (t[None, :] < t[:, None])).astype(jnp.int32), axis=1
    )
    start = jnp.sum(jnp.where(group[:, None] > ids[None, :], need[None, :], 0), axis=1)
    place = jnp.where(alive, start * CHUNK + rank, -1)
    q = lax.iota(jnp.int32, chunks * CHUNK)
    hit = place[None, :] == q[:, None]
    lead = place[None, :] == (q // CHUNK * CHUNK)[:, None]
    valid = jnp.any(hit, axis=1)
    slot = jnp.sum(jnp.where(hit, t[None, :], 0), axis=1)
    slot = jnp.where(valid, slot, jnp.sum(jnp.where(lead, t[None, :], 0), axis=1))
    block = jnp.where(valid, jnp.sum(jnp.where(hit, where_to[None, :], 0), axis=1), n_aux)
    gid = jnp.sum(
        (lax.iota(jnp.int32, chunks)[:, None] >= ends[None, :]).astype(jnp.int32), axis=1
    )
    return slot, block, jnp.concatenate([gid % AB_DEV, ends])


def bits_of(where_to, which, alive, n_aux):
    return jnp.max(
        jnp.where(
            (where_to[None, :] == lax.iota(jnp.int32, n_aux)[:, None]) & alive[None, :],
            which[None, :],
            0,
        ),
        axis=1,
    )


def slab(tiles, slot):
    return jnp.concatenate([tiles[slot, p] for p in range(tiles.shape[1])], axis=1)


def chunk_ends(gid_ref, slots):
    chunks = slots // CHUNK + 2 * AB_DEV
    return gid_ref[chunks + AB_DEV - 1], gid_ref[chunks + 2 * AB_DEV - 1]


def turn(ct, bit_ref, m, source):
    blk = ct.shape[2]
    row = pl.multiple_of(bit_ref[m] * blk, blk)
    ct[m] = source[pl.ds(row, blk), :].T


def sweep(low, high, body):
    for size in TURNS:
        whole = (high - low) // size

        @pl.loop(0, whole)
        def _(step, low=low, size=size):
            body([low + step * size + u for u in range(size)])

        low = low + whole * size


def fit(lists, tiles, ct, zacc, low, high):
    slot_ref, block_ref, gid_ref = lists

    def body(group):
        for chunk in group:
            spots = [chunk * CHUNK + i for i in range(CHUNK)]
            left = jnp.concatenate([ct[block_ref[pos]] for pos in spots], axis=1)
            right = jnp.concatenate([slab(tiles, slot_ref[pos]) for pos in spots], axis=0)
            zacc[gid_ref[chunk]] += jnp.dot(left, right, preferred_element_type=jnp.float32)

    sweep(low, high, body)


def apply_fitted(lists, tiles, zb, acc, low, high):
    slot_ref, block_ref, gid_ref = lists
    blk = acc.shape[1]

    def body(group):
        for chunk in group:
            spots = [chunk * CHUNK + i for i in range(CHUNK)]
            left = jnp.concatenate([slab(tiles, slot_ref[pos]) for pos in spots], axis=0)
            value = lax.dot_general(
                left,
                zb[gid_ref[chunk]],
                (((1,), (1,)), ((), ())),
                preferred_element_type=jnp.float32,
            )
            for i, pos in enumerate(spots):
                acc[block_ref[pos]] += value[i * blk : (i + 1) * blk]

    sweep(low, high, body)


def begin(n_aux, lists, bit, packed, tiles_array, own_array, shards, sources):
    slots, auxb, blk, nocc = tiles_array.shape
    n_in = len(shards)

    def kernel(slot_ref, block_ref, gid_ref, bit_ref, packed_ref, tiles, own, *refs):
        c_refs, (zacc, passed, ct) = refs[:n_in], refs[n_in:]
        passed[...] = packed_ref[...]
        zacc[...] = jnp.zeros(zacc.shape, zacc.dtype)
        ct[n_aux] = jnp.zeros((nocc, blk), ct.dtype)
        turn(ct, bit_ref, 0, own)
        for m, (ref, i) in sources:
            turn(ct, bit_ref, m, c_refs[ref] if i is None else c_refs[ref].at[i])
        early, _ = chunk_ends(gid_ref, slots)
        fit((slot_ref, block_ref, gid_ref), tiles, ct, zacc, 0, early)

    smem = pl.BlockSpec(memory_space=pltpu.SMEM)
    vmem = pl.BlockSpec(memory_space=pltpu.VMEM)
    return pl.pallas_call(
        kernel,
        out_shape=[
            jax.ShapeDtypeStruct((AB_DEV, nocc, auxb * nocc), jnp.float32),
            jax.ShapeDtypeStruct(packed.shape, packed.dtype),
        ],
        in_specs=[smem] * 4 + [vmem] * (3 + n_in),
        out_specs=[vmem] * 2,
        scratch_shapes=[pltpu.VMEM((n_aux + 1, nocc, blk), jnp.bfloat16)],
        compiler_params=pltpu.CompilerParams(vmem_limit_bytes=20 * 1024 * 1024),
        cost_estimate=pl.CostEstimate(
            flops=2 * tiles_array.size * nocc, bytes_accessed=tiles_array.size, transcendentals=0
        ),
        name="begin",
    )(*lists, bit, packed, tiles_array, own_array, *shards)


def put(bit_ref, acc, m, out_ref, place):
    blk, nocc = acc.shape[1:]
    out_ref[place, :blk, :] = acc[m].astype(out_ref.dtype)
    out_ref[place, blk:, :] = jnp.full((TAIL, nocc), bit_ref[m], jnp.int32).astype(
        jnp.float32
    ).astype(out_ref.dtype)


def clear(n_aux, ct, acc):
    ct[n_aux] = jnp.zeros(ct.shape[1:], ct.dtype)
    acc[...] = jnp.zeros(acc.shape, acc.dtype)


def round_fitted(zacc, zb):
    for g in range(zacc.shape[0]):
        zb[g] = zacc[g].astype(zb.dtype)


def first_part(n_aux, fit_lists, lists, bit, tiles_array, partial_fit, shards, sources):
    slots, auxb, blk, nocc = tiles_array.shape
    n_in = len(shards)

    def kernel(*refs):
        fit_refs, refs = refs[:3], refs[3:]
        list_refs, bit_ref, tiles = refs[:3], refs[3], refs[4]
        c_refs, out_refs = refs[6 : 6 + n_in], refs[6 + n_in : -4]
        zb, zacc, ct, acc = refs[-4:]
        clear(n_aux, ct, acc)
        for m, (ref, i) in sources:
            turn(ct, bit_ref, m, c_refs[ref] if i is None else c_refs[ref].at[i])
        fit(fit_refs, tiles, ct, zacc, *chunk_ends(fit_refs[2], slots))
        round_fitted(zacc, zb)
        far, _ = chunk_ends(list_refs[2], slots)
        apply_fitted(list_refs, tiles, zb, acc, 0, far)
        for m in range(PLANE, n_aux):
            put(bit_ref, acc, m, out_refs[m % PLANE], m // PLANE - 1)

    smem = pl.BlockSpec(memory_space=pltpu.SMEM)
    vmem = pl.BlockSpec(memory_space=pltpu.VMEM)
    shape = (n_aux // PLANE - 1, blk + TAIL, nocc)
    out_shape = [jax.ShapeDtypeStruct(shape, jnp.bfloat16)] * PLANE
    out_shape = out_shape + [
        jax.ShapeDtypeStruct((AB_DEV, nocc, auxb * nocc), jnp.bfloat16),
        jax.ShapeDtypeStruct(partial_fit.shape, partial_fit.dtype),
    ]
    return pl.pallas_call(
        kernel,
        out_shape=out_shape,
        in_specs=[smem] * 7 + [vmem] * (2 + n_in),
        out_specs=[vmem] * len(out_shape),
        scratch_shapes=[
            pltpu.VMEM((n_aux + 1, nocc, blk), jnp.bfloat16),
            pltpu.VMEM((n_aux + 1, blk, nocc), jnp.float32),
        ],
        input_output_aliases={8: PLANE + 1},
        compiler_params=pltpu.CompilerParams(vmem_limit_bytes=20 * 1024 * 1024),
        cost_estimate=pl.CostEstimate(
            flops=3 * tiles_array.size * nocc, bytes_accessed=tiles_array.size, transcendentals=0
        ),
        name="first_part",
    )(*fit_lists, *lists, bit, tiles_array, partial_fit, *shards)


def second_part(n_aux, lists, bit, tiles_array, fitted, after):
    slots, auxb, blk, nocc = tiles_array.shape

    def kernel(slot_ref, block_ref, gid_ref, bit_ref, tiles, zb, _, *refs):
        out_refs, acc = refs[:-1], refs[-1]
        acc[...] = jnp.zeros(acc.shape, acc.dtype)
        apply_fitted(
            (slot_ref, block_ref, gid_ref), tiles, zb, acc, *chunk_ends(gid_ref, slots)
        )
        for m in range(PLANE):
            put(bit_ref, acc, m, out_refs[m], 0)

    smem = pl.BlockSpec(memory_space=pltpu.SMEM)
    vmem = pl.BlockSpec(memory_space=pltpu.VMEM)
    shape = (1, blk + TAIL, nocc)
    return pl.pallas_call(
        kernel,
        out_shape=[jax.ShapeDtypeStruct(shape, jnp.bfloat16)] * PLANE,
        in_specs=[smem] * 4 + [vmem, vmem, pl.BlockSpec(memory_space=pl.ANY)],
        out_specs=[vmem] * PLANE,
        scratch_shapes=[pltpu.VMEM((n_aux + 1, blk, nocc), jnp.float32)],
        compiler_params=pltpu.CompilerParams(vmem_limit_bytes=20 * 1024 * 1024),
        cost_estimate=pl.CostEstimate(
            flops=10**10, bytes_accessed=tiles_array.size, transcendentals=0
        ),
        name="second_part",
    )(*lists, bit, tiles_array, fitted, after)


def all_in_one(n_aux, lists, bit, tiles_array, whole):
    slots, auxb, blk, nocc = tiles_array.shape

    def kernel(slot_ref, block_ref, gid_ref, bit_ref, tiles, c_ref, out_ref, ct, zacc, zb, acc):
        lists = (slot_ref, block_ref, gid_ref)
        clear(n_aux, ct, acc)
        zacc[...] = jnp.zeros(zacc.shape, zacc.dtype)

        @pl.loop(0, n_aux)
        def _(m):
            turn(ct, bit_ref, m, c_ref.at[m])

        _, total = chunk_ends(gid_ref, slots)
        fit(lists, tiles, ct, zacc, 0, total)
        round_fitted(zacc, zb)
        apply_fitted(lists, tiles, zb, acc, 0, total)

        @pl.loop(0, n_aux)
        def _(m):
            put(bit_ref, acc, m, out_ref, m)

    smem = pl.BlockSpec(memory_space=pltpu.SMEM)
    vmem = pl.BlockSpec(memory_space=pltpu.VMEM)
    return pl.pallas_call(
        kernel,
        out_shape=jax.ShapeDtypeStruct((n_aux, blk + TAIL, nocc), jnp.bfloat16),
        in_specs=[smem] * 4 + [vmem] * 2,
        out_specs=vmem,
        scratch_shapes=[
            pltpu.VMEM((n_aux + 1, nocc, blk), jnp.bfloat16),
            pltpu.VMEM((AB_DEV, nocc, auxb * nocc), jnp.float32),
            pltpu.VMEM((AB_DEV, nocc, auxb * nocc), jnp.bfloat16),
            pltpu.VMEM((n_aux + 1, blk, nocc), jnp.float32),
        ],
        compiler_params=pltpu.CompilerParams(vmem_limit_bytes=46 * 1024 * 1024),
        name="all_in_one",
    )(*lists, bit, tiles_array, whole)


def gate(arrays, after):
    counts = [array.shape[0] if array.ndim == 3 else 1 for array in arrays]

    def kernel(*refs):
        target, place = refs[-1], 0
        for ref, count in zip(refs, counts):
            value = ref[...]
            target[place : place + count] = value.reshape((count,) + value.shape[-2:])
            place += count

    vmem = pl.BlockSpec(memory_space=pltpu.VMEM)
    return pl.pallas_call(
        kernel,
        out_shape=jax.ShapeDtypeStruct((sum(counts),) + arrays[0].shape[-2:], arrays[0].dtype),
        in_specs=[vmem] * len(arrays) + [pl.BlockSpec(memory_space=pl.ANY)],
        out_specs=vmem,
        compiler_params=pltpu.CompilerParams(vmem_limit_bytes=4 * 1024 * 1024),
        name="gate",
    )(*arrays, after)


def merge(arrays, after, cost):
    def kernel(*refs):
        for i, ref in enumerate(refs[: len(arrays)]):
            refs[-1][i] = ref[...]

    vmem = pl.BlockSpec(memory_space=pltpu.VMEM)
    return pl.pallas_call(
        kernel,
        out_shape=jax.ShapeDtypeStruct((len(arrays),) + arrays[0].shape, arrays[0].dtype),
        in_specs=[vmem] * len(arrays) + [pl.BlockSpec(memory_space=pl.ANY)] * len(after),
        out_specs=vmem,
        compiler_params=pltpu.CompilerParams(vmem_limit_bytes=4 * 1024 * 1024),
        cost_estimate=pl.CostEstimate(flops=cost, bytes_accessed=cost // 1000, transcendentals=0),
        name="merge",
    )(*arrays, *after)


def placed_sum(sources, i, blk, bb_dev):
    nocc = sources[0].shape[2]
    sums = [jnp.zeros((blk, nocc), jnp.float32) for _ in range(bb_dev)]
    for source in sources:
        value = source[i, :blk, :].astype(jnp.float32)
        which = source[i, blk:, :][:1].astype(jnp.float32)
        for b in range(bb_dev):
            sums[b] = sums[b] + jnp.where(which == b, value, 0.0)
    return sums


def spread(parts, dtype, blk, bb_dev):
    count, rows, nocc = parts[0].shape

    def kernel(*refs):
        sources, targets = refs[: len(parts)], refs[len(parts) :]
        for i in range(count):
            for b, value in enumerate(placed_sum(sources, i, blk, bb_dev)):
                targets[i][b * blk : (b + 1) * blk, :] = value.astype(targets[i].dtype)

    vmem = pl.BlockSpec(memory_space=pltpu.VMEM)
    return pl.pallas_call(
        kernel,
        out_shape=[jax.ShapeDtypeStruct((bb_dev * blk, nocc), dtype)] * count,
        in_specs=[vmem] * len(parts),
        out_specs=[vmem] * count,
        compiler_params=pltpu.CompilerParams(vmem_limit_bytes=4 * 1024 * 1024),
        cost_estimate=pl.CostEstimate(
            flops=SPREAD_COST, bytes_accessed=SPREAD_COST // 1000, transcendentals=0
        ),
        name="spread",
    )(*parts)


def total_of(arrays):
    def kernel(*refs):
        value = refs[0][...].astype(jnp.float32)
        for ref in refs[1:-1]:
            value = value + ref[...].astype(jnp.float32)
        refs[-1][...] = value.astype(refs[-1].dtype)

    vmem = pl.BlockSpec(memory_space=pltpu.VMEM)
    return pl.pallas_call(
        kernel,
        out_shape=jax.ShapeDtypeStruct(arrays[0].shape, jnp.bfloat16),
        in_specs=[vmem] * len(arrays),
        out_specs=vmem,
        compiler_params=pltpu.CompilerParams(vmem_limit_bytes=4 * 1024 * 1024),
        name="total_of",
    )(*arrays)


def owner_sum(parts, blk, bb_dev):
    n_aux, rows, nocc = parts.shape

    def kernel(parts_ref, out_ref):
        sums = [jnp.zeros((blk, nocc), jnp.float32) for _ in range(bb_dev)]
        for s in range(n_aux):
            value = parts_ref[s, :blk, :].astype(jnp.float32)
            which = parts_ref[s, blk:, :][:1].astype(jnp.float32)
            for b in range(bb_dev):
                sums[b] = sums[b] + jnp.where(which == b, value, 0.0)
        for b in range(bb_dev):
            out_ref[b * blk : (b + 1) * blk, :] = sums[b].astype(out_ref.dtype)

    vmem = pl.BlockSpec(memory_space=pltpu.VMEM)
    return pl.pallas_call(
        kernel,
        out_shape=jax.ShapeDtypeStruct((bb_dev * blk, nocc), jnp.bfloat16),
        in_specs=[vmem],
        out_specs=vmem,
        name="owner_sum",
    )(parts)


def on_device(tiles, c_orbitals, basis_order, tile_block, tile_aux, live):
    blk, nocc = tiles.shape[2:]
    n_aux = lax.axis_size("aux")
    bb_dev = basis_order.shape[0] // n_aux
    direct = n_aux == DIRECT

    def swap(array, m):
        return lax.ppermute(array, "aux", [(i, i ^ m) for i in range(n_aux)])

    base = lax.axis_index("aux").astype(jnp.int32) if direct else jnp.int32(0)
    packed = pack_slots(tile_block, tile_aux, live, basis_order, base, bb_dev)
    where_to, which, group, alive = unpack_slots(packed, bb_dev)
    bit = bits_of(where_to, which, alive, n_aux)
    if not direct:
        lists = chunk_lists(where_to, where_to < 0, alive, group, n_aux)
        whole = lax.all_gather(c_orbitals, "aux", axis=0, tiled=True)
        whole = whole.reshape(n_aux, bb_dev * blk, nocc)
        parts = all_in_one(n_aux, lists, bit, tiles, whole)
        moved = lax.all_to_all(parts, "aux", 0, 0, tiled=True)
        return owner_sum(moved, blk, bb_dev)

    depth = n_aux // PLANE
    side = where_to % PLANE >= 2
    last = (where_to >= 3 * PLANE) | ((where_to >= PLANE) & side)
    fit_lists = chunk_lists(where_to, last, alive, group, n_aux)
    two = swap(c_orbitals, 2 * PLANE)
    one = swap(c_orbitals, PLANE)
    beside = swap(c_orbitals, 2)
    across = swap(c_orbitals, 1)
    three = swap(c_orbitals, 3 * PLANE)
    pair = merge([one, two], [], SPREAD_COST)
    pair_beside = swap(pair, 2)
    three_beside = swap(three, 2)
    early = [pair, swap(pair, 1), across, beside, swap(beside, 1)]
    early_from = [(1, (2, None)), (2, (3, None)), (3, (4, None))]
    late_from = []
    for core in range(2):
        early_from += [(PLANE + core, (core, 0)), (2 * PLANE + core, (core, 1))]
        late_from += [
            (PLANE + 2 + core, (core, 0)),
            (2 * PLANE + 2 + core, (core, 1)),
            (3 * PLANE + core, (core, 2)),
            (3 * PLANE + 2 + core, (core, 3)),
        ]
    partial_fit, packed = begin(
        n_aux, fit_lists, bit, packed, tiles, c_orbitals, early, early_from
    )
    late = gate([pair_beside, three, three_beside], partial_fit)
    where_to, _, group, alive = unpack_slots(packed, bb_dev)
    lists = chunk_lists(where_to, where_to < PLANE, alive, group, n_aux)
    *far, fitted, _ = first_part(
        n_aux, fit_lists, lists, bit, tiles, partial_fit, [late, swap(late, 1)], late_from
    )
    far = [far[0]] + [swap(far[r], r) for r in range(1, PLANE)]
    near = second_part(n_aux, lists, bit, tiles, fitted, far[1])
    near = [near[0]] + [swap(near[r], r) for r in range(1, PLANE)]
    far = spread(far, jnp.bfloat16, blk, bb_dev)
    far = [swap(far[dz - 1], dz * PLANE) for dz in range(depth - 1, 0, -1)]
    near = spread(near, jnp.float32, blk, bb_dev)
    return total_of(list(near) + far)


def solution(mesh):
    return jax.shard_map(
        on_device,
        mesh=mesh,
        in_specs=(
            P(("grp", "aux"), None, None, None),
            P(("grp", "aux"), None),
            P("grp"),
            P(("grp", "aux")),
            P(("grp", "aux")),
            P(("grp", "aux")),
        ),
        out_specs=P(("grp", "aux"), None),
        check_vma=False,
    )
```

```python
import functools

import jax
import jax.numpy as jnp
from jax import lax
from jax.experimental import pallas as pl
from jax.experimental.pallas import tpu as pltpu
from jax.sharding import PartitionSpec as P

AB_DEV = 8
CHUNK = 2
TURNS = (8, 2, 1)
TAIL = 16
PLANE = 4
SPREAD_COST = 10**10
DIRECT = 16


def pack_slots(tile_block, tile_aux, live, basis_order, base, bb_dev):
    slots, nbb = tile_block.shape[0], basis_order.shape[0]
    k = lax.iota(jnp.int32, nbb)
    owner = jnp.bitwise_xor(k // bb_dev, base)
    value = (owner * bb_dev + k % bb_dev)[None, :] * AB_DEV + tile_aux[:, None]
    value = jnp.where(basis_order[None, :] == tile_block[:, None], value * 2, 0)
    alive = jnp.pad(live, (0, nbb - 1))[None, :] > lax.iota(jnp.int32, slots)[:, None]
    return jnp.sum(value + alive.astype(jnp.int32), axis=1)


def unpack_slots(packed, bb_dev):
    rest = packed // 2
    tile_aux = rest % AB_DEV
    rest = rest // AB_DEV
    return rest // bb_dev, rest % bb_dev, tile_aux, packed % 2 == 1


def chunk_lists(where_to, later, alive, tile_aux, n_aux):
    slots = where_to.shape[0]
    keys = 2 * AB_DEV
    chunks = slots // CHUNK + keys
    t = lax.iota(jnp.int32, slots)
    group = jnp.where(alive, tile_aux + jnp.where(later, AB_DEV, 0), keys)
    ids = lax.iota(jnp.int32, keys)
    counts = jnp.sum((group[None, :] == ids[:, None]).astype(jnp.int32), axis=1)
    need = (counts + CHUNK - 1) // CHUNK
    ends = jnp.sum(jnp.where(ids[None, :] <= ids[:, None], need[None, :], 0), axis=1)
    rank = jnp.sum(
        ((group[None, :] == group[:, None]) & (t[None, :] < t[:, None])).astype(jnp.int32), axis=1
    )
    start = jnp.sum(jnp.where(group[:, None] > ids[None, :], need[None, :], 0), axis=1)
    place = jnp.where(alive, start * CHUNK + rank, -1)
    q = lax.iota(jnp.int32, chunks * CHUNK)
    hit = place[None, :] == q[:, None]
    lead = place[None, :] == (q // CHUNK * CHUNK)[:, None]
    valid = jnp.any(hit, axis=1)
    slot = jnp.sum(jnp.where(hit, t[None, :], 0), axis=1)
    slot = jnp.where(valid, slot, jnp.sum(jnp.where(lead, t[None, :], 0), axis=1))
    block = jnp.where(valid, jnp.sum(jnp.where(hit, where_to[None, :], 0), axis=1), n_aux)
    gid = jnp.sum(
        (lax.iota(jnp.int32, chunks)[:, None] >= ends[None, :]).astype(jnp.int32), axis=1
    )
    return slot, block, jnp.concatenate([gid % AB_DEV, ends])


def bits_of(where_to, which, alive, n_aux):
    return jnp.max(
        jnp.where(
            (where_to[None, :] == lax.iota(jnp.int32, n_aux)[:, None]) & alive[None, :],
            which[None, :],
            0,
        ),
        axis=1,
    )


def slab(tiles, slot):
    return jnp.concatenate([tiles[slot, p] for p in range(tiles.shape[1])], axis=1)


def chunk_ends(gid_ref, slots):
    chunks = slots // CHUNK + 2 * AB_DEV
    return gid_ref[chunks + AB_DEV - 1], gid_ref[chunks + 2 * AB_DEV - 1]


def turn(ct, bit_ref, m, source):
    blk = ct.shape[2]
    row = pl.multiple_of(bit_ref[m] * blk, blk)
    ct[m] = source[pl.ds(row, blk), :].T


def sweep(low, high, body):
    for size in TURNS:
        whole = (high - low) // size

        @pl.loop(0, whole)
        def _(step, low=low, size=size):
            body([low + step * size + u for u in range(size)])

        low = low + whole * size


def fit(lists, tiles, ct, zacc, low, high):
    slot_ref, block_ref, gid_ref = lists

    def body(group):
        for chunk in group:
            spots = [chunk * CHUNK + i for i in range(CHUNK)]
            left = jnp.concatenate([ct[block_ref[pos]] for pos in spots], axis=1)
            right = jnp.concatenate([slab(tiles, slot_ref[pos]) for pos in spots], axis=0)
            zacc[gid_ref[chunk]] += jnp.dot(left, right, preferred_element_type=jnp.float32)

    sweep(low, high, body)


def apply_fitted(lists, tiles, zb, acc, low, high):
    slot_ref, block_ref, gid_ref = lists
    blk = acc.shape[1]

    def body(group):
        for chunk in group:
            spots = [chunk * CHUNK + i for i in range(CHUNK)]
            left = jnp.concatenate([slab(tiles, slot_ref[pos]) for pos in spots], axis=0)
            value = lax.dot_general(
                left,
                zb[gid_ref[chunk]],
                (((1,), (1,)), ((), ())),
                preferred_element_type=jnp.float32,
            )
            for i, pos in enumerate(spots):
                acc[block_ref[pos]] += value[i * blk : (i + 1) * blk]

    sweep(low, high, body)


def begin(n_aux, lists, bit, packed, tiles_array, own_array, shards, sources):
    slots, auxb, blk, nocc = tiles_array.shape
    n_in = len(shards)

    def kernel(slot_ref, block_ref, gid_ref, bit_ref, packed_ref, tiles, own, *refs):
        c_refs, (zacc, passed, ct) = refs[:n_in], refs[n_in:]
        passed[...] = packed_ref[...]
        zacc[...] = jnp.zeros(zacc.shape, zacc.dtype)
        ct[n_aux] = jnp.zeros((nocc, blk), ct.dtype)
        turn(ct, bit_ref, 0, own)
        for m, (ref, i) in sources:
            turn(ct, bit_ref, m, c_refs[ref] if i is None else c_refs[ref].at[i])
        early, _ = chunk_ends(gid_ref, slots)
        fit((slot_ref, block_ref, gid_ref), tiles, ct, zacc, 0, early)

    smem = pl.BlockSpec(memory_space=pltpu.SMEM)
    vmem = pl.BlockSpec(memory_space=pltpu.VMEM)
    return pl.pallas_call(
        kernel,
        out_shape=[
            jax.ShapeDtypeStruct((AB_DEV, nocc, auxb * nocc), jnp.float32),
            jax.ShapeDtypeStruct(packed.shape, packed.dtype),
        ],
        in_specs=[smem] * 4 + [vmem] * (3 + n_in),
        out_specs=[vmem] * 2,
        scratch_shapes=[pltpu.VMEM((n_aux + 1, nocc, blk), jnp.bfloat16)],
        compiler_params=pltpu.CompilerParams(vmem_limit_bytes=20 * 1024 * 1024),
        cost_estimate=pl.CostEstimate(
            flops=2 * tiles_array.size * nocc, bytes_accessed=tiles_array.size, transcendentals=0
        ),
        name="begin",
    )(*lists, bit, packed, tiles_array, own_array, *shards)


def put(bit_ref, acc, m, out_ref, place):
    blk, nocc = acc.shape[1:]
    out_ref[place, :blk, :] = acc[m].astype(out_ref.dtype)
    out_ref[place, blk:, :] = jnp.full((TAIL, nocc), bit_ref[m], jnp.int32).astype(
        jnp.float32
    ).astype(out_ref.dtype)


def clear(n_aux, ct, acc):
    ct[n_aux] = jnp.zeros(ct.shape[1:], ct.dtype)
    acc[...] = jnp.zeros(acc.shape, acc.dtype)


def round_fitted(zacc, zb):
    for g in range(zacc.shape[0]):
        zb[g] = zacc[g].astype(zb.dtype)


def first_part(n_aux, fit_lists, lists, bit, tiles_array, partial_fit, shards, sources):
    slots, auxb, blk, nocc = tiles_array.shape
    n_in = len(shards)

    def kernel(*refs):
        fit_refs, refs = refs[:3], refs[3:]
        list_refs, bit_ref, tiles = refs[:3], refs[3], refs[4]
        c_refs, out_refs = refs[6 : 6 + n_in], refs[6 + n_in : -4]
        zb, zacc, ct, acc = refs[-4:]
        clear(n_aux, ct, acc)
        for m, (ref, i) in sources:
            turn(ct, bit_ref, m, c_refs[ref] if i is None else c_refs[ref].at[i])
        fit(fit_refs, tiles, ct, zacc, *chunk_ends(fit_refs[2], slots))
        round_fitted(zacc, zb)
        far, _ = chunk_ends(list_refs[2], slots)
        apply_fitted(list_refs, tiles, zb, acc, 0, far)
        for m in range(PLANE, n_aux):
            put(bit_ref, acc, m, out_refs[m % PLANE], m // PLANE - 1)

    smem = pl.BlockSpec(memory_space=pltpu.SMEM)
    vmem = pl.BlockSpec(memory_space=pltpu.VMEM)
    shape = (n_aux // PLANE - 1, blk + TAIL, nocc)
    out_shape = [jax.ShapeDtypeStruct(shape, jnp.bfloat16)] * PLANE
    out_shape = out_shape + [
        jax.ShapeDtypeStruct((AB_DEV, nocc, auxb * nocc), jnp.bfloat16),
        jax.ShapeDtypeStruct(partial_fit.shape, partial_fit.dtype),
    ]
    return pl.pallas_call(
        kernel,
        out_shape=out_shape,
        in_specs=[smem] * 7 + [vmem] * (2 + n_in),
        out_specs=[vmem] * len(out_shape),
        scratch_shapes=[
            pltpu.VMEM((n_aux + 1, nocc, blk), jnp.bfloat16),
            pltpu.VMEM((n_aux + 1, blk, nocc), jnp.float32),
        ],
        input_output_aliases={8: PLANE + 1},
        compiler_params=pltpu.CompilerParams(vmem_limit_bytes=20 * 1024 * 1024),
        cost_estimate=pl.CostEstimate(
            flops=3 * tiles_array.size * nocc, bytes_accessed=tiles_array.size, transcendentals=0
        ),
        name="first_part",
    )(*fit_lists, *lists, bit, tiles_array, partial_fit, *shards)


def second_part(n_aux, lists, bit, tiles_array, fitted, after):
    slots, auxb, blk, nocc = tiles_array.shape

    def kernel(slot_ref, block_ref, gid_ref, bit_ref, tiles, zb, _, *refs):
        out_refs, acc = refs[:-1], refs[-1]
        acc[...] = jnp.zeros(acc.shape, acc.dtype)
        apply_fitted(
            (slot_ref, block_ref, gid_ref), tiles, zb, acc, *chunk_ends(gid_ref, slots)
        )
        for m in range(PLANE):
            put(bit_ref, acc, m, out_refs[m], 0)

    smem = pl.BlockSpec(memory_space=pltpu.SMEM)
    vmem = pl.BlockSpec(memory_space=pltpu.VMEM)
    shape = (1, blk + TAIL, nocc)
    return pl.pallas_call(
        kernel,
        out_shape=[jax.ShapeDtypeStruct(shape, jnp.bfloat16)] * PLANE,
        in_specs=[smem] * 4 + [vmem, vmem, pl.BlockSpec(memory_space=pl.ANY)],
        out_specs=[vmem] * PLANE,
        scratch_shapes=[pltpu.VMEM((n_aux + 1, blk, nocc), jnp.float32)],
        compiler_params=pltpu.CompilerParams(vmem_limit_bytes=20 * 1024 * 1024),
        cost_estimate=pl.CostEstimate(
            flops=10**10, bytes_accessed=tiles_array.size, transcendentals=0
        ),
        name="second_part",
    )(*lists, bit, tiles_array, fitted, after)


def all_in_one(n_aux, lists, bit, tiles_array, whole):
    slots, auxb, blk, nocc = tiles_array.shape

    def kernel(slot_ref, block_ref, gid_ref, bit_ref, tiles, c_ref, out_ref, ct, zacc, zb, acc):
        lists = (slot_ref, block_ref, gid_ref)
        clear(n_aux, ct, acc)
        zacc[...] = jnp.zeros(zacc.shape, zacc.dtype)

        @pl.loop(0, n_aux)
        def _(m):
            turn(ct, bit_ref, m, c_ref.at[m])

        _, total = chunk_ends(gid_ref, slots)
        fit(lists, tiles, ct, zacc, 0, total)
        round_fitted(zacc, zb)
        apply_fitted(lists, tiles, zb, acc, 0, total)

        @pl.loop(0, n_aux)
        def _(m):
            put(bit_ref, acc, m, out_ref, m)

    smem = pl.BlockSpec(memory_space=pltpu.SMEM)
    vmem = pl.BlockSpec(memory_space=pltpu.VMEM)
    return pl.pallas_call(
        kernel,
        out_shape=jax.ShapeDtypeStruct((n_aux, blk + TAIL, nocc), jnp.bfloat16),
        in_specs=[smem] * 4 + [vmem] * 2,
        out_specs=vmem,
        scratch_shapes=[
            pltpu.VMEM((n_aux + 1, nocc, blk), jnp.bfloat16),
            pltpu.VMEM((AB_DEV, nocc, auxb * nocc), jnp.float32),
            pltpu.VMEM((AB_DEV, nocc, auxb * nocc), jnp.bfloat16),
            pltpu.VMEM((n_aux + 1, blk, nocc), jnp.float32),
        ],
        compiler_params=pltpu.CompilerParams(vmem_limit_bytes=46 * 1024 * 1024),
        name="all_in_one",
    )(*lists, bit, tiles_array, whole)


def gate(arrays, after):
    counts = [array.shape[0] if array.ndim == 3 else 1 for array in arrays]

    def kernel(*refs):
        target, place = refs[-1], 0
        for ref, count in zip(refs, counts):
            value = ref[...]
            target[place : place + count] = value.reshape((count,) + value.shape[-2:])
            place += count

    vmem = pl.BlockSpec(memory_space=pltpu.VMEM)
    return pl.pallas_call(
        kernel,
        out_shape=jax.ShapeDtypeStruct((sum(counts),) + arrays[0].shape[-2:], arrays[0].dtype),
        in_specs=[vmem] * len(arrays) + [pl.BlockSpec(memory_space=pl.ANY)],
        out_specs=vmem,
        compiler_params=pltpu.CompilerParams(vmem_limit_bytes=4 * 1024 * 1024),
        name="gate",
    )(*arrays, after)


def merge(arrays, after, cost):
    def kernel(*refs):
        for i, ref in enumerate(refs[: len(arrays)]):
            refs[-1][i] = ref[...]

    vmem = pl.BlockSpec(memory_space=pltpu.VMEM)
    return pl.pallas_call(
        kernel,
        out_shape=jax.ShapeDtypeStruct((len(arrays),) + arrays[0].shape, arrays[0].dtype),
        in_specs=[vmem] * len(arrays) + [pl.BlockSpec(memory_space=pl.ANY)] * len(after),
        out_specs=vmem,
        compiler_params=pltpu.CompilerParams(vmem_limit_bytes=4 * 1024 * 1024),
        cost_estimate=pl.CostEstimate(flops=cost, bytes_accessed=cost // 1000, transcendentals=0),
        name="merge",
    )(*arrays, *after)


def placed_sum(sources, i, blk, bb_dev):
    nocc = sources[0].shape[2]
    sums = [jnp.zeros((blk, nocc), jnp.float32) for _ in range(bb_dev)]
    for source in sources:
        value = source[i, :blk, :].astype(jnp.float32)
        which = source[i, blk:, :][:1].astype(jnp.float32)
        for b in range(bb_dev):
            sums[b] = sums[b] + jnp.where(which == b, value, 0.0)
    return sums


def spread(parts, dtype, blk, bb_dev):
    count, rows, nocc = parts[0].shape

    def kernel(*refs):
        sources, targets = refs[: len(parts)], refs[len(parts) :]
        for i in range(count):
            for b, value in enumerate(placed_sum(sources, i, blk, bb_dev)):
                targets[i][b * blk : (b + 1) * blk, :] = value.astype(targets[i].dtype)

    vmem = pl.BlockSpec(memory_space=pltpu.VMEM)
    return pl.pallas_call(
        kernel,
        out_shape=[jax.ShapeDtypeStruct((bb_dev * blk, nocc), dtype)] * count,
        in_specs=[vmem] * len(parts),
        out_specs=[vmem] * count,
        compiler_params=pltpu.CompilerParams(vmem_limit_bytes=4 * 1024 * 1024),
        cost_estimate=pl.CostEstimate(
            flops=SPREAD_COST, bytes_accessed=SPREAD_COST // 1000, transcendentals=0
        ),
        name="spread",
    )(*parts)


def total_of(arrays):
    def kernel(*refs):
        value = refs[0][...].astype(jnp.float32)
        for ref in refs[1:-1]:
            value = value + ref[...].astype(jnp.float32)
        refs[-1][...] = value.astype(refs[-1].dtype)

    vmem = pl.BlockSpec(memory_space=pltpu.VMEM)
    return pl.pallas_call(
        kernel,
        out_shape=jax.ShapeDtypeStruct(arrays[0].shape, jnp.bfloat16),
        in_specs=[vmem] * len(arrays),
        out_specs=vmem,
        compiler_params=pltpu.CompilerParams(vmem_limit_bytes=4 * 1024 * 1024),
        name="total_of",
    )(*arrays)


def owner_sum(parts, blk, bb_dev):
    n_aux, rows, nocc = parts.shape

    def kernel(parts_ref, out_ref):
        sums = [jnp.zeros((blk, nocc), jnp.float32) for _ in range(bb_dev)]
        for s in range(n_aux):
            value = parts_ref[s, :blk, :].astype(jnp.float32)
            which = parts_ref[s, blk:, :][:1].astype(jnp.float32)
            for b in range(bb_dev):
                sums[b] = sums[b] + jnp.where(which == b, value, 0.0)
        for b in range(bb_dev):
            out_ref[b * blk : (b + 1) * blk, :] = sums[b].astype(out_ref.dtype)

    vmem = pl.BlockSpec(memory_space=pltpu.VMEM)
    return pl.pallas_call(
        kernel,
        out_shape=jax.ShapeDtypeStruct((bb_dev * blk, nocc), jnp.bfloat16),
        in_specs=[vmem],
        out_specs=vmem,
        name="owner_sum",
    )(parts)


def on_device(tiles, c_orbitals, basis_order, tile_block, tile_aux, live):
    blk, nocc = tiles.shape[2:]
    n_aux = lax.axis_size("aux")
    bb_dev = basis_order.shape[0] // n_aux
    direct = n_aux == DIRECT

    def swap(array, m):
        return lax.ppermute(array, "aux", [(i, i ^ m) for i in range(n_aux)])

    base = lax.axis_index("aux").astype(jnp.int32) if direct else jnp.int32(0)
    packed = pack_slots(tile_block, tile_aux, live, basis_order, base, bb_dev)
    where_to, which, group, alive = unpack_slots(packed, bb_dev)
    bit = bits_of(where_to, which, alive, n_aux)
    if not direct:
        lists = chunk_lists(where_to, where_to < 0, alive, group, n_aux)
        whole = lax.all_gather(c_orbitals, "aux", axis=0, tiled=True)
        whole = whole.reshape(n_aux, bb_dev * blk, nocc)
        parts = all_in_one(n_aux, lists, bit, tiles, whole)
        moved = lax.all_to_all(parts, "aux", 0, 0, tiled=True)
        return owner_sum(moved, blk, bb_dev)

    depth = n_aux // PLANE
    side = where_to % PLANE >= 2
    last = (where_to >= 3 * PLANE) | ((where_to > 2) & side)
    fit_lists = chunk_lists(where_to, last, alive, group, n_aux)
    two = swap(c_orbitals, 2 * PLANE)
    one = swap(c_orbitals, PLANE)
    beside = swap(c_orbitals, 2)
    across = swap(c_orbitals, 1)
    three = swap(c_orbitals, 3 * PLANE)
    pair = merge([one, two], [], SPREAD_COST)
    pair_beside = swap(pair, 2)
    three_beside = swap(three, 2)
    early = [pair, swap(pair, 1), across, beside]
    early_from = [(1, (2, None)), (2, (3, None))]
    late_from = [(3, (1, 4))]
    for core in range(2):
        early_from += [(PLANE + core, (core, 0)), (2 * PLANE + core, (core, 1))]
        late_from += [
            (PLANE + 2 + core, (core, 0)),
            (2 * PLANE + 2 + core, (core, 1)),
            (3 * PLANE + core, (core, 2)),
            (3 * PLANE + 2 + core, (core, 3)),
        ]
    partial_fit, packed = begin(
        n_aux, fit_lists, bit, packed, tiles, c_orbitals, early, early_from
    )
    late = gate([pair_beside, three, three_beside, beside], partial_fit)
    where_to, _, group, alive = unpack_slots(packed, bb_dev)
    lists = chunk_lists(where_to, where_to < PLANE, alive, group, n_aux)
    *far, fitted, _ = first_part(
        n_aux, fit_lists, lists, bit, tiles, partial_fit, [late, swap(late, 1)], late_from
    )
    far = [far[0]] + [swap(far[r], r) for r in range(1, PLANE)]
    near = second_part(n_aux, lists, bit, tiles, fitted, far[1])
    near = [near[0]] + [swap(near[r], r) for r in range(1, PLANE)]
    far = spread(far, jnp.bfloat16, blk, bb_dev)
    far = [swap(far[dz - 1], dz * PLANE) for dz in range(depth - 1, 0, -1)]
    near = spread(near, jnp.float32, blk, bb_dev)
    return total_of(list(near) + far)


def solution(mesh):
    return jax.shard_map(
        on_device,
        mesh=mesh,
        in_specs=(
            P(("grp", "aux"), None, None, None),
            P(("grp", "aux"), None),
            P("grp"),
            P(("grp", "aux")),
            P(("grp", "aux")),
            P(("grp", "aux")),
        ),
        out_specs=P(("grp", "aux"), None),
        check_vma=False,
    )
```

```python
import functools

import jax
import jax.numpy as jnp
from jax import lax
from jax.experimental import pallas as pl
from jax.experimental.pallas import tpu as pltpu
from jax.sharding import PartitionSpec as P

AB_DEV = 8
CHUNK = 2
TURNS = (8, 4, 2, 1)
TAIL = 16
PLANE = 4
SPREAD_COST = 10**10
DIRECT = 16


def pack_slots(tile_block, tile_aux, live, basis_order, base, bb_dev):
    slots, nbb = tile_block.shape[0], basis_order.shape[0]
    k = lax.iota(jnp.int32, nbb)
    owner = jnp.bitwise_xor(k // bb_dev, base)
    value = (owner * bb_dev + k % bb_dev)[None, :] * AB_DEV + tile_aux[:, None]
    value = jnp.where(basis_order[None, :] == tile_block[:, None], value * 2, 0)
    alive = jnp.pad(live, (0, nbb - 1))[None, :] > lax.iota(jnp.int32, slots)[:, None]
    return jnp.sum(value + alive.astype(jnp.int32), axis=1)


def unpack_slots(packed, bb_dev):
    rest = packed // 2
    tile_aux = rest % AB_DEV
    rest = rest // AB_DEV
    return rest // bb_dev, rest % bb_dev, tile_aux, packed % 2 == 1


def chunk_lists(where_to, later, alive, tile_aux, n_aux):
    slots = where_to.shape[0]
    keys = 2 * AB_DEV
    chunks = slots // CHUNK + keys
    t = lax.iota(jnp.int32, slots)
    group = jnp.where(alive, tile_aux + jnp.where(later, AB_DEV, 0), keys)
    ids = lax.iota(jnp.int32, keys)
    counts = jnp.sum((group[None, :] == ids[:, None]).astype(jnp.int32), axis=1)
    need = (counts + CHUNK - 1) // CHUNK
    ends = jnp.sum(jnp.where(ids[None, :] <= ids[:, None], need[None, :], 0), axis=1)
    rank = jnp.sum(
        ((group[None, :] == group[:, None]) & (t[None, :] < t[:, None])).astype(jnp.int32), axis=1
    )
    start = jnp.sum(jnp.where(group[:, None] > ids[None, :], need[None, :], 0), axis=1)
    place = jnp.where(alive, start * CHUNK + rank, -1)
    q = lax.iota(jnp.int32, chunks * CHUNK)
    hit = place[None, :] == q[:, None]
    lead = place[None, :] == (q // CHUNK * CHUNK)[:, None]
    valid = jnp.any(hit, axis=1)
    slot = jnp.sum(jnp.where(hit, t[None, :], 0), axis=1)
    slot = jnp.where(valid, slot, jnp.sum(jnp.where(lead, t[None, :], 0), axis=1))
    block = jnp.where(valid, jnp.sum(jnp.where(hit, where_to[None, :], 0), axis=1), n_aux)
    gid = jnp.sum(
        (lax.iota(jnp.int32, chunks)[:, None] >= ends[None, :]).astype(jnp.int32), axis=1
    )
    return slot, block, jnp.concatenate([gid % AB_DEV, ends])


def bits_of(where_to, which, alive, n_aux):
    return jnp.max(
        jnp.where(
            (where_to[None, :] == lax.iota(jnp.int32, n_aux)[:, None]) & alive[None, :],
            which[None, :],
            0,
        ),
        axis=1,
    )


def slab(tiles, slot):
    return jnp.concatenate([tiles[slot, p] for p in range(tiles.shape[1])], axis=1)


def chunk_ends(gid_ref, slots):
    chunks = slots // CHUNK + 2 * AB_DEV
    return gid_ref[chunks + AB_DEV - 1], gid_ref[chunks + 2 * AB_DEV - 1]


def turn(ct, bit_ref, m, source):
    blk = ct.shape[2]
    row = pl.multiple_of(bit_ref[m] * blk, blk)
    ct[m] = source[pl.ds(row, blk), :].T


def sweep(low, high, body):
    for size in TURNS:
        whole = (high - low) // size

        @pl.loop(0, whole)
        def _(step, low=low, size=size):
            body([low + step * size + u for u in range(size)])

        low = low + whole * size


def fit(lists, tiles, ct, zacc, low, high):
    slot_ref, block_ref, gid_ref = lists

    def body(group):
        for chunk in group:
            spots = [chunk * CHUNK + i for i in range(CHUNK)]
            left = jnp.concatenate([ct[block_ref[pos]] for pos in spots], axis=1)
            right = jnp.concatenate([slab(tiles, slot_ref[pos]) for pos in spots], axis=0)
            zacc[gid_ref[chunk]] += jnp.dot(left, right, preferred_element_type=jnp.float32)

    sweep(low, high, body)


def apply_fitted(lists, tiles, zb, acc, low, high):
    slot_ref, block_ref, gid_ref = lists
    blk = acc.shape[1]

    def body(group):
        for chunk in group:
            spots = [chunk * CHUNK + i for i in range(CHUNK)]
            left = jnp.concatenate([slab(tiles, slot_ref[pos]) for pos in spots], axis=0)
            value = lax.dot_general(
                left,
                zb[gid_ref[chunk]],
                (((1,), (1,)), ((), ())),
                preferred_element_type=jnp.float32,
            )
            for i, pos in enumerate(spots):
                acc[block_ref[pos]] += value[i * blk : (i + 1) * blk]

    sweep(low, high, body)


def begin(n_aux, lists, bit, packed, tiles_array, own_array, shards, sources):
    slots, auxb, blk, nocc = tiles_array.shape
    n_in = len(shards)

    def kernel(slot_ref, block_ref, gid_ref, bit_ref, packed_ref, tiles, own, *refs):
        c_refs, (zacc, passed, ct) = refs[:n_in], refs[n_in:]
        passed[...] = packed_ref[...]
        zacc[...] = jnp.zeros(zacc.shape, zacc.dtype)
        ct[n_aux] = jnp.zeros((nocc, blk), ct.dtype)
        turn(ct, bit_ref, 0, own)
        for m, (ref, i) in sources:
            turn(ct, bit_ref, m, c_refs[ref] if i is None else c_refs[ref].at[i])
        early, _ = chunk_ends(gid_ref, slots)
        fit((slot_ref, block_ref, gid_ref), tiles, ct, zacc, 0, early)

    smem = pl.BlockSpec(memory_space=pltpu.SMEM)
    vmem = pl.BlockSpec(memory_space=pltpu.VMEM)
    return pl.pallas_call(
        kernel,
        out_shape=[
            jax.ShapeDtypeStruct((AB_DEV, nocc, auxb * nocc), jnp.float32),
            jax.ShapeDtypeStruct(packed.shape, packed.dtype),
        ],
        in_specs=[smem] * 4 + [vmem] * (3 + n_in),
        out_specs=[vmem] * 2,
        scratch_shapes=[pltpu.VMEM((n_aux + 1, nocc, blk), jnp.bfloat16)],
        compiler_params=pltpu.CompilerParams(vmem_limit_bytes=20 * 1024 * 1024),
        cost_estimate=pl.CostEstimate(
            flops=2 * tiles_array.size * nocc, bytes_accessed=tiles_array.size, transcendentals=0
        ),
        name="begin",
    )(*lists, bit, packed, tiles_array, own_array, *shards)


def put(bit_ref, acc, m, out_ref, place):
    blk, nocc = acc.shape[1:]
    out_ref[place, :blk, :] = acc[m].astype(out_ref.dtype)
    out_ref[place, blk:, :] = jnp.full((TAIL, nocc), bit_ref[m], jnp.int32).astype(
        jnp.float32
    ).astype(out_ref.dtype)


def clear(n_aux, ct, acc):
    ct[n_aux] = jnp.zeros(ct.shape[1:], ct.dtype)
    acc[...] = jnp.zeros(acc.shape, acc.dtype)


def round_fitted(zacc, zb):
    for g in range(zacc.shape[0]):
        zb[g] = zacc[g].astype(zb.dtype)


def first_part(n_aux, fit_lists, lists, bit, tiles_array, partial_fit, shards, sources):
    slots, auxb, blk, nocc = tiles_array.shape
    n_in = len(shards)

    def kernel(*refs):
        fit_refs, refs = refs[:3], refs[3:]
        list_refs, bit_ref, tiles = refs[:3], refs[3], refs[4]
        c_refs, out_refs = refs[6 : 6 + n_in], refs[6 + n_in : -4]
        zb, zacc, ct, acc = refs[-4:]
        clear(n_aux, ct, acc)
        for m, (ref, i) in sources:
            turn(ct, bit_ref, m, c_refs[ref] if i is None else c_refs[ref].at[i])
        fit(fit_refs, tiles, ct, zacc, *chunk_ends(fit_refs[2], slots))
        round_fitted(zacc, zb)
        far, _ = chunk_ends(list_refs[2], slots)
        apply_fitted(list_refs, tiles, zb, acc, 0, far)
        for m in range(PLANE, n_aux):
            put(bit_ref, acc, m, out_refs[m % PLANE], m // PLANE - 1)

    smem = pl.BlockSpec(memory_space=pltpu.SMEM)
    vmem = pl.BlockSpec(memory_space=pltpu.VMEM)
    shape = (n_aux // PLANE - 1, blk + TAIL, nocc)
    out_shape = [jax.ShapeDtypeStruct(shape, jnp.bfloat16)] * PLANE
    out_shape = out_shape + [
        jax.ShapeDtypeStruct((AB_DEV, nocc, auxb * nocc), jnp.bfloat16),
        jax.ShapeDtypeStruct(partial_fit.shape, partial_fit.dtype),
    ]
    return pl.pallas_call(
        kernel,
        out_shape=out_shape,
        in_specs=[smem] * 7 + [vmem] * (2 + n_in),
        out_specs=[vmem] * len(out_shape),
        scratch_shapes=[
            pltpu.VMEM((n_aux + 1, nocc, blk), jnp.bfloat16),
            pltpu.VMEM((n_aux + 1, blk, nocc), jnp.float32),
        ],
        input_output_aliases={8: PLANE + 1},
        compiler_params=pltpu.CompilerParams(vmem_limit_bytes=20 * 1024 * 1024),
        cost_estimate=pl.CostEstimate(
            flops=3 * tiles_array.size * nocc, bytes_accessed=tiles_array.size, transcendentals=0
        ),
        name="first_part",
    )(*fit_lists, *lists, bit, tiles_array, partial_fit, *shards)


def second_part(n_aux, lists, bit, tiles_array, fitted, after):
    slots, auxb, blk, nocc = tiles_array.shape

    def kernel(slot_ref, block_ref, gid_ref, bit_ref, tiles, zb, _, *refs):
        out_refs, acc = refs[:-1], refs[-1]
        acc[...] = jnp.zeros(acc.shape, acc.dtype)
        apply_fitted(
            (slot_ref, block_ref, gid_ref), tiles, zb, acc, *chunk_ends(gid_ref, slots)
        )
        for m in range(PLANE):
            put(bit_ref, acc, m, out_refs[m], 0)

    smem = pl.BlockSpec(memory_space=pltpu.SMEM)
    vmem = pl.BlockSpec(memory_space=pltpu.VMEM)
    shape = (1, blk + TAIL, nocc)
    return pl.pallas_call(
        kernel,
        out_shape=[jax.ShapeDtypeStruct(shape, jnp.bfloat16)] * PLANE,
        in_specs=[smem] * 4 + [vmem, vmem, pl.BlockSpec(memory_space=pl.ANY)],
        out_specs=[vmem] * PLANE,
        scratch_shapes=[pltpu.VMEM((n_aux + 1, blk, nocc), jnp.float32)],
        compiler_params=pltpu.CompilerParams(vmem_limit_bytes=20 * 1024 * 1024),
        cost_estimate=pl.CostEstimate(
            flops=10**10, bytes_accessed=tiles_array.size, transcendentals=0
        ),
        name="second_part",
    )(*lists, bit, tiles_array, fitted, after)


def all_in_one(n_aux, lists, bit, tiles_array, whole):
    slots, auxb, blk, nocc = tiles_array.shape

    def kernel(slot_ref, block_ref, gid_ref, bit_ref, tiles, c_ref, out_ref, ct, zacc, zb, acc):
        lists = (slot_ref, block_ref, gid_ref)
        clear(n_aux, ct, acc)
        zacc[...] = jnp.zeros(zacc.shape, zacc.dtype)

        @pl.loop(0, n_aux)
        def _(m):
            turn(ct, bit_ref, m, c_ref.at[m])

        _, total = chunk_ends(gid_ref, slots)
        fit(lists, tiles, ct, zacc, 0, total)
        round_fitted(zacc, zb)
        apply_fitted(lists, tiles, zb, acc, 0, total)

        @pl.loop(0, n_aux)
        def _(m):
            put(bit_ref, acc, m, out_ref, m)

    smem = pl.BlockSpec(memory_space=pltpu.SMEM)
    vmem = pl.BlockSpec(memory_space=pltpu.VMEM)
    return pl.pallas_call(
        kernel,
        out_shape=jax.ShapeDtypeStruct((n_aux, blk + TAIL, nocc), jnp.bfloat16),
        in_specs=[smem] * 4 + [vmem] * 2,
        out_specs=vmem,
        scratch_shapes=[
            pltpu.VMEM((n_aux + 1, nocc, blk), jnp.bfloat16),
            pltpu.VMEM((AB_DEV, nocc, auxb * nocc), jnp.float32),
            pltpu.VMEM((AB_DEV, nocc, auxb * nocc), jnp.bfloat16),
            pltpu.VMEM((n_aux + 1, blk, nocc), jnp.float32),
        ],
        compiler_params=pltpu.CompilerParams(vmem_limit_bytes=46 * 1024 * 1024),
        name="all_in_one",
    )(*lists, bit, tiles_array, whole)


def gate(arrays, after):
    counts = [array.shape[0] if array.ndim == 3 else 1 for array in arrays]

    def kernel(*refs):
        target, place = refs[-1], 0
        for ref, count in zip(refs, counts):
            value = ref[...]
            target[place : place + count] = value.reshape((count,) + value.shape[-2:])
            place += count

    vmem = pl.BlockSpec(memory_space=pltpu.VMEM)
    return pl.pallas_call(
        kernel,
        out_shape=jax.ShapeDtypeStruct((sum(counts),) + arrays[0].shape[-2:], arrays[0].dtype),
        in_specs=[vmem] * len(arrays) + [pl.BlockSpec(memory_space=pl.ANY)],
        out_specs=vmem,
        compiler_params=pltpu.CompilerParams(vmem_limit_bytes=4 * 1024 * 1024),
        name="gate",
    )(*arrays, after)


def merge(arrays, after, cost):
    def kernel(*refs):
        for i, ref in enumerate(refs[: len(arrays)]):
            refs[-1][i] = ref[...]

    vmem = pl.BlockSpec(memory_space=pltpu.VMEM)
    return pl.pallas_call(
        kernel,
        out_shape=jax.ShapeDtypeStruct((len(arrays),) + arrays[0].shape, arrays[0].dtype),
        in_specs=[vmem] * len(arrays) + [pl.BlockSpec(memory_space=pl.ANY)] * len(after),
        out_specs=vmem,
        compiler_params=pltpu.CompilerParams(vmem_limit_bytes=4 * 1024 * 1024),
        cost_estimate=pl.CostEstimate(flops=cost, bytes_accessed=cost // 1000, transcendentals=0),
        name="merge",
    )(*arrays, *after)


def placed_sum(sources, i, blk, bb_dev):
    nocc = sources[0].shape[2]
    sums = [jnp.zeros((blk, nocc), jnp.float32) for _ in range(bb_dev)]
    for source in sources:
        value = source[i, :blk, :].astype(jnp.float32)
        which = source[i, blk:, :][:1].astype(jnp.float32)
        for b in range(bb_dev):
            sums[b] = sums[b] + jnp.where(which == b, value, 0.0)
    return sums


def spread(parts, dtype, blk, bb_dev):
    count, rows, nocc = parts[0].shape

    def kernel(*refs):
        sources, targets = refs[: len(parts)], refs[len(parts) :]
        for i in range(count):
            for b, value in enumerate(placed_sum(sources, i, blk, bb_dev)):
                targets[i][b * blk : (b + 1) * blk, :] = value.astype(targets[i].dtype)

    vmem = pl.BlockSpec(memory_space=pltpu.VMEM)
    return pl.pallas_call(
        kernel,
        out_shape=[jax.ShapeDtypeStruct((bb_dev * blk, nocc), dtype)] * count,
        in_specs=[vmem] * len(parts),
        out_specs=[vmem] * count,
        compiler_params=pltpu.CompilerParams(vmem_limit_bytes=4 * 1024 * 1024),
        cost_estimate=pl.CostEstimate(
            flops=SPREAD_COST, bytes_accessed=SPREAD_COST // 1000, transcendentals=0
        ),
        name="spread",
    )(*parts)


def total_of(arrays):
    def kernel(*refs):
        value = refs[0][...].astype(jnp.float32)
        for ref in refs[1:-1]:
            value = value + ref[...].astype(jnp.float32)
        refs[-1][...] = value.astype(refs[-1].dtype)

    vmem = pl.BlockSpec(memory_space=pltpu.VMEM)
    return pl.pallas_call(
        kernel,
        out_shape=jax.ShapeDtypeStruct(arrays[0].shape, jnp.bfloat16),
        in_specs=[vmem] * len(arrays),
        out_specs=vmem,
        compiler_params=pltpu.CompilerParams(vmem_limit_bytes=4 * 1024 * 1024),
        name="total_of",
    )(*arrays)


def owner_sum(parts, blk, bb_dev):
    n_aux, rows, nocc = parts.shape

    def kernel(parts_ref, out_ref):
        sums = [jnp.zeros((blk, nocc), jnp.float32) for _ in range(bb_dev)]
        for s in range(n_aux):
            value = parts_ref[s, :blk, :].astype(jnp.float32)
            which = parts_ref[s, blk:, :][:1].astype(jnp.float32)
            for b in range(bb_dev):
                sums[b] = sums[b] + jnp.where(which == b, value, 0.0)
        for b in range(bb_dev):
            out_ref[b * blk : (b + 1) * blk, :] = sums[b].astype(out_ref.dtype)

    vmem = pl.BlockSpec(memory_space=pltpu.VMEM)
    return pl.pallas_call(
        kernel,
        out_shape=jax.ShapeDtypeStruct((bb_dev * blk, nocc), jnp.bfloat16),
        in_specs=[vmem],
        out_specs=vmem,
        name="owner_sum",
    )(parts)


def on_device(tiles, c_orbitals, basis_order, tile_block, tile_aux, live):
    blk, nocc = tiles.shape[2:]
    n_aux = lax.axis_size("aux")
    bb_dev = basis_order.shape[0] // n_aux
    direct = n_aux == DIRECT

    def swap(array, m):
        return lax.ppermute(array, "aux", [(i, i ^ m) for i in range(n_aux)])

    base = lax.axis_index("aux").astype(jnp.int32) if direct else jnp.int32(0)
    packed = pack_slots(tile_block, tile_aux, live, basis_order, base, bb_dev)
    where_to, which, group, alive = unpack_slots(packed, bb_dev)
    bit = bits_of(where_to, which, alive, n_aux)
    if not direct:
        lists = chunk_lists(where_to, where_to < 0, alive, group, n_aux)
        whole = lax.all_gather(c_orbitals, "aux", axis=0, tiled=True)
        whole = whole.reshape(n_aux, bb_dev * blk, nocc)
        parts = all_in_one(n_aux, lists, bit, tiles, whole)
        moved = lax.all_to_all(parts, "aux", 0, 0, tiled=True)
        return owner_sum(moved, blk, bb_dev)

    depth = n_aux // PLANE
    side = where_to % PLANE >= 2
    last = (where_to >= 3 * PLANE) | ((where_to >= PLANE) & side)
    fit_lists = chunk_lists(where_to, last, alive, group, n_aux)
    two = swap(c_orbitals, 2 * PLANE)
    one = swap(c_orbitals, PLANE)
    beside = swap(c_orbitals, 2)
    across = swap(c_orbitals, 1)
    three = swap(c_orbitals, 3 * PLANE)
    pair = merge([one, two], [], SPREAD_COST)
    pair_beside = swap(pair, 2)
    three_beside = swap(three, 2)
    early = [pair, swap(pair, 1), across, beside, swap(beside, 1)]
    early_from = [(1, (2, None)), (2, (3, None)), (3, (4, None))]
    late_from = []
    for core in range(2):
        early_from += [(PLANE + core, (core, 0)), (2 * PLANE + core, (core, 1))]
        late_from += [
            (PLANE + 2 + core, (core, 0)),
            (2 * PLANE + 2 + core, (core, 1)),
            (3 * PLANE + core, (core, 2)),
            (3 * PLANE + 2 + core, (core, 3)),
        ]
    partial_fit, packed = begin(
        n_aux, fit_lists, bit, packed, tiles, c_orbitals, early, early_from
    )
    late = gate([pair_beside, three, three_beside], partial_fit)
    where_to, _, group, alive = unpack_slots(packed, bb_dev)
    lists = chunk_lists(where_to, where_to < PLANE, alive, group, n_aux)
    *far, fitted, _ = first_part(
        n_aux, fit_lists, lists, bit, tiles, partial_fit, [late, swap(late, 1)], late_from
    )
    far = [far[0]] + [swap(far[r], r) for r in range(1, PLANE)]
    near = second_part(n_aux, lists, bit, tiles, fitted, far[1])
    near = [near[0]] + [swap(near[r], r) for r in range(1, PLANE)]
    far = spread(far, jnp.bfloat16, blk, bb_dev)
    far = [swap(far[dz - 1], dz * PLANE) for dz in range(1, depth)]
    near = spread(near, jnp.float32, blk, bb_dev)
    return total_of(list(near) + far)


def solution(mesh):
    return jax.shard_map(
        on_device,
        mesh=mesh,
        in_specs=(
            P(("grp", "aux"), None, None, None),
            P(("grp", "aux"), None),
            P("grp"),
            P(("grp", "aux")),
            P(("grp", "aux")),
            P(("grp", "aux")),
        ),
        out_specs=P(("grp", "aux"), None),
        check_vma=False,
    )
```

```python
import functools

import jax
import jax.numpy as jnp
from jax import lax
from jax.experimental import pallas as pl
from jax.experimental.pallas import tpu as pltpu
from jax.sharding import PartitionSpec as P

AB_DEV = 8
CHUNK = 2
TURNS = (8, 2, 1)
TAIL = 16
PLANE = 4
SPREAD_COST = 10**10
DIRECT = 16


def pack_slots(tile_block, tile_aux, live, basis_order, base, bb_dev):
    slots, nbb = tile_block.shape[0], basis_order.shape[0]
    k = lax.iota(jnp.int32, nbb)
    owner = jnp.bitwise_xor(k // bb_dev, base)
    value = (owner * bb_dev + k % bb_dev)[None, :] * AB_DEV + tile_aux[:, None]
    value = jnp.where(basis_order[None, :] == tile_block[:, None], value * 2, 0)
    alive = jnp.pad(live, (0, nbb - 1))[None, :] > lax.iota(jnp.int32, slots)[:, None]
    return jnp.sum(value + alive.astype(jnp.int32), axis=1)


def unpack_slots(packed, bb_dev):
    rest = packed // 2
    tile_aux = rest % AB_DEV
    rest = rest // AB_DEV
    return rest // bb_dev, rest % bb_dev, tile_aux, packed % 2 == 1


def chunk_lists(where_to, later, alive, tile_aux, n_aux):
    slots = where_to.shape[0]
    keys = 2 * AB_DEV
    chunks = slots // CHUNK + keys
    t = lax.iota(jnp.int32, slots)
    group = jnp.where(alive, tile_aux + jnp.where(later, AB_DEV, 0), keys)
    ids = lax.iota(jnp.int32, keys)
    counts = jnp.sum((group[None, :] == ids[:, None]).astype(jnp.int32), axis=1)
    need = (counts + CHUNK - 1) // CHUNK
    ends = jnp.sum(jnp.where(ids[None, :] <= ids[:, None], need[None, :], 0), axis=1)
    rank = jnp.sum(
        ((group[None, :] == group[:, None]) & (t[None, :] < t[:, None])).astype(jnp.int32), axis=1
    )
    start = jnp.sum(jnp.where(group[:, None] > ids[None, :], need[None, :], 0), axis=1)
    place = jnp.where(alive, start * CHUNK + rank, -1)
    q = lax.iota(jnp.int32, chunks * CHUNK)
    hit = place[None, :] == q[:, None]
    lead = place[None, :] == (q // CHUNK * CHUNK)[:, None]
    valid = jnp.any(hit, axis=1)
    slot = jnp.sum(jnp.where(hit, t[None, :], 0), axis=1)
    slot = jnp.where(valid, slot, jnp.sum(jnp.where(lead, t[None, :], 0), axis=1))
    block = jnp.where(valid, jnp.sum(jnp.where(hit, where_to[None, :], 0), axis=1), n_aux)
    gid = jnp.sum(
        (lax.iota(jnp.int32, chunks)[:, None] >= ends[None, :]).astype(jnp.int32), axis=1
    )
    return slot, block, jnp.concatenate([gid % AB_DEV, ends])


def bits_of(where_to, which, alive, n_aux):
    return jnp.max(
        jnp.where(
            (where_to[None, :] == lax.iota(jnp.int32, n_aux)[:, None]) & alive[None, :],
            which[None, :],
            0,
        ),
        axis=1,
    )


def slab(tiles, slot):
    return jnp.concatenate([tiles[slot, p] for p in range(tiles.shape[1])], axis=1)


def chunk_ends(gid_ref, slots):
    chunks = slots // CHUNK + 2 * AB_DEV
    return gid_ref[chunks + AB_DEV - 1], gid_ref[chunks + 2 * AB_DEV - 1]


def turn(ct, bit_ref, m, source):
    blk = ct.shape[2]
    row = pl.multiple_of(bit_ref[m] * blk, blk)
    ct[m] = source[pl.ds(row, blk), :].T


def sweep(low, high, body):
    for size in TURNS:
        whole = (high - low) // size

        @pl.loop(0, whole)
        def _(step, low=low, size=size):
            body([low + step * size + u for u in range(size)])

        low = low + whole * size


def fit(lists, tiles, ct, zacc, low, high):
    slot_ref, block_ref, gid_ref = lists

    def body(group):
        for chunk in group:
            spots = [chunk * CHUNK + i for i in range(CHUNK)]
            left = jnp.concatenate([ct[block_ref[pos]] for pos in spots], axis=1)
            right = jnp.concatenate([slab(tiles, slot_ref[pos]) for pos in spots], axis=0)
            zacc[gid_ref[chunk]] += jnp.dot(left, right, preferred_element_type=jnp.float32)

    sweep(low, high, body)


def apply_fitted(lists, tiles, zb, acc, low, high):
    slot_ref, block_ref, gid_ref = lists
    blk = acc.shape[1]

    def body(group):
        for chunk in group:
            spots = [chunk * CHUNK + i for i in range(CHUNK)]
            left = jnp.concatenate([slab(tiles, slot_ref[pos]) for pos in spots], axis=0)
            value = lax.dot_general(
                left,
                zb[gid_ref[chunk]],
                (((1,), (1,)), ((), ())),
                preferred_element_type=jnp.float32,
            )
            for i, pos in enumerate(spots):
                acc[block_ref[pos]] += value[i * blk : (i + 1) * blk]

    sweep(low, high, body)


def begin(n_aux, lists, bit, packed, tiles_array, own_array, shards, sources):
    slots, auxb, blk, nocc = tiles_array.shape
    n_in = len(shards)

    def kernel(slot_ref, block_ref, gid_ref, bit_ref, packed_ref, tiles, own, *refs):
        c_refs, (zacc, passed, ct) = refs[:n_in], refs[n_in:]
        passed[...] = packed_ref[...]
        zacc[...] = jnp.zeros(zacc.shape, zacc.dtype)
        ct[n_aux] = jnp.zeros((nocc, blk), ct.dtype)
        turn(ct, bit_ref, 0, own)
        for m, (ref, i) in sources:
            turn(ct, bit_ref, m, c_refs[ref] if i is None else c_refs[ref].at[i])
        early, _ = chunk_ends(gid_ref, slots)
        fit((slot_ref, block_ref, gid_ref), tiles, ct, zacc, 0, early)

    smem = pl.BlockSpec(memory_space=pltpu.SMEM)
    vmem = pl.BlockSpec(memory_space=pltpu.VMEM)
    return pl.pallas_call(
        kernel,
        out_shape=[
            jax.ShapeDtypeStruct((AB_DEV, nocc, auxb * nocc), jnp.float32),
            jax.ShapeDtypeStruct(packed.shape, packed.dtype),
        ],
        in_specs=[smem] * 4 + [vmem] * (3 + n_in),
        out_specs=[vmem] * 2,
        scratch_shapes=[pltpu.VMEM((n_aux + 1, nocc, blk), jnp.bfloat16)],
        compiler_params=pltpu.CompilerParams(vmem_limit_bytes=20 * 1024 * 1024),
        cost_estimate=pl.CostEstimate(
            flops=2 * tiles_array.size * nocc, bytes_accessed=tiles_array.size, transcendentals=0
        ),
        name="begin",
    )(*lists, bit, packed, tiles_array, own_array, *shards)


def put(bit_ref, acc, m, out_ref, place):
    blk, nocc = acc.shape[1:]
    out_ref[place, :blk, :] = acc[m].astype(out_ref.dtype)
    out_ref[place, blk:, :] = jnp.full((TAIL, nocc), bit_ref[m], jnp.int32).astype(
        jnp.float32
    ).astype(out_ref.dtype)


def clear(n_aux, ct, acc):
    ct[n_aux] = jnp.zeros(ct.shape[1:], ct.dtype)
    acc[...] = jnp.zeros(acc.shape, acc.dtype)


def round_fitted(zacc, zb):
    for g in range(zacc.shape[0]):
        zb[g] = zacc[g].astype(zb.dtype)


def first_part(n_aux, fit_lists, lists, bit, tiles_array, partial_fit, shards, sources):
    slots, auxb, blk, nocc = tiles_array.shape
    n_in = len(shards)

    def kernel(*refs):
        fit_refs, refs = refs[:3], refs[3:]
        list_refs, bit_ref, tiles = refs[:3], refs[3], refs[4]
        c_refs, out_refs = refs[6 : 6 + n_in], refs[6 + n_in : -4]
        zb, zacc, ct, acc = refs[-4:]
        clear(n_aux, ct, acc)
        for m, (ref, i) in sources:
            turn(ct, bit_ref, m, c_refs[ref] if i is None else c_refs[ref].at[i])
        fit(fit_refs, tiles, ct, zacc, *chunk_ends(fit_refs[2], slots))
        round_fitted(zacc, zb)
        far, _ = chunk_ends(list_refs[2], slots)
        apply_fitted(list_refs, tiles, zb, acc, 0, far)
        for m in range(PLANE, n_aux):
            put(bit_ref, acc, m, out_refs[m % PLANE], m // PLANE - 1)

    smem = pl.BlockSpec(memory_space=pltpu.SMEM)
    vmem = pl.BlockSpec(memory_space=pltpu.VMEM)
    shape = (n_aux // PLANE - 1, blk + TAIL, nocc)
    out_shape = [jax.ShapeDtypeStruct(shape, jnp.bfloat16)] * PLANE
    out_shape = out_shape + [
        jax.ShapeDtypeStruct((AB_DEV, nocc, auxb * nocc), jnp.bfloat16),
        jax.ShapeDtypeStruct(partial_fit.shape, partial_fit.dtype),
    ]
    return pl.pallas_call(
        kernel,
        out_shape=out_shape,
        in_specs=[smem] * 7 + [vmem] * (2 + n_in),
        out_specs=[vmem] * len(out_shape),
        scratch_shapes=[
            pltpu.VMEM((n_aux + 1, nocc, blk), jnp.bfloat16),
            pltpu.VMEM((n_aux + 1, blk, nocc), jnp.float32),
        ],
        input_output_aliases={8: PLANE + 1},
        compiler_params=pltpu.CompilerParams(vmem_limit_bytes=20 * 1024 * 1024),
        cost_estimate=pl.CostEstimate(
            flops=3 * tiles_array.size * nocc, bytes_accessed=tiles_array.size, transcendentals=0
        ),
        name="first_part",
    )(*fit_lists, *lists, bit, tiles_array, partial_fit, *shards)


def second_part(n_aux, lists, bit, tiles_array, fitted, after):
    slots, auxb, blk, nocc = tiles_array.shape

    def kernel(slot_ref, block_ref, gid_ref, bit_ref, tiles, zb, _, *refs):
        out_refs, acc = refs[:-1], refs[-1]
        acc[...] = jnp.zeros(acc.shape, acc.dtype)
        apply_fitted(
            (slot_ref, block_ref, gid_ref), tiles, zb, acc, *chunk_ends(gid_ref, slots)
        )
        for m in range(PLANE):
            put(bit_ref, acc, m, out_refs[m], 0)

    smem = pl.BlockSpec(memory_space=pltpu.SMEM)
    vmem = pl.BlockSpec(memory_space=pltpu.VMEM)
    shape = (1, blk + TAIL, nocc)
    return pl.pallas_call(
        kernel,
        out_shape=[jax.ShapeDtypeStruct(shape, jnp.bfloat16)] * PLANE,
        in_specs=[smem] * 4 + [vmem, vmem, pl.BlockSpec(memory_space=pl.ANY)],
        out_specs=[vmem] * PLANE,
        scratch_shapes=[pltpu.VMEM((n_aux + 1, blk, nocc), jnp.float32)],
        compiler_params=pltpu.CompilerParams(vmem_limit_bytes=20 * 1024 * 1024),
        cost_estimate=pl.CostEstimate(
            flops=10**10, bytes_accessed=tiles_array.size, transcendentals=0
        ),
        name="second_part",
    )(*lists, bit, tiles_array, fitted, after)


def all_in_one(n_aux, lists, bit, tiles_array, whole):
    slots, auxb, blk, nocc = tiles_array.shape

    def kernel(slot_ref, block_ref, gid_ref, bit_ref, tiles, c_ref, out_ref, ct, zacc, zb, acc):
        lists = (slot_ref, block_ref, gid_ref)
        clear(n_aux, ct, acc)
        zacc[...] = jnp.zeros(zacc.shape, zacc.dtype)

        @pl.loop(0, n_aux)
        def _(m):
            turn(ct, bit_ref, m, c_ref.at[m])

        _, total = chunk_ends(gid_ref, slots)
        fit(lists, tiles, ct, zacc, 0, total)
        round_fitted(zacc, zb)
        apply_fitted(lists, tiles, zb, acc, 0, total)

        @pl.loop(0, n_aux)
        def _(m):
            put(bit_ref, acc, m, out_ref, m)

    smem = pl.BlockSpec(memory_space=pltpu.SMEM)
    vmem = pl.BlockSpec(memory_space=pltpu.VMEM)
    return pl.pallas_call(
        kernel,
        out_shape=jax.ShapeDtypeStruct((n_aux, blk + TAIL, nocc), jnp.bfloat16),
        in_specs=[smem] * 4 + [vmem] * 2,
        out_specs=vmem,
        scratch_shapes=[
            pltpu.VMEM((n_aux + 1, nocc, blk), jnp.bfloat16),
            pltpu.VMEM((AB_DEV, nocc, auxb * nocc), jnp.float32),
            pltpu.VMEM((AB_DEV, nocc, auxb * nocc), jnp.bfloat16),
            pltpu.VMEM((n_aux + 1, blk, nocc), jnp.float32),
        ],
        compiler_params=pltpu.CompilerParams(vmem_limit_bytes=46 * 1024 * 1024),
        name="all_in_one",
    )(*lists, bit, tiles_array, whole)


def gate(arrays, after):
    counts = [array.shape[0] if array.ndim == 3 else 1 for array in arrays]

    def kernel(*refs):
        target, place = refs[-1], 0
        for ref, count in zip(refs, counts):
            value = ref[...]
            target[place : place + count] = value.reshape((count,) + value.shape[-2:])
            place += count

    vmem = pl.BlockSpec(memory_space=pltpu.VMEM)
    return pl.pallas_call(
        kernel,
        out_shape=jax.ShapeDtypeStruct((sum(counts),) + arrays[0].shape[-2:], arrays[0].dtype),
        in_specs=[vmem] * len(arrays) + [pl.BlockSpec(memory_space=pl.ANY)],
        out_specs=vmem,
        compiler_params=pltpu.CompilerParams(vmem_limit_bytes=4 * 1024 * 1024),
        name="gate",
    )(*arrays, after)


def merge(arrays, after, cost):
    def kernel(*refs):
        for i, ref in enumerate(refs[: len(arrays)]):
            refs[-1][i] = ref[...]

    vmem = pl.BlockSpec(memory_space=pltpu.VMEM)
    return pl.pallas_call(
        kernel,
        out_shape=jax.ShapeDtypeStruct((len(arrays),) + arrays[0].shape, arrays[0].dtype),
        in_specs=[vmem] * len(arrays) + [pl.BlockSpec(memory_space=pl.ANY)] * len(after),
        out_specs=vmem,
        compiler_params=pltpu.CompilerParams(vmem_limit_bytes=4 * 1024 * 1024),
        cost_estimate=pl.CostEstimate(flops=cost, bytes_accessed=cost // 1000, transcendentals=0),
        name="merge",
    )(*arrays, *after)


def placed_sum(sources, i, blk, bb_dev):
    nocc = sources[0].shape[2]
    sums = [jnp.zeros((blk, nocc), jnp.float32) for _ in range(bb_dev)]
    for source in sources:
        value = source[i, :blk, :].astype(jnp.float32)
        which = source[i, blk:, :][:1].astype(jnp.float32)
        for b in range(bb_dev):
            sums[b] = sums[b] + jnp.where(which == b, value, 0.0)
    return sums


def spread(parts, dtype, blk, bb_dev):
    count, rows, nocc = parts[0].shape

    def kernel(*refs):
        sources, targets = refs[: len(parts)], refs[len(parts) :]
        for i in range(count):
            for b, value in enumerate(placed_sum(sources, i, blk, bb_dev)):
                targets[i][b * blk : (b + 1) * blk, :] = value.astype(targets[i].dtype)

    vmem = pl.BlockSpec(memory_space=pltpu.VMEM)
    return pl.pallas_call(
        kernel,
        out_shape=[jax.ShapeDtypeStruct((bb_dev * blk, nocc), dtype)] * count,
        in_specs=[vmem] * len(parts),
        out_specs=[vmem] * count,
        compiler_params=pltpu.CompilerParams(vmem_limit_bytes=4 * 1024 * 1024),
        cost_estimate=pl.CostEstimate(
            flops=SPREAD_COST, bytes_accessed=SPREAD_COST // 1000, transcendentals=0
        ),
        name="spread",
    )(*parts)


def total_of(arrays):
    def kernel(*refs):
        value = refs[0][...].astype(jnp.float32)
        for ref in refs[1:-1]:
            value = value + ref[...].astype(jnp.float32)
        refs[-1][...] = value.astype(refs[-1].dtype)

    vmem = pl.BlockSpec(memory_space=pltpu.VMEM)
    return pl.pallas_call(
        kernel,
        out_shape=jax.ShapeDtypeStruct(arrays[0].shape, jnp.bfloat16),
        in_specs=[vmem] * len(arrays),
        out_specs=vmem,
        compiler_params=pltpu.CompilerParams(vmem_limit_bytes=4 * 1024 * 1024),
        name="total_of",
    )(*arrays)


def owner_sum(parts, blk, bb_dev):
    n_aux, rows, nocc = parts.shape

    def kernel(parts_ref, out_ref):
        sums = [jnp.zeros((blk, nocc), jnp.float32) for _ in range(bb_dev)]
        for s in range(n_aux):
            value = parts_ref[s, :blk, :].astype(jnp.float32)
            which = parts_ref[s, blk:, :][:1].astype(jnp.float32)
            for b in range(bb_dev):
                sums[b] = sums[b] + jnp.where(which == b, value, 0.0)
        for b in range(bb_dev):
            out_ref[b * blk : (b + 1) * blk, :] = sums[b].astype(out_ref.dtype)

    vmem = pl.BlockSpec(memory_space=pltpu.VMEM)
    return pl.pallas_call(
        kernel,
        out_shape=jax.ShapeDtypeStruct((bb_dev * blk, nocc), jnp.bfloat16),
        in_specs=[vmem],
        out_specs=vmem,
        name="owner_sum",
    )(parts)


def on_device(tiles, c_orbitals, basis_order, tile_block, tile_aux, live):
    blk, nocc = tiles.shape[2:]
    n_aux = lax.axis_size("aux")
    bb_dev = basis_order.shape[0] // n_aux
    direct = n_aux == DIRECT

    def swap(array, m):
        return lax.ppermute(array, "aux", [(i, i ^ m) for i in range(n_aux)])

    base = lax.axis_index("aux").astype(jnp.int32) if direct else jnp.int32(0)
    packed = pack_slots(tile_block, tile_aux, live, basis_order, base, bb_dev)
    where_to, which, group, alive = unpack_slots(packed, bb_dev)
    bit = bits_of(where_to, which, alive, n_aux)
    if not direct:
        lists = chunk_lists(where_to, where_to < 0, alive, group, n_aux)
        whole = lax.all_gather(c_orbitals, "aux", axis=0, tiled=True)
        whole = whole.reshape(n_aux, bb_dev * blk, nocc)
        parts = all_in_one(n_aux, lists, bit, tiles, whole)
        moved = lax.all_to_all(parts, "aux", 0, 0, tiled=True)
        return owner_sum(moved, blk, bb_dev)

    depth = n_aux // PLANE
    side = where_to % PLANE >= 2
    last = (where_to >= 3 * PLANE) | ((where_to >= PLANE) & side)
    fit_lists = chunk_lists(where_to, last, alive, group, n_aux)
    two = swap(c_orbitals, 2 * PLANE)
    one = swap(c_orbitals, PLANE)
    beside = swap(c_orbitals, 2)
    across = swap(c_orbitals, 1)
    three = swap(c_orbitals, 3 * PLANE)
    pair = merge([one, two], [], SPREAD_COST)
    pair_beside = swap(pair, 2)
    three_beside = swap(three, 2)
    early = [pair, swap(pair, 1), across, beside, swap(beside, 1)]
    early_from = [(1, (2, None)), (2, (3, None)), (3, (4, None))]
    late_from = []
    for core in range(2):
        early_from += [(PLANE + core, (core, 0)), (2 * PLANE + core, (core, 1))]
        late_from += [
            (PLANE + 2 + core, (core, 0)),
            (2 * PLANE + 2 + core, (core, 1)),
            (3 * PLANE + core, (core, 2)),
            (3 * PLANE + 2 + core, (core, 3)),
        ]
    partial_fit, packed = begin(
        n_aux, fit_lists, bit, packed, tiles, c_orbitals, early, early_from
    )
    late = gate([pair_beside, three, three_beside], partial_fit)
    where_to, _, group, alive = unpack_slots(packed, bb_dev)
    lists = chunk_lists(where_to, where_to < PLANE, alive, group, n_aux)
    *far, fitted, _ = first_part(
        n_aux, fit_lists, lists, bit, tiles, partial_fit, [late, swap(late, 1)], late_from
    )
    far = [far[0]] + [swap(far[r], r) for r in range(1, PLANE)]
    near = second_part(n_aux, lists, bit, tiles, fitted, far[1])
    near = [near[0]] + [swap(near[r], r) for r in range(1, PLANE)]
    far = spread(far, jnp.bfloat16, blk, bb_dev)
    far = [swap(far[dz - 1], dz * PLANE) for dz in [*range(2, depth), 1]]
    near = spread(near, jnp.float32, blk, bb_dev)
    return total_of(list(near) + far)


def solution(mesh):
    return jax.shard_map(
        on_device,
        mesh=mesh,
        in_specs=(
            P(("grp", "aux"), None, None, None),
            P(("grp", "aux"), None),
            P("grp"),
            P(("grp", "aux")),
            P(("grp", "aux")),
            P(("grp", "aux")),
        ),
        out_specs=P(("grp", "aux"), None),
        check_vma=False,
    )
```

```python
import functools

import jax
import jax.numpy as jnp
from jax import lax
from jax.experimental import pallas as pl
from jax.experimental.pallas import tpu as pltpu
from jax.sharding import PartitionSpec as P

AB_DEV = 8
CHUNK = 2
TURNS = (4, 1)
TAIL = 16
PLANE = 4
SPREAD_COST = 10**10
DIRECT = 16


def pack_slots(tile_block, tile_aux, live, basis_order, base, bb_dev):
    slots, nbb = tile_block.shape[0], basis_order.shape[0]
    k = lax.iota(jnp.int32, nbb)
    owner = jnp.bitwise_xor(k // bb_dev, base)
    value = (owner * bb_dev + k % bb_dev)[None, :] * AB_DEV + tile_aux[:, None]
    value = jnp.where(basis_order[None, :] == tile_block[:, None], value * 2, 0)
    alive = jnp.pad(live, (0, nbb - 1))[None, :] > lax.iota(jnp.int32, slots)[:, None]
    return jnp.sum(value + alive.astype(jnp.int32), axis=1)


def unpack_slots(packed, bb_dev):
    rest = packed // 2
    tile_aux = rest % AB_DEV
    rest = rest // AB_DEV
    return rest // bb_dev, rest % bb_dev, tile_aux, packed % 2 == 1


def chunk_lists(where_to, later, alive, tile_aux, n_aux):
    slots = where_to.shape[0]
    keys = 2 * AB_DEV
    chunks = slots // CHUNK + keys
    t = lax.iota(jnp.int32, slots)
    group = jnp.where(alive, tile_aux + jnp.where(later, AB_DEV, 0), keys)
    ids = lax.iota(jnp.int32, keys)
    counts = jnp.sum((group[None, :] == ids[:, None]).astype(jnp.int32), axis=1)
    need = (counts + CHUNK - 1) // CHUNK
    ends = jnp.sum(jnp.where(ids[None, :] <= ids[:, None], need[None, :], 0), axis=1)
    rank = jnp.sum(
        ((group[None, :] == group[:, None]) & (t[None, :] < t[:, None])).astype(jnp.int32), axis=1
    )
    start = jnp.sum(jnp.where(group[:, None] > ids[None, :], need[None, :], 0), axis=1)
    place = jnp.where(alive, start * CHUNK + rank, -1)
    q = lax.iota(jnp.int32, chunks * CHUNK)
    hit = place[None, :] == q[:, None]
    lead = place[None, :] == (q // CHUNK * CHUNK)[:, None]
    valid = jnp.any(hit, axis=1)
    slot = jnp.sum(jnp.where(hit, t[None, :], 0), axis=1)
    slot = jnp.where(valid, slot, jnp.sum(jnp.where(lead, t[None, :], 0), axis=1))
    block = jnp.where(valid, jnp.sum(jnp.where(hit, where_to[None, :], 0), axis=1), n_aux)
    gid = jnp.sum(
        (lax.iota(jnp.int32, chunks)[:, None] >= ends[None, :]).astype(jnp.int32), axis=1
    )
    return slot, block, jnp.concatenate([gid % AB_DEV, ends])


def bits_of(where_to, which, alive, n_aux):
    return jnp.max(
        jnp.where(
            (where_to[None, :] == lax.iota(jnp.int32, n_aux)[:, None]) & alive[None, :],
            which[None, :],
            0,
        ),
        axis=1,
    )


def slab(tiles, slot):
    return jnp.concatenate([tiles[slot, p] for p in range(tiles.shape[1])], axis=1)


def chunk_ends(gid_ref, slots):
    chunks = slots // CHUNK + 2 * AB_DEV
    return gid_ref[chunks + AB_DEV - 1], gid_ref[chunks + 2 * AB_DEV - 1]


def turn(ct, bit_ref, m, source):
    blk = ct.shape[2]
    row = pl.multiple_of(bit_ref[m] * blk, blk)
    ct[m] = source[pl.ds(row, blk), :].T


def sweep(low, high, body):
    for size in TURNS:
        whole = (high - low) // size

        @pl.loop(0, whole)
        def _(step, low=low, size=size):
            body([low + step * size + u for u in range(size)])

        low = low + whole * size


def fit(lists, tiles, ct, zacc, low, high):
    slot_ref, block_ref, gid_ref = lists

    def body(group):
        for chunk in group:
            spots = [chunk * CHUNK + i for i in range(CHUNK)]
            left = jnp.concatenate([ct[block_ref[pos]] for pos in spots], axis=1)
            right = jnp.concatenate([slab(tiles, slot_ref[pos]) for pos in spots], axis=0)
            zacc[gid_ref[chunk]] += jnp.dot(left, right, preferred_element_type=jnp.float32)

    sweep(low, high, body)


def apply_fitted(lists, tiles, zb, acc, low, high):
    slot_ref, block_ref, gid_ref = lists
    blk = acc.shape[1]

    def body(group):
        for chunk in group:
            spots = [chunk * CHUNK + i for i in range(CHUNK)]
            left = jnp.concatenate([slab(tiles, slot_ref[pos]) for pos in spots], axis=0)
            value = lax.dot_general(
                left,
                zb[gid_ref[chunk]],
                (((1,), (1,)), ((), ())),
                preferred_element_type=jnp.float32,
            )
            for i, pos in enumerate(spots):
                acc[block_ref[pos]] += value[i * blk : (i + 1) * blk]

    sweep(low, high, body)


def begin(n_aux, lists, bit, packed, tiles_array, own_array, shards, sources):
    slots, auxb, blk, nocc = tiles_array.shape
    n_in = len(shards)

    def kernel(slot_ref, block_ref, gid_ref, bit_ref, packed_ref, tiles, own, *refs):
        c_refs, (zacc, passed, ct) = refs[:n_in], refs[n_in:]
        passed[...] = packed_ref[...]
        zacc[...] = jnp.zeros(zacc.shape, zacc.dtype)
        ct[n_aux] = jnp.zeros((nocc, blk), ct.dtype)
        turn(ct, bit_ref, 0, own)
        for m, (ref, i) in sources:
            turn(ct, bit_ref, m, c_refs[ref] if i is None else c_refs[ref].at[i])
        early, _ = chunk_ends(gid_ref, slots)
        fit((slot_ref, block_ref, gid_ref), tiles, ct, zacc, 0, early)

    smem = pl.BlockSpec(memory_space=pltpu.SMEM)
    vmem = pl.BlockSpec(memory_space=pltpu.VMEM)
    return pl.pallas_call(
        kernel,
        out_shape=[
            jax.ShapeDtypeStruct((AB_DEV, nocc, auxb * nocc), jnp.float32),
            jax.ShapeDtypeStruct(packed.shape, packed.dtype),
        ],
        in_specs=[smem] * 4 + [vmem] * (3 + n_in),
        out_specs=[vmem] * 2,
        scratch_shapes=[pltpu.VMEM((n_aux + 1, nocc, blk), jnp.bfloat16)],
        compiler_params=pltpu.CompilerParams(vmem_limit_bytes=20 * 1024 * 1024),
        cost_estimate=pl.CostEstimate(
            flops=2 * tiles_array.size * nocc, bytes_accessed=tiles_array.size, transcendentals=0
        ),
        name="begin",
    )(*lists, bit, packed, tiles_array, own_array, *shards)


def put(bit_ref, acc, m, out_ref, place):
    blk, nocc = acc.shape[1:]
    out_ref[place, :blk, :] = acc[m].astype(out_ref.dtype)
    out_ref[place, blk:, :] = jnp.full((TAIL, nocc), bit_ref[m], jnp.int32).astype(
        jnp.float32
    ).astype(out_ref.dtype)


def clear(n_aux, ct, acc):
    ct[n_aux] = jnp.zeros(ct.shape[1:], ct.dtype)
    acc[...] = jnp.zeros(acc.shape, acc.dtype)


def round_fitted(zacc, zb):
    for g in range(zacc.shape[0]):
        zb[g] = zacc[g].astype(zb.dtype)


def first_part(n_aux, fit_lists, lists, bit, tiles_array, partial_fit, shards, sources):
    slots, auxb, blk, nocc = tiles_array.shape
    n_in = len(shards)

    def kernel(*refs):
        fit_refs, refs = refs[:3], refs[3:]
        list_refs, bit_ref, tiles = refs[:3], refs[3], refs[4]
        c_refs, out_refs = refs[6 : 6 + n_in], refs[6 + n_in : -4]
        zb, zacc, ct, acc = refs[-4:]
        clear(n_aux, ct, acc)
        for m, (ref, i) in sources:
            turn(ct, bit_ref, m, c_refs[ref] if i is None else c_refs[ref].at[i])
        fit(fit_refs, tiles, ct, zacc, *chunk_ends(fit_refs[2], slots))
        round_fitted(zacc, zb)
        far, _ = chunk_ends(list_refs[2], slots)
        apply_fitted(list_refs, tiles, zb, acc, 0, far)
        for m in range(PLANE, n_aux):
            put(bit_ref, acc, m, out_refs[m % PLANE], m // PLANE - 1)

    smem = pl.BlockSpec(memory_space=pltpu.SMEM)
    vmem = pl.BlockSpec(memory_space=pltpu.VMEM)
    shape = (n_aux // PLANE - 1, blk + TAIL, nocc)
    out_shape = [jax.ShapeDtypeStruct(shape, jnp.bfloat16)] * PLANE
    out_shape = out_shape + [
        jax.ShapeDtypeStruct((AB_DEV, nocc, auxb * nocc), jnp.bfloat16),
        jax.ShapeDtypeStruct(partial_fit.shape, partial_fit.dtype),
    ]
    return pl.pallas_call(
        kernel,
        out_shape=out_shape,
        in_specs=[smem] * 7 + [vmem] * (2 + n_in),
        out_specs=[vmem] * len(out_shape),
        scratch_shapes=[
            pltpu.VMEM((n_aux + 1, nocc, blk), jnp.bfloat16),
            pltpu.VMEM((n_aux + 1, blk, nocc), jnp.float32),
        ],
        input_output_aliases={8: PLANE + 1},
        compiler_params=pltpu.CompilerParams(vmem_limit_bytes=20 * 1024 * 1024),
        cost_estimate=pl.CostEstimate(
            flops=3 * tiles_array.size * nocc, bytes_accessed=tiles_array.size, transcendentals=0
        ),
        name="first_part",
    )(*fit_lists, *lists, bit, tiles_array, partial_fit, *shards)


def second_part(n_aux, lists, bit, tiles_array, fitted, after):
    slots, auxb, blk, nocc = tiles_array.shape

    def kernel(slot_ref, block_ref, gid_ref, bit_ref, tiles, zb, _, *refs):
        out_refs, acc = refs[:-1], refs[-1]
        acc[...] = jnp.zeros(acc.shape, acc.dtype)
        apply_fitted(
            (slot_ref, block_ref, gid_ref), tiles, zb, acc, *chunk_ends(gid_ref, slots)
        )
        for m in range(PLANE):
            put(bit_ref, acc, m, out_refs[m], 0)

    smem = pl.BlockSpec(memory_space=pltpu.SMEM)
    vmem = pl.BlockSpec(memory_space=pltpu.VMEM)
    shape = (1, blk + TAIL, nocc)
    return pl.pallas_call(
        kernel,
        out_shape=[jax.ShapeDtypeStruct(shape, jnp.bfloat16)] * PLANE,
        in_specs=[smem] * 4 + [vmem, vmem, pl.BlockSpec(memory_space=pl.ANY)],
        out_specs=[vmem] * PLANE,
        scratch_shapes=[pltpu.VMEM((n_aux + 1, blk, nocc), jnp.float32)],
        compiler_params=pltpu.CompilerParams(vmem_limit_bytes=20 * 1024 * 1024),
        cost_estimate=pl.CostEstimate(
            flops=10**10, bytes_accessed=tiles_array.size, transcendentals=0
        ),
        name="second_part",
    )(*lists, bit, tiles_array, fitted, after)


def all_in_one(n_aux, lists, bit, tiles_array, whole):
    slots, auxb, blk, nocc = tiles_array.shape

    def kernel(slot_ref, block_ref, gid_ref, bit_ref, tiles, c_ref, out_ref, ct, zacc, zb, acc):
        lists = (slot_ref, block_ref, gid_ref)
        clear(n_aux, ct, acc)
        zacc[...] = jnp.zeros(zacc.shape, zacc.dtype)

        @pl.loop(0, n_aux)
        def _(m):
            turn(ct, bit_ref, m, c_ref.at[m])

        _, total = chunk_ends(gid_ref, slots)
        fit(lists, tiles, ct, zacc, 0, total)
        round_fitted(zacc, zb)
        apply_fitted(lists, tiles, zb, acc, 0, total)

        @pl.loop(0, n_aux)
        def _(m):
            put(bit_ref, acc, m, out_ref, m)

    smem = pl.BlockSpec(memory_space=pltpu.SMEM)
    vmem = pl.BlockSpec(memory_space=pltpu.VMEM)
    return pl.pallas_call(
        kernel,
        out_shape=jax.ShapeDtypeStruct((n_aux, blk + TAIL, nocc), jnp.bfloat16),
        in_specs=[smem] * 4 + [vmem] * 2,
        out_specs=vmem,
        scratch_shapes=[
            pltpu.VMEM((n_aux + 1, nocc, blk), jnp.bfloat16),
            pltpu.VMEM((AB_DEV, nocc, auxb * nocc), jnp.float32),
            pltpu.VMEM((AB_DEV, nocc, auxb * nocc), jnp.bfloat16),
            pltpu.VMEM((n_aux + 1, blk, nocc), jnp.float32),
        ],
        compiler_params=pltpu.CompilerParams(vmem_limit_bytes=46 * 1024 * 1024),
        name="all_in_one",
    )(*lists, bit, tiles_array, whole)


def gate(arrays, after):
    counts = [array.shape[0] if array.ndim == 3 else 1 for array in arrays]

    def kernel(*refs):
        target, place = refs[-1], 0
        for ref, count in zip(refs, counts):
            value = ref[...]
            target[place : place + count] = value.reshape((count,) + value.shape[-2:])
            place += count

    vmem = pl.BlockSpec(memory_space=pltpu.VMEM)
    return pl.pallas_call(
        kernel,
        out_shape=jax.ShapeDtypeStruct((sum(counts),) + arrays[0].shape[-2:], arrays[0].dtype),
        in_specs=[vmem] * len(arrays) + [pl.BlockSpec(memory_space=pl.ANY)],
        out_specs=vmem,
        compiler_params=pltpu.CompilerParams(vmem_limit_bytes=4 * 1024 * 1024),
        name="gate",
    )(*arrays, after)


def merge(arrays, after, cost):
    def kernel(*refs):
        for i, ref in enumerate(refs[: len(arrays)]):
            refs[-1][i] = ref[...]

    vmem = pl.BlockSpec(memory_space=pltpu.VMEM)
    return pl.pallas_call(
        kernel,
        out_shape=jax.ShapeDtypeStruct((len(arrays),) + arrays[0].shape, arrays[0].dtype),
        in_specs=[vmem] * len(arrays) + [pl.BlockSpec(memory_space=pl.ANY)] * len(after),
        out_specs=vmem,
        compiler_params=pltpu.CompilerParams(vmem_limit_bytes=4 * 1024 * 1024),
        cost_estimate=pl.CostEstimate(flops=cost, bytes_accessed=cost // 1000, transcendentals=0),
        name="merge",
    )(*arrays, *after)


def placed_sum(sources, i, blk, bb_dev):
    nocc = sources[0].shape[2]
    sums = [jnp.zeros((blk, nocc), jnp.float32) for _ in range(bb_dev)]
    for source in sources:
        value = source[i, :blk, :].astype(jnp.float32)
        which = source[i, blk:, :][:1].astype(jnp.float32)
        for b in range(bb_dev):
            sums[b] = sums[b] + jnp.where(which == b, value, 0.0)
    return sums


def spread(parts, dtype, blk, bb_dev):
    count, rows, nocc = parts[0].shape

    def kernel(*refs):
        sources, targets = refs[: len(parts)], refs[len(parts) :]
        for i in range(count):
            for b, value in enumerate(placed_sum(sources, i, blk, bb_dev)):
                targets[i][b * blk : (b + 1) * blk, :] = value.astype(targets[i].dtype)

    vmem = pl.BlockSpec(memory_space=pltpu.VMEM)
    return pl.pallas_call(
        kernel,
        out_shape=[jax.ShapeDtypeStruct((bb_dev * blk, nocc), dtype)] * count,
        in_specs=[vmem] * len(parts),
        out_specs=[vmem] * count,
        compiler_params=pltpu.CompilerParams(vmem_limit_bytes=4 * 1024 * 1024),
        cost_estimate=pl.CostEstimate(
            flops=SPREAD_COST, bytes_accessed=SPREAD_COST // 1000, transcendentals=0
        ),
        name="spread",
    )(*parts)


def total_of(arrays):
    def kernel(*refs):
        value = refs[0][...].astype(jnp.float32)
        for ref in refs[1:-1]:
            value = value + ref[...].astype(jnp.float32)
        refs[-1][...] = value.astype(refs[-1].dtype)

    vmem = pl.BlockSpec(memory_space=pltpu.VMEM)
    return pl.pallas_call(
        kernel,
        out_shape=jax.ShapeDtypeStruct(arrays[0].shape, jnp.bfloat16),
        in_specs=[vmem] * len(arrays),
        out_specs=vmem,
        compiler_params=pltpu.CompilerParams(vmem_limit_bytes=4 * 1024 * 1024),
        name="total_of",
    )(*arrays)


def owner_sum(parts, blk, bb_dev):
    n_aux, rows, nocc = parts.shape

    def kernel(parts_ref, out_ref):
        sums = [jnp.zeros((blk, nocc), jnp.float32) for _ in range(bb_dev)]
        for s in range(n_aux):
            value = parts_ref[s, :blk, :].astype(jnp.float32)
            which = parts_ref[s, blk:, :][:1].astype(jnp.float32)
            for b in range(bb_dev):
                sums[b] = sums[b] + jnp.where(which == b, value, 0.0)
        for b in range(bb_dev):
            out_ref[b * blk : (b + 1) * blk, :] = sums[b].astype(out_ref.dtype)

    vmem = pl.BlockSpec(memory_space=pltpu.VMEM)
    return pl.pallas_call(
        kernel,
        out_shape=jax.ShapeDtypeStruct((bb_dev * blk, nocc), jnp.bfloat16),
        in_specs=[vmem],
        out_specs=vmem,
        name="owner_sum",
    )(parts)


def on_device(tiles, c_orbitals, basis_order, tile_block, tile_aux, live):
    blk, nocc = tiles.shape[2:]
    n_aux = lax.axis_size("aux")
    bb_dev = basis_order.shape[0] // n_aux
    direct = n_aux == DIRECT

    def swap(array, m):
        return lax.ppermute(array, "aux", [(i, i ^ m) for i in range(n_aux)])

    base = lax.axis_index("aux").astype(jnp.int32) if direct else jnp.int32(0)
    packed = pack_slots(tile_block, tile_aux, live, basis_order, base, bb_dev)
    where_to, which, group, alive = unpack_slots(packed, bb_dev)
    bit = bits_of(where_to, which, alive, n_aux)
    if not direct:
        lists = chunk_lists(where_to, where_to < 0, alive, group, n_aux)
        whole = lax.all_gather(c_orbitals, "aux", axis=0, tiled=True)
        whole = whole.reshape(n_aux, bb_dev * blk, nocc)
        parts = all_in_one(n_aux, lists, bit, tiles, whole)
        moved = lax.all_to_all(parts, "aux", 0, 0, tiled=True)
        return owner_sum(moved, blk, bb_dev)

    depth = n_aux // PLANE
    side = where_to % PLANE >= 2
    last = (where_to >= 3 * PLANE) | ((where_to >= PLANE) & side)
    fit_lists = chunk_lists(where_to, last, alive, group, n_aux)
    two = swap(c_orbitals, 2 * PLANE)
    one = swap(c_orbitals, PLANE)
    beside = swap(c_orbitals, 2)
    across = swap(c_orbitals, 1)
    three = swap(c_orbitals, 3 * PLANE)
    pair = merge([one, two], [], SPREAD_COST)
    pair_beside = swap(pair, 2)
    three_beside = swap(three, 2)
    early = [pair, swap(pair, 1), across, beside, swap(beside, 1)]
    early_from = [(1, (2, None)), (2, (3, None)), (3, (4, None))]
    late_from = []
    for core in range(2):
        early_from += [(PLANE + core, (core, 0)), (2 * PLANE + core, (core, 1))]
        late_from += [
            (PLANE + 2 + core, (core, 0)),
            (2 * PLANE + 2 + core, (core, 1)),
            (3 * PLANE + core, (core, 2)),
            (3 * PLANE + 2 + core, (core, 3)),
        ]
    partial_fit, packed = begin(
        n_aux, fit_lists, bit, packed, tiles, c_orbitals, early, early_from
    )
    late = gate([pair_beside, three, three_beside], partial_fit)
    where_to, _, group, alive = unpack_slots(packed, bb_dev)
    lists = chunk_lists(where_to, where_to < PLANE, alive, group, n_aux)
    *far, fitted, _ = first_part(
        n_aux, fit_lists, lists, bit, tiles, partial_fit, [late, swap(late, 1)], late_from
    )
    far = [far[0]] + [swap(far[r], r) for r in range(1, PLANE)]
    near = second_part(n_aux, lists, bit, tiles, fitted, far[1])
    near = [near[0]] + [swap(near[r], r) for r in range(1, PLANE)]
    far = spread(far, jnp.bfloat16, blk, bb_dev)
    far = [swap(far[dz - 1], dz * PLANE) for dz in range(depth - 1, 0, -1)]
    near = spread(near, jnp.float32, blk, bb_dev)
    return total_of(list(near) + far)


def solution(mesh):
    return jax.shard_map(
        on_device,
        mesh=mesh,
        in_specs=(
            P(("grp", "aux"), None, None, None),
            P(("grp", "aux"), None),
            P("grp"),
            P(("grp", "aux")),
            P(("grp", "aux")),
            P(("grp", "aux")),
        ),
        out_specs=P(("grp", "aux"), None),
        check_vma=False,
    )
```
